256 devices in a mesh: lon: 16 (over x_hi, y, core), lat: 8 (over z), rep: 2 (over x_lo).
Axes of the slice: x: 4 (x_hi: 2, x_lo: 2; x = x_hi * 2 + x_lo), y: 4, z: 8, core: 2. Of those that a mesh axis runs over, the one named last changes fastest.
Arguments:
- fine_field: bfloat16 [4, 96, 384, 192], P('rep', 'lat', 'lon'), may hold values from -6 to 6
- fine_gain: float32 [192], replicated, may hold values from 0.1 to 1.9
- fine_qkv: bfloat16 [192, 576], replicated, may hold values from -0.4375 to 0.4375
- fine_proj: bfloat16 [192, 192], replicated, may hold values from -0.4375 to 0.4375
- fine_table: float32 [2, 16, 6, 3312], P('rep', 'lat'), may hold values from -6 to 6
- merge_gain: float32 [768], replicated, may hold values from 0.1 to 1.9
- merge_weight: bfloat16 [768, 384], replicated, may hold values from -0.21875 to 0.21875
- coarse_gain: float32 [384], replicated, may hold values from 0.1 to 1.9
- coarse_qkv: bfloat16 [384, 1152], replicated, may hold values from -0.3125 to 0.3125
- coarse_proj: bfloat16 [384, 384], replicated, may hold values from -0.3125 to 0.3125
- coarse_table: float32 [2, 8, 12, 3312], P('rep', 'lat'), may hold values from -6 to 6
- cotangent: bfloat16 [4, 48, 192, 384], P('rep', 'lat', 'lon'), may hold values from -6 to 6
Outputs:
- coarse_out: bfloat16 [4, 48, 192, 384], P('rep', 'lat', 'lon')
- field_grad: bfloat16 [4, 96, 384, 192], P('rep', 'lat', 'lon')
- fine_gain_grad: float32 [192], replicated
- fine_qkv_grad: float32 [192, 576], replicated
- fine_proj_grad: float32 [192, 192], replicated
- fine_table_grad: float32 [2, 16, 6, 3312], P('rep', 'lat')
- merge_gain_grad: float32 [768], replicated
- merge_weight_grad: float32 [768, 384], replicated
- coarse_gain_grad: float32 [384], replicated
- coarse_qkv_grad: float32 [384, 1152], replicated
- coarse_proj_grad: float32 [384, 384], replicated
- coarse_table_grad: float32 [2, 8, 12, 3312], P('rep', 'lat')
The draws below stay inside these ranges and needn't reach their ends.
All inputs are finite; a program needn't handle non-finite values.
Results may differ from the reference program's by a relative error of at most 0.033.
Values may be sent and summed in bfloat16 or wider, within the bound.
No kernel may reach another device: no remote copies, remote signals or barrier semaphores. Data moves between devices by JAX's collectives and lax.ppermute only.
A program may use at most 192 MiB of HBM per device.

```python
import jax
import jax.numpy as jnp
from jax import lax

C1 = 192
HEADS1 = 6
C2 = 384
HEADS2 = 12
WIN_LEV = 2
WIN_LAT = 6
WIN_LON = 12
WIN_TOK = 144
POS = 3312
Z = 4
H = 96
W = 384
H2 = 48
W2 = 192


def level_of(stream_key, extent, cuts, smallest, largest):
    factor_of, own = 1.0, jax.random.fold_in(stream_key, 6)
    for dim, blocks in cuts:
        heights = jnp.exp(jax.random.uniform(jax.random.fold_in(own, dim), (blocks,), jnp.float32, smallest / len(cuts), largest / len(cuts)))
        factor_of = factor_of * jnp.repeat(heights, extent[dim] // blocks).reshape([-1 if axis == dim else 1 for axis in range(len(extent))])
    return factor_of


def scatter_about(key, dims, scale, reach, cuts=(), kind=jnp.bfloat16):
    entries = jax.random.normal(key, dims, jnp.float32) * scale
    if len(cuts) > 0:
        entries = level_of(key, dims, cuts, -0.22, 0.18) * entries
    return jnp.clip(entries, min=-reach, max=reach).astype(kind)


def setup_inputs(seed: int = 0) -> dict:
    arg_keys = jax.random.split(jax.random.key(seed), 13)
    fine_field = scatter_about(arg_keys[0], (Z, H, W, C1), 1.0, 6.0, ((0, 2), (1, 8), (2, 16)))
    fine_gain = jnp.clip(1.0 + 0.18 * jax.random.normal(arg_keys[1], (C1,), jnp.float32), 0.1, 1.9)
    fine_qkv = scatter_about(arg_keys[2], (C1, 3 * C1), C1 ** -0.5, 0.4375)
    fine_proj = scatter_about(arg_keys[3], (C1, C1), C1 ** -0.5, 0.4375)
    fine_table = scatter_about(arg_keys[4], (Z // WIN_LEV, H // WIN_LAT, HEADS1, POS), 1.0, 6.0, ((0, 2), (1, 8)), jnp.float32)
    merge_gain = jnp.clip(1.0 + 0.18 * jax.random.normal(arg_keys[5], (4 * C1,), jnp.float32), 0.1, 1.9)
    merge_weight = scatter_about(arg_keys[6], (4 * C1, C2), (4 * C1) ** -0.5, 0.21875)
    coarse_gain = jnp.clip(1.0 + 0.18 * jax.random.normal(arg_keys[7], (C2,), jnp.float32), 0.1, 1.9)
    coarse_qkv = scatter_about(arg_keys[8], (C2, 3 * C2), C2 ** -0.5, 0.3125)
    coarse_proj = scatter_about(arg_keys[9], (C2, C2), C2 ** -0.5, 0.3125)
    coarse_table = scatter_about(arg_keys[10], (Z // WIN_LEV, H2 // WIN_LAT, HEADS2, POS), 1.0, 6.0, ((0, 2), (1, 8)), jnp.float32)
    cotangent = scatter_about(arg_keys[11], (Z, H2, W2, C2), 1.0, 6.0, ((0, 2), (1, 8), (2, 16)))
    return {"fine_field": fine_field, "fine_gain": fine_gain, "fine_qkv": fine_qkv, "fine_proj": fine_proj, "fine_table": fine_table, "merge_gain": merge_gain, "merge_weight": merge_weight, "coarse_gain": coarse_gain, "coarse_qkv": coarse_qkv, "coarse_proj": coarse_proj, "coarse_table": coarse_table, "cotangent": cotangent}


EPS = 1e-05

def layer_norm(values, gain_vec):
    full = values.astype(jnp.float32)
    centre = lax.optimization_barrier(jnp.mean(full, axis=-1, keepdims=True))
    shifted = full - centre
    spread = lax.optimization_barrier(jnp.mean(shifted * shifted, axis=-1, keepdims=True))
    inv_std = lax.rsqrt(spread + EPS)
    normed = shifted * inv_std
    return ((normed * gain_vec).astype(jnp.bfloat16), normed, inv_std)

def layer_norm_back(grad_in, gain_vec, normed, inv_std):
    grad_full = grad_in.astype(jnp.float32)
    scaled = grad_full * gain_vec
    gain_grad = lax.optimization_barrier(jnp.sum((grad_full * normed).reshape(-1, normed.shape[-1]), axis=0))
    first = lax.optimization_barrier(jnp.mean(scaled, axis=-1, keepdims=True))
    second = lax.optimization_barrier(jnp.mean(scaled * normed, axis=-1, keepdims=True))
    return (inv_std * (scaled - first - normed * second), gain_grad)

def to_windows(tensor):
    levels, lat_rows, lon_cols = tensor.shape[:3]
    trailing = tensor.shape[3:]
    shaped = tensor.reshape((levels // WIN_LEV, WIN_LEV, lat_rows // WIN_LAT, WIN_LAT, lon_cols // WIN_LON, WIN_LON) + trailing)
    axes_order = (0, 2, 4, 1, 3, 5) + tuple(range(6, 6 + len(trailing)))
    return jnp.transpose(shaped, axes_order).reshape((levels // WIN_LEV, lat_rows // WIN_LAT, lon_cols // WIN_LON, WIN_TOK) + trailing)

def from_windows(tensor, levels, lat_rows, lon_cols):
    trailing = tensor.shape[4:]
    shaped = tensor.reshape((levels // WIN_LEV, lat_rows // WIN_LAT, lon_cols // WIN_LON, WIN_LEV, WIN_LAT, WIN_LON) + trailing)
    axes_order = (0, 3, 1, 4, 2, 5) + tuple(range(6, 6 + len(trailing)))
    return jnp.transpose(shaped, axes_order).reshape((levels, lat_rows, lon_cols) + trailing)

def lon_onehot():
    shape_three = (WIN_LON, WIN_LON, 2 * WIN_LON - 1)
    query_col = lax.broadcasted_iota(jnp.int32, shape_three, 0)
    key_col = lax.broadcasted_iota(jnp.int32, shape_three, 1)
    offsets = lax.broadcasted_iota(jnp.int32, shape_three, 2)
    return (offsets == query_col - key_col + WIN_LON - 1).astype(jnp.float32)

def expand_bias(table):
    blocks_lev, blocks_lat, head_count = table.shape[:3]
    parted = table.reshape(blocks_lev, blocks_lat, head_count, WIN_LEV, WIN_LEV, WIN_LAT, WIN_LAT, 2 * WIN_LON - 1)
    spread = jnp.einsum('abnwxyzd,pqd->abnwypxzq', parted, lon_onehot(), precision=lax.Precision.HIGHEST)
    return spread.reshape(blocks_lev, blocks_lat, head_count, WIN_TOK, WIN_TOK)

def bias_grad(grad_bias):
    blocks_lev, blocks_lat, head_count = grad_bias.shape[:3]
    parted = grad_bias.reshape(blocks_lev, blocks_lat, head_count, WIN_LEV, WIN_LAT, WIN_LON, WIN_LEV, WIN_LAT, WIN_LON)
    folded = jnp.einsum('abnwypxzq,pqd->abnwxyzd', parted, lon_onehot(), precision=lax.Precision.HIGHEST)
    return folded.reshape(blocks_lev, blocks_lat, head_count, POS)

def window_mask(levels, lat_rows, lev_start, lat_start, lev_total, lat_total):
    lev_pos = lev_start + jnp.arange(levels, dtype=jnp.int32)
    lat_pos = lat_start + jnp.arange(lat_rows, dtype=jnp.int32)
    lev_tag = (lev_pos >= lev_total - WIN_LEV // 2).astype(jnp.int32)
    lat_tag = (lat_pos >= lat_total - WIN_LAT // 2).astype(jnp.int32)
    tags = 2 * lev_tag[:, None] + lat_tag[None, :]
    tags = tags.reshape(levels // WIN_LEV, WIN_LEV, lat_rows // WIN_LAT, WIN_LAT).transpose(0, 2, 1, 3)
    tags = jnp.broadcast_to(tags[..., None], tags.shape + (WIN_LON,))
    tags = tags.reshape(levels // WIN_LEV, lat_rows // WIN_LAT, WIN_TOK)
    return (tags[:, :, :, None] == tags[:, :, None, :])[:, :, None, None]

def batched(form, left, right):
    return jnp.einsum(form, left.astype(jnp.float32), right.astype(jnp.float32))

def attention_pieces(rolled, qkv_weight, bias, same, head_count):
    levels, lat_rows, lon_cols, width = rolled.shape
    head_size = width // head_count
    projected = jnp.dot(rolled.reshape(-1, width), qkv_weight, preferred_element_type=jnp.float32)
    windows = to_windows(projected.reshape(levels, lat_rows, lon_cols, 3, head_count, head_size))
    queries = (windows[..., 0, :, :] * head_size ** (-0.5)).astype(jnp.bfloat16)
    keys_win = windows[..., 1, :, :].astype(jnp.bfloat16)
    values_win = windows[..., 2, :, :].astype(jnp.bfloat16)
    scores = batched('abcind,abcjnd->abcnij', queries, keys_win) + bias[:, :, None]
    raised = jnp.where(same, jnp.exp(scores), 0.0)
    probs = raised / lax.optimization_barrier(jnp.sum(raised, axis=-1, keepdims=True))
    probs_low = probs.astype(jnp.bfloat16)
    mixed = batched('abcnij,abcjnd->abcind', probs_low, values_win).astype(jnp.bfloat16)
    mixed_flat = from_windows(mixed.reshape(mixed.shape[:4] + (width,)), levels, lat_rows, lon_cols).reshape(-1, width)
    return (queries, keys_win, values_win, probs, probs_low, mixed_flat)

def block_forward(rolled, qkv_weight, proj_weight, bias, same, head_count):
    pieces = attention_pieces(rolled, qkv_weight, bias, same, head_count)
    output = jnp.dot(pieces[5], proj_weight, preferred_element_type=jnp.float32).astype(jnp.bfloat16)
    return output.reshape(rolled.shape)

def block_backward(rolled, grad_out, qkv_weight, proj_weight, bias, same, head_count):
    queries, keys_win, values_win, probs, probs_low, mixed_flat = attention_pieces(rolled, qkv_weight, bias, same, head_count)
    levels, lat_rows, lon_cols, width = rolled.shape
    head_size = width // head_count
    grad_flat = grad_out.reshape(-1, width)
    proj_grad = lax.dot_general(mixed_flat, grad_flat, (((0,), (0,)), ((), ())), preferred_element_type=jnp.float32)
    grad_mixed = lax.dot_general(grad_flat, proj_weight, (((1,), (1,)), ((), ())), preferred_element_type=jnp.float32).astype(jnp.bfloat16)
    grad_mixed = to_windows(grad_mixed.reshape(levels, lat_rows, lon_cols, head_count, head_size))
    grad_probs = batched('abcind,abcjnd->abcnij', grad_mixed, values_win)
    grad_values = batched('abcnij,abcind->abcjnd', probs_low, grad_mixed)
    grad_scores = probs * (grad_probs - lax.optimization_barrier(jnp.sum(probs * grad_probs, axis=-1, keepdims=True)))
    bias_part = lax.optimization_barrier(jnp.sum(grad_scores, axis=2))
    scores_low = grad_scores.astype(jnp.bfloat16)
    grad_queries = batched('abcnij,abcjnd->abcind', scores_low, keys_win) * head_size ** (-0.5)
    grad_keys = batched('abcnij,abcind->abcjnd', scores_low, queries)
    stacked = jnp.stack([grad_queries, grad_keys, grad_values], axis=4).astype(jnp.bfloat16)
    stacked_flat = from_windows(stacked, levels, lat_rows, lon_cols).reshape(-1, 3 * width)
    qkv_grad = lax.dot_general(rolled.reshape(-1, width), stacked_flat, (((0,), (0,)), ((), ())), preferred_element_type=jnp.float32)
    grad_rolled = lax.dot_general(stacked_flat, qkv_weight, (((1,), (1,)), ((), ())), preferred_element_type=jnp.float32)
    return (grad_rolled.astype(jnp.bfloat16).reshape(rolled.shape), qkv_grad, proj_grad, bias_part)

def by_columns(tensor):
    levels, lat_rows, lon_cols, width = tensor.shape
    return jnp.moveaxis(tensor.reshape(levels, lat_rows, lon_cols // WIN_LON, WIN_LON, width), 2, 0)

def from_columns(columns):
    moved = jnp.moveaxis(columns, 0, 2)
    return moved.reshape(moved.shape[0], moved.shape[1], moved.shape[2] * moved.shape[3], moved.shape[4])

def whole_forward(rolled, qkv_weight, proj_weight, bias, same, head_count):

    def one_column(column):
        return block_forward(column, qkv_weight, proj_weight, bias, same, head_count)
    return from_columns(lax.map(one_column, by_columns(rolled)))

def whole_backward(rolled, grad_out, qkv_weight, proj_weight, bias, same, head_count):
    width = rolled.shape[-1]
    initial = (jnp.zeros((width, 3 * width), jnp.float32), jnp.zeros((width, width), jnp.float32), jnp.zeros(bias.shape, jnp.float32))

    def advance(running, inputs_pair):
        grad_rolled, qkv_grad, proj_grad, bias_part = block_backward(inputs_pair[0], inputs_pair[1], qkv_weight, proj_weight, bias, same, head_count)
        return ((running[0] + qkv_grad, running[1] + proj_grad, running[2] + bias_part), grad_rolled)
    totals, columns = lax.scan(advance, initial, (by_columns(rolled), by_columns(grad_out)))
    return (from_columns(columns), totals)

def roll_in(tensor):
    return jnp.roll(tensor, (-(WIN_LEV // 2), -(WIN_LAT // 2), -(WIN_LON // 2)), axis=(0, 1, 2))

def roll_out(tensor):
    return jnp.roll(tensor, (WIN_LEV // 2, WIN_LAT // 2, WIN_LON // 2), axis=(0, 1, 2))

def merge_rows(tensor):
    levels, lat_rows, lon_cols, width = tensor.shape
    shaped = tensor.reshape(levels, lat_rows // 2, 2, lon_cols // 2, 2, width).transpose(0, 1, 3, 2, 4, 5)
    return shaped.reshape(levels, lat_rows // 2, lon_cols // 2, 4 * width)

def split_rows(tensor):
    levels, half_lat, half_lon, wide = tensor.shape
    shaped = tensor.reshape(levels, half_lat, half_lon, 2, 2, wide // 4).transpose(0, 1, 3, 2, 4, 5)
    return shaped.reshape(levels, 2 * half_lat, 2 * half_lon, wide // 4)

def reference(fine_field, fine_gain, fine_qkv, fine_proj, fine_table, merge_gain, merge_weight, coarse_gain, coarse_qkv, coarse_proj, coarse_table, cotangent):
    levels, lat_rows, lon_cols, width = fine_field.shape
    fine_heads = fine_table.shape[2]
    coarse_heads = coarse_table.shape[2]
    fine_bias = expand_bias(fine_table)
    coarse_bias = expand_bias(coarse_table)
    fine_same = window_mask(levels, lat_rows, 0, 0, levels, lat_rows)
    coarse_same = window_mask(levels, lat_rows // 2, 0, 0, levels, lat_rows // 2)
    normed_fine, hat_fine, inv_fine = layer_norm(fine_field, fine_gain)
    rolled_fine = roll_in(normed_fine)
    fine_branch = roll_out(whole_forward(rolled_fine, fine_qkv, fine_proj, fine_bias, fine_same, fine_heads))
    fine_out = (fine_field.astype(jnp.float32) + fine_branch.astype(jnp.float32)).astype(jnp.bfloat16)
    merged = merge_rows(fine_out)
    normed_merge, hat_merge, inv_merge = layer_norm(merged, merge_gain)
    merge_flat = normed_merge.reshape(-1, 4 * width)
    coarse_in = jnp.dot(merge_flat, merge_weight, preferred_element_type=jnp.float32).astype(jnp.bfloat16)
    coarse_in = coarse_in.reshape(merged.shape[:3] + (merge_weight.shape[1],))
    normed_coarse, hat_coarse, inv_coarse = layer_norm(coarse_in, coarse_gain)
    rolled_coarse = roll_in(normed_coarse)
    coarse_branch = roll_out(whole_forward(rolled_coarse, coarse_qkv, coarse_proj, coarse_bias, coarse_same, coarse_heads))
    coarse_out = (coarse_in.astype(jnp.float32) + coarse_branch.astype(jnp.float32)).astype(jnp.bfloat16)
    grad_coarse_rolled, coarse_totals = whole_backward(rolled_coarse, roll_in(cotangent), coarse_qkv, coarse_proj, coarse_bias, coarse_same, coarse_heads)
    grad_coarse_ln, coarse_gain_grad = layer_norm_back(roll_out(grad_coarse_rolled), coarse_gain, hat_coarse, inv_coarse)
    grad_coarse_in = (cotangent.astype(jnp.float32) + grad_coarse_ln).astype(jnp.bfloat16)
    grad_flat = grad_coarse_in.reshape(-1, grad_coarse_in.shape[-1])
    merge_weight_grad = lax.dot_general(merge_flat, grad_flat, (((0,), (0,)), ((), ())), preferred_element_type=jnp.float32)
    grad_merge_ln = lax.dot_general(grad_flat, merge_weight, (((1,), (1,)), ((), ())), preferred_element_type=jnp.float32)
    grad_merge_ln = grad_merge_ln.astype(jnp.bfloat16).reshape(merged.shape)
    grad_merged, merge_gain_grad = layer_norm_back(grad_merge_ln, merge_gain, hat_merge, inv_merge)
    grad_fine_out = split_rows(grad_merged).astype(jnp.bfloat16)
    grad_fine_rolled, fine_totals = whole_backward(rolled_fine, roll_in(grad_fine_out), fine_qkv, fine_proj, fine_bias, fine_same, fine_heads)
    grad_fine_ln, fine_gain_grad = layer_norm_back(roll_out(grad_fine_rolled), fine_gain, hat_fine, inv_fine)
    field_grad = (grad_fine_out.astype(jnp.float32) + grad_fine_ln).astype(jnp.bfloat16)
    fine_scale = (levels * lat_rows * lon_cols) ** (-0.5)
    coarse_scale = (levels * (lat_rows // 2) * (lon_cols // 2)) ** (-0.5)
    fine_table_scale = (lon_cols // WIN_LON) ** (-0.5)
    coarse_table_scale = (lon_cols // (2 * WIN_LON)) ** (-0.5)
    return (coarse_out, field_grad, fine_gain_grad * fine_scale, fine_totals[0] * fine_scale, fine_totals[1] * fine_scale, bias_grad(fine_totals[2]) * fine_table_scale, merge_gain_grad * coarse_scale, merge_weight_grad * coarse_scale, coarse_gain_grad * coarse_scale, coarse_totals[0] * coarse_scale, coarse_totals[1] * coarse_scale, bias_grad(coarse_totals[2]) * coarse_table_scale)
```

```python
import numpy as np
import jax
import jax.numpy as jnp
from jax import lax
from jax.experimental import pallas as pl
from jax.experimental.pallas import tpu as pltpu
from jax.sharding import PartitionSpec as P

F32, BF = jnp.float32, jnp.bfloat16
EPS = 1e-05
TOK, HALF, LANES = 144, 72, 256
POS, DIAG = 3312, 23
RUN = 6 * DIAG
HEAD = 32
NEG = -1e30
COARSE_ROWS, FINE_ROWS = 2560, 512
VMEM_LIMIT = 56 * 1024 * 1024


def dot(a, b, ca, cb):
    return lax.dot_general(a, b, (((ca,), (cb,)), ((), ())), preferred_element_type=F32)


def mm(a, b):
    return dot(a, b, 1, 0)


def mm_t(a, b):
    return dot(a, b, 1, 1)


def t_mm(a, b):
    return dot(a, b, 0, 0)


def low(x):
    return x.astype(BF)


def split3(x):
    hi = low(x)
    rest = x - hi.astype(F32)
    mid = low(rest)
    return hi, mid, low(rest - mid.astype(F32))


def iota(shape, dim):
    return lax.broadcasted_iota(jnp.int32, shape, dim)


def div_const(x, n):
    return lax.shift_right_logical(x * (65536 // n + 1), 16)


def one_hot(target, count):
    return jnp.where(iota((target.shape[0], count), 1) == target, 1.0, 0.0).astype(BF)


def window_index(rows):
    r = iota((rows, 1), 0)
    z = div_const(r, 72)
    r = r - z * 72
    h = div_const(r, 12)
    return z, h, r - h * 12


def pad_keys(x):
    gap = jnp.zeros((128 - HALF, x.shape[1]), F32)
    return low(jnp.concatenate([x[:HALF], gap, x[HALF:], gap], axis=0))


def unpad_keys(x):
    return jnp.concatenate([x[:HALF], x[128 : 128 + HALF]], axis=0)


def norm(x):
    width = sum(p.shape[1] for p in x)
    mean = sum(jnp.sum(p, axis=1, keepdims=True) for p in x) * (1.0 / width)
    shifted = [p - mean for p in x]
    var = sum(jnp.sum(p * p, axis=1, keepdims=True) for p in shifted) * (1.0 / width)
    inv = lax.rsqrt(var + EPS)
    return [p * inv for p in shifted], inv


def norm_back(grad, gain, hat, inv):
    width = sum(p.shape[1] for p in grad)
    scaled = [g * a for g, a in zip(grad, gain)]
    first = sum(jnp.sum(s, axis=1, keepdims=True) for s in scaled) * (1.0 / width)
    second = sum(jnp.sum(s * n, axis=1, keepdims=True) for s, n in zip(scaled, hat)) * (1.0 / width)
    gains = [jnp.sum(g * n, axis=0, keepdims=True) for g, n in zip(grad, hat)]
    return [inv * (s - first - n * second) for s, n in zip(scaled, hat)], gains


def load_bias(ref, kind, rows):
    return jnp.concatenate([ref[kind, 0, rows], ref[kind, 1, rows]], axis=1)


def head_mask(width, slot):
    lane = iota((1, width), 1)
    return (lane >= slot * HEAD) & (lane < (slot + 1) * HEAD)


def probabilities(q_h, keys, bias):
    e = jnp.exp(mm_t(q_h, keys) + bias)
    return e * (1.0 / jnp.sum(e, axis=1, keepdims=True))


def tile_forward(q, keys, values, bias_of, slots):
    mixed = None
    for slot in range(slots):
        mask = head_mask(q.shape[1], slot)
        p = probabilities(low(jnp.where(mask, q, 0.0)), keys, bias_of(slot))
        o = mm(low(p), values)
        mixed = o if mixed is None else jnp.where(mask, o, mixed)
    return mixed


def tile_both(q, keys, values, gmix, bias_of, bias_grad_to, slots):
    q_low, gmix_low = low(q), low(gmix)
    mixed = gq = gk = gv = None
    for slot in range(slots):
        mask = head_mask(q.shape[1], slot)
        p = probabilities(low(jnp.where(mask, q, 0.0)), keys, bias_of(slot))
        p_low = low(p)
        o = mm(p_low, values)
        gp = mm_t(low(jnp.where(mask, gmix, 0.0)), values)
        gs = p * (gp - jnp.sum(p * gp, axis=1, keepdims=True))
        bias_grad_to(slot, gs)
        gs_low = low(gs)
        dq = mm(gs_low, keys)
        dk = t_mm(gs_low, q_low)
        dv = t_mm(p_low, gmix_low)
        if slot == 0:
            mixed, gq, gk, gv = o, dq, dk, dv
        else:
            mixed = jnp.where(mask, o, mixed)
            gq = jnp.where(mask, dq, gq)
            gk = jnp.where(mask, dk, gk)
            gv = jnp.where(mask, dv, gv)
    return mixed, gq, gk, gv


def diagonal_select(wq):
    lane = iota((1, 128), 1)
    hk = div_const(lane, 12)
    wk = lane - hk * 12
    target = jnp.where(lane < HALF, hk * DIAG + wq - wk + 11, -1)
    return jnp.where(iota((RUN, 128), 0) == target, 1.0, 0.0).astype(BF)


def table_groups():
    return [(g, g // 12, (g // 6) % 2, g % 6) for g in range(24)]


def expand_tables(flags_ref, types, heads, pad, table_of, out_ref, u_ref, lat_flag):
    lane = iota((1, 128), 1)
    lev = flags_ref[0]
    for t in range(types):
        u_ref[...] = jnp.zeros(u_ref.shape, F32)
        table = table_of(t)
        for g, zq, zk, hq in table_groups():
            u_ref[g * pad : g * pad + heads] = table[:, g * RUN : (g + 1) * RUN]
        parts = split3(u_ref[...])
        lat = lat_flag(t)
        lev_term = jnp.where(lev > 0, NEG, 0.0)
        upper = jnp.where((lane >= 36) & (lat > 0), NEG, 0.0)
        lower = jnp.where((lane < 36) & (lat > 0), NEG, 0.0)
        outside = jnp.where(lane >= HALF, NEG, 0.0)
        for wq in range(12):
            sel = diagonal_select(wq)
            x = sum(mm(part, sel) for part in parts)
            for g, zq, zk, hq in table_groups():
                extra = outside + (upper if hq < 3 else lower)
                if zq != zk:
                    extra = extra + lev_term
                rows = x[g * pad : g * pad + heads] + extra
                out_ref[t, zk, pl.ds(zq * 72 + hq * 12 + wq, heads, stride=TOK)] = rows


def fold_tables(types, heads, pad, grad_ref, out_to, y_ref):
    y_ref[...] = jnp.zeros(y_ref.shape, F32)
    for t in range(types):
        acc = None
        for wq in range(12):
            sel = diagonal_select(wq)
            for g, zq, zk, hq in table_groups():
                y_ref[g * pad : g * pad + heads] = grad_ref[
                    t, zk, pl.ds(zq * 72 + hq * 12 + wq, heads, stride=TOK)
                ]
            y = y_ref[...]
            hi = low(y)
            part = mm_t(hi, sel) + mm_t(low(y - hi.astype(F32)), sel)
            acc = part if acc is None else acc + part
        out_to(t, acc)


def bias_kernel(flags_ref, fine_ref, coarse_ref, fine_out, coarse_out, uf_ref, uc_ref):
    last = flags_ref[1]
    expand_tables(
        flags_ref, 2, 6, 8, lambda t: fine_ref[t], fine_out, uf_ref,
        lambda t: last if t == 1 else 0,
    )
    expand_tables(
        flags_ref, 1, 12, 16, lambda t: coarse_ref[t], coarse_out, uc_ref, lambda t: last
    )


def next_bias_kernel(flags_ref, fine_ref, fine_out, uf_ref):
    expand_tables(flags_ref, 1, 6, 8, lambda t: fine_ref[t], fine_out, uf_ref, lambda t: 0)


def pack_kernel(field_ref, cot_ref, *outs):
    for s in range(2):
        for t in range(2):
            out = outs[2 * s + t]
            lev = 1 - s
            row, crow = (3, 3) if t == 0 else (0, 0)
            for h in range(9):
                out[h * 24 : h * 24 + 24] = field_ref[lev, row + h]
            for h in range(3):
                part = cot_ref[lev, crow + h].astype(F32)
                both = jnp.concatenate([part[:, :192], part[:, 192:]], axis=0)
                out[216 + h * 24 : 240 + h * 24] = low(both)


def fine_weights(qkv_ref):
    w = qkv_ref[...]
    return w[:, :192], w[:, 192:384], w[:, 384:]


FINE_TILES = ((0, 128, 4), (128, 64, 2))


def main_kernel(
    b000, b001, b010, b011, b100, b101, b110, b111,
    bias_ref, next_bias_ref, cbias_ref,
    fgain_ref, fqkv_ref, fproj_ref, mgain_ref, mw_ref, cgain_ref, cqkv_ref, cproj_ref,
    x_out, cout_out, gfo_out, latp_out, lonp_out, pack_out, ctab_out,
    x_ref, fo_ref, q_ref, k_ref, v_ref, gm_ref, mix_ref, gq_ref, gk_ref, gv_ref, gb_ref, y_ref,
):
    bufs = ((b000, b001), (b010, b011)), ((b100, b101), (b110, b111))
    _, hh, ww = window_index(HALF)
    for wr in range(3):
        for wc in range(3):
            acc = [None, None]
            for t in ((0,), (0, 1), (1,))[wr]:
                for u in ((0,), (0, 1), (1,))[wc]:
                    lat = 6 * wr + hh - 9 * t
                    lon = 12 * wc + ww - 18 * u
                    good = (lat >= 0) & (lat < 9) & (lon >= 0) & (lon < 18)
                    hot = one_hot(jnp.where(good, lat * 24 + lon + (6 if u == 0 else 0), -1), 288)
                    for z in range(2):
                        part = mm(hot, bufs[z][t][u][...])
                        acc[z] = part if acc[z] is None else acc[z] + part
            for z in range(2):
                x_ref[3 * wr + wc, z * HALF : (z + 1) * HALF] = acc[z]
    for wr in range(2):
        for wc in range(2):
            x_out[2 * wr + wc] = low(x_ref[3 * wr + wc])
    wq, wk, wv = fine_weights(fqkv_ref)

    def fine_window(w, table_ref, wr):
        x = x_ref[w]
        (hat,), _ = norm([x])
        xn = low(hat * fgain_ref[...])
        q = low(mm(xn, wq) * HEAD**-0.5).astype(F32)
        keys = pad_keys(mm(xn, wk))
        values = pad_keys(mm(xn, wv))
        out = None
        for start, width, slots in FINE_TILES:
            lanes = slice(start, start + width)

            def bias_of(slot):
                h = (start // HEAD + slot) * TOK
                return load_bias(table_ref, wr, slice(h, h + TOK))

            mixed = tile_forward(q[:, lanes], keys[:, lanes], values[:, lanes], bias_of, slots)
            part = mm(low(mixed), fproj_ref[lanes])
            out = part if out is None else out + part
        fo_ref[pl.ds(pl.multiple_of(w * TOK, 16), TOK)] = low(x + low(out).astype(F32))

    @pl.loop(0, 6)
    def _(w):
        fine_window(w, bias_ref, div_const(w, 3))

    @pl.loop(6, 9)
    def _(w):
        fine_window(w, next_bias_ref, 0)

    z, i, j = window_index(TOK)
    merged = []
    for p in range(4):
        lat = 3 + 2 * i + p // 2
        lon = 6 + 2 * j + p % 2
        wr, wc = div_const(lat, 6), div_const(lon, 12)
        target = (3 * wr + wc) * TOK + z * HALF + (lat - 6 * wr) * 12 + lon - 12 * wc
        merged.append(mm(one_hot(target, 9 * TOK), fo_ref[...]))
    mhat, minv = norm(merged)
    mgain = [mgain_ref[p : p + 1] for p in range(4)]
    mnorm = [low(h * g) for h, g in zip(mhat, mgain)]
    mweight = [mw_ref[192 * p : 192 * p + 192] for p in range(4)]
    cin = low(sum(mm(n, w) for n, w in zip(mnorm, mweight))).astype(F32)
    (chat,), cinv = norm([cin])
    cgain = cgain_ref[...]
    xc = low(chat * cgain)
    _, ci, cj = window_index(HALF)
    cot_rows = []
    for s in range(2):
        acc = [None, None]
        for t in range(2):
            for u in range(2):
                lat, lon = ci - 3 * t, cj - 6 * u
                good = (lat >= 0) & (lat < 3) & (lon >= 0) & (lon < 6)
                col = 216 + lat * 24 + lon + (6 if u == 0 else 0)
                for half in range(2):
                    hot = one_hot(jnp.where(good, col + half * 12, -1), 288)
                    part = mm(hot, bufs[s][t][u][...])
                    acc[half] = part if acc[half] is None else acc[half] + part
        cot_rows.append(jnp.concatenate(acc, axis=1))
    cot = jnp.concatenate(cot_rows, axis=0)
    gy = low(cot)
    gmix = low(mm_t(gy, cproj_ref[...])).astype(F32)
    for tile in range(3):
        lanes = slice(128 * tile, 128 * tile + 128)
        q_ref[tile] = low(mm(xc, cqkv_ref[:, lanes]) * HEAD**-0.5).astype(F32)
        k_ref[tile] = pad_keys(mm(xc, cqkv_ref[:, 384 + 128 * tile : 512 + 128 * tile]))
        v_ref[tile] = pad_keys(mm(xc, cqkv_ref[:, 768 + 128 * tile : 896 + 128 * tile]))
        gm_ref[tile] = gmix[:, lanes]

    def coarse_tile(tile, carry):
        def bias_of(slot):
            return load_bias(cbias_ref, 0, pl.ds(pl.multiple_of((4 * tile + slot) * TOK, 8), TOK))

        def bias_grad_to(slot, gs):
            rows = pl.ds(pl.multiple_of((4 * tile + slot) * TOK, 8), TOK)
            gb_ref[0, 0, rows] = gs[:, :128]
            gb_ref[0, 1, rows] = gs[:, 128:]

        mixed, gq, gk, gv = tile_both(
            q_ref[tile], k_ref[tile], v_ref[tile], gm_ref[tile], bias_of, bias_grad_to, 4
        )
        mix_ref[tile] = low(mixed)
        gq_ref[tile] = low(gq * HEAD**-0.5)
        gk_ref[tile] = low(unpad_keys(gk))
        gv_ref[tile] = low(unpad_keys(gv))
        return carry

    lax.fori_loop(0, 3, coarse_tile, 0)
    out = None
    grolled = None
    for tile in range(3):
        lanes = slice(128 * tile, 128 * tile + 128)
        part = mm(mix_ref[tile], cproj_ref[lanes])
        out = part if out is None else out + part
        pack_out[1920 + 128 * tile : 2048 + 128 * tile] = low(t_mm(mix_ref[tile], gy))
        for m, ref in enumerate((gq_ref, gk_ref, gv_ref)):
            g = ref[tile]
            pack_out[768 + 384 * m : 1152 + 384 * m, lanes] = low(t_mm(xc, g))
            wcols = slice(384 * m + 128 * tile, 384 * m + 128 * tile + 128)
            part = mm_t(g, cqkv_ref[:, wcols])
            grolled = part if grolled is None else grolled + part
    cout_out[...] = low(cin + low(out).astype(F32))
    (gci,), (cgain_grad,) = norm_back([low(grolled).astype(F32)], [cgain], [chat], cinv)
    gci = low(cot + gci)
    gml = []
    for p in range(4):
        pack_out[192 * p : 192 * p + 192] = low(t_mm(mnorm[p], gci))
        gml.append(low(mm_t(gci, mweight[p])).astype(F32))
    gmerged, mgain_grad = norm_back(gml, mgain, mhat, minv)
    blank = jnp.zeros((1, 192), F32)
    rows = [jnp.concatenate([g, blank], axis=1) for g in mgain_grad] + [cgain_grad]
    rows.append(jnp.zeros((11, 384), F32))
    pack_out[2304:2320] = low(jnp.concatenate(rows, axis=0))
    pack_out[2320:] = jnp.zeros((COARSE_ROWS - 2320, 384), BF)
    r40 = iota((40, 1), 0)
    zi = div_const(r40, 3)
    lon_hot = one_hot(jnp.where(r40 < 36, zi * 12 + 9 + r40 - 3 * zi, -1), TOK)
    for p in range(4):
        g = low(gmerged[p])
        gfo_out[p] = g
        gf = g.astype(F32)
        latp_out[48 * p : 48 * p + 48] = low(jnp.concatenate([gf[48:72], gf[120:144]], axis=0))
        lonp_out[40 * p : 40 * p + 40] = low(mm(lon_hot, g))

    def ctab(t, acc):
        for g in range(24):
            ctab_out[:, g * RUN : (g + 1) * RUN] = low(acc[g * 16 : g * 16 + 12])

    fold_tables(1, 12, 16, gb_ref, ctab, y_ref)


def back_kernel(
    x_in, gfo_ref, latp_ref, lonp_ref, corner_ref, bias_ref, fgain_ref, fqkv_ref, fproj_ref,
    fg_out, pack_out, ftab_out,
    gy_ref, gqkv_ref, gproj_ref, gain_ref, gb_ref, y_ref,
):
    z, h, w = window_index(TOK)
    for wr in range(2):
        for wc in range(2):
            lat, lon = 6 * wr + h, 12 * wc + w
            own = (lat >= 3) & (lon >= 6)

            def parity(a, b):
                return 2 * (a & 1) + (b & 1), lax.shift_right_logical(a, 1), lax.shift_right_logical(b, 1)

            p, i, j = parity(jnp.maximum(lat - 3, 0), jnp.maximum(lon - 6, 0))
            hot = one_hot(jnp.where(own, p * TOK + z * HALF + i * 12 + j, -1), 4 * TOK)
            acc = mm(hot, gfo_ref[...])
            if wr == 0:
                p, i, j = parity(lat + 9, jnp.maximum(lon - 6, 0))
                good = (lat < 3) & (lon >= 6)
                target = p * 48 + z * 24 + (i - 4) * 12 + j
                acc += mm(one_hot(jnp.where(good, target, -1), 192), latp_ref[...])
            if wc == 0:
                p, i, j = parity(jnp.maximum(lat - 3, 0), lon + 18)
                good = (lat >= 3) & (lon < 6)
                target = p * 40 + z * 18 + i * 3 + j - 9
                acc += mm(one_hot(jnp.where(good, target, -1), 160), lonp_ref[...])
            if wr == 0 and wc == 0:
                p, i, j = parity(lat + 9, lon + 18)
                good = (lat < 3) & (lon < 6)
                target = p * 40 + z * 18 + i * 3 + j - 9
                acc += mm(one_hot(jnp.where(good, target, -1), 160), corner_ref[...])
            gy_ref[2 * wr + wc] = acc
    gqkv_ref[...] = jnp.zeros(gqkv_ref.shape, F32)
    gproj_ref[...] = jnp.zeros(gproj_ref.shape, F32)
    gain_ref[...] = jnp.zeros(gain_ref.shape, F32)
    gb_ref[...] = jnp.zeros(gb_ref.shape, F32)
    weights = fine_weights(fqkv_ref)
    gain = fgain_ref[...]

    def fine_window(n, carry):
        x = x_in[n].astype(F32)
        gy32 = gy_ref[n]
        gy = low(gy32)
        (hat,), inv = norm([x])
        xn = low(hat * gain)
        q = low(mm(xn, weights[0]) * HEAD**-0.5).astype(F32)
        keys = pad_keys(mm(xn, weights[1]))
        values = pad_keys(mm(xn, weights[2]))
        gmix = low(mm_t(gy, fproj_ref[...])).astype(F32)
        wr = lax.shift_right_logical(n, 1)
        grolled = None
        for start, width, slots in FINE_TILES:
            lanes = slice(start, start + width)

            def rows_of(slot):
                h = (start // HEAD + slot) * TOK
                return slice(h, h + TOK)

            def bias_grad_to(slot, gs):
                gb_ref[wr, 0, rows_of(slot)] += gs[:, :128]
                gb_ref[wr, 1, rows_of(slot)] += gs[:, 128:]

            mixed, gq, gk, gv = tile_both(
                q[:, lanes], keys[:, lanes], values[:, lanes], gmix[:, lanes],
                lambda slot: load_bias(bias_ref, wr, rows_of(slot)), bias_grad_to, slots,
            )
            gproj_ref[lanes] += t_mm(low(mixed), gy)
            grads = low(gq * HEAD**-0.5), low(unpad_keys(gk)), low(unpad_keys(gv))
            for m, g in enumerate(grads):
                gqkv_ref[m, :, lanes] += t_mm(xn, g)
                part = mm_t(g, weights[m][:, lanes])
                grolled = part if grolled is None else grolled + part
        (gx,), (ggain,) = norm_back([low(grolled).astype(F32)], [gain], [hat], inv)
        gain_ref[...] += ggain
        fg = low(gy32 + gx)
        fg_out[0, pl.ds(pl.multiple_of(n * HALF, 8), HALF)] = fg[:HALF]
        fg_out[1, pl.ds(pl.multiple_of(n * HALF, 8), HALF)] = fg[HALF:]
        return carry

    lax.fori_loop(0, 4, fine_window, 0)
    pack_out[:192] = low(jnp.concatenate([gqkv_ref[0], gqkv_ref[1]], axis=1))
    pack_out[192:384] = low(jnp.concatenate([gqkv_ref[2], gproj_ref[...]], axis=1))
    row = jnp.concatenate([gain_ref[...], jnp.zeros((1, 192), F32)], axis=1)
    pack_out[384:400] = low(jnp.concatenate([row, jnp.zeros((15, 384), F32)], axis=0))
    pack_out[400:] = jnp.zeros((FINE_ROWS - 400, 384), BF)

    def ftab(t, acc):
        for g in range(24):
            ftab_out[t, :, g * RUN : (g + 1) * RUN] = low(acc[g * 8 : g * 8 + 6])

    fold_tables(2, 6, 8, gb_ref, ftab, y_ref)


def place_kernel(*refs):
    fine, coarse, (field_out, coarse_out) = refs[:8], refs[8:16], refs[16:]
    for lev in range(2):
        s = 1 - lev
        for t in range(2):
            rows = 72 if t == 1 else 216
            r = iota((rows, 1), 0)
            row = div_const(r, 24)
            col = r - row * 24
            lat = row + (9 if t == 1 else 0)
            acc = None
            for u in range(2):
                lon = jnp.where(col >= 6, col - 6, col + 18)
                mine = (col < 6) if u == 1 else (col >= 6)
                wr, wc = div_const(lat, 6), div_const(lon, 12)
                inside = (lat - 6 * wr) * 12 + lon - 12 * wc
                wrow = wr - 1 if t == 1 else wr
                wcol = wc - 1 if u == 1 else wc
                cols = 1 if u == 1 else 2
                target = (wrow * cols + wcol) * HALF + inside
                ref = fine[4 * s + 2 * t + u]
                count = ref.shape[0]
                part = mm(one_hot(jnp.where(mine, target, -1), count), ref[...])
                acc = part if acc is None else acc + part
            for h in range(rows // 24):
                field_out[lev, h + (0 if t == 1 else 3)] = low(acc[24 * h : 24 * h + 24])
        acc = None
        r = iota((HALF, 1), 0)
        row = div_const(r, 12)
        col = r - row * 12
        for t in range(2):
            for u in range(2):
                i = row + 3 if t == 1 else row - 3
                j = col + 6 if u == 1 else col - 6
                good = ((row < 3) if t == 1 else (row >= 3)) & ((col < 6) if u == 1 else (col >= 6))
                ref = coarse[4 * s + 2 * t + u]
                part = mm(one_hot(jnp.where(good, i * 12 + j, -1), HALF), ref[...])
                acc = part if acc is None else acc + part
        for h in range(6):
            coarse_out[lev, h] = low(acc[12 * h : 12 * h + 12])


def coarse_unpack_kernel(scale, sums_ref, tab_ref, table_scale, *outs):
    mgain_out, mw_out, cgain_out, cqkv_out, cproj_out, ctab_out = outs
    mw_out[...] = sums_ref[:768].astype(F32) * scale
    for m in range(3):
        cqkv_out[:, 384 * m : 384 * m + 384] = sums_ref[768 + 384 * m : 1152 + 384 * m].astype(F32) * scale
    cproj_out[...] = sums_ref[1920:2304].astype(F32) * scale
    gains = sums_ref[2304:2320].astype(F32) * scale
    mgain_out[...] = jnp.concatenate([gains[p : p + 1, :192] for p in range(4)], axis=1)
    cgain_out[...] = gains[4:5]
    ctab_out[0] = tab_ref[...].astype(F32) * table_scale


def fine_unpack_kernel(scale, sums_ref, tab_ref, table_scale, *outs):
    gain_out, qkv_out, proj_out, ftab_out = outs
    first = sums_ref[:192].astype(F32) * scale
    second = sums_ref[192:384].astype(F32) * scale
    qkv_out[:, :384] = first
    qkv_out[:, 384:] = second[:, :192]
    proj_out[...] = second[:, 192:]
    gain_out[...] = (sums_ref[384:400].astype(F32) * scale)[:1, :192]
    ftab_out[0] = tab_ref[...].astype(F32) * table_scale


def call(kernel, out_shapes, scratch=(), smem=0, flops=0, moved=0):
    def run(*args):
        specs = [pl.BlockSpec(memory_space=pltpu.SMEM)] * smem
        specs += [pl.BlockSpec(memory_space=pltpu.VMEM)] * (len(args) - smem)
        return pl.pallas_call(
            kernel,
            out_shape=[jax.ShapeDtypeStruct(s, d) for s, d in out_shapes],
            in_specs=specs,
            out_specs=[pl.BlockSpec(memory_space=pltpu.VMEM)] * len(out_shapes),
            scratch_shapes=[pltpu.VMEM(s, d) for s, d in scratch],
            compiler_params=pltpu.CompilerParams(vmem_limit_bytes=VMEM_LIMIT),
            cost_estimate=pl.CostEstimate(flops=flops, bytes_accessed=moved, transcendentals=0),
        )(*args)

    return run


def shifted(x, offset, sign):
    names = [n for n, o in zip(("lon", "lat", "rep"), offset[::-1]) if o]
    sizes = [lax.axis_size(n) for n in names]
    pairs = []
    for place in np.ndindex(*sizes):
        target = [(p - sign) % s for p, s in zip(place, sizes)]
        pairs.append((int(np.ravel_multi_index(place, sizes)), int(np.ravel_multi_index(target, sizes))))
    return lax.ppermute(x, tuple(names), pairs)


CORNERS = [(s, t, u) for s in range(2) for t in range(2) for u in range(2)]


def total(x, axes):
    return lax.psum(x, axes)


def body(
    fine_field, fine_gain, fine_qkv, fine_proj, fine_table, merge_gain, merge_weight,
    coarse_gain, coarse_qkv, coarse_proj, coarse_table, cotangent,
):
    rep, lat, lon = (lax.axis_size(n) for n in ("rep", "lat", "lon"))
    everywhere = ("lon", "lat", "rep")
    flags = jnp.stack([lax.axis_index("rep") == rep - 1, lax.axis_index("lat") == lat - 1]).astype(jnp.int32)

    packs = call(pack_kernel, [((288, 192), BF)] * 4)(fine_field, cotangent)
    bufs = []
    for s, t, u in CORNERS:
        b = packs[2 * s + t]
        bufs.append(shifted(b, (s, t, u), 1) if s + t + u else b)
    next_table = shifted(fine_table[:, :1], (0, 1, 0), 1)[0]
    bias, cbias = call(
        bias_kernel,
        [((2, 2, 6 * TOK, 128), F32), ((1, 2, 12 * TOK, 128), F32)],
        [((192, RUN), F32), ((384, RUN), F32)],
        smem=1,
    )(flags, fine_table[0], coarse_table[0])
    (next_bias,) = call(next_bias_kernel, [((1, 2, 6 * TOK, 128), F32)], [((192, RUN), F32)], smem=1)(
        flags, next_table
    )
    fgain = fine_gain.reshape(1, 192)
    x, cout, gfo, latp, lonp, cpack, ctab = call(
        main_kernel,
        [
            ((4, TOK, 192), BF), ((TOK, 384), BF), ((4, TOK, 192), BF), ((192, 192), BF), ((160, 192), BF),
            ((COARSE_ROWS, 384), BF), ((12, POS), BF),
        ],
        [
            ((9, TOK, 192), F32), ((9 * TOK, 192), BF),
            ((3, TOK, 128), F32), ((3, LANES, 128), BF), ((3, LANES, 128), BF), ((3, TOK, 128), F32),
            ((3, TOK, 128), BF), ((3, TOK, 128), BF), ((3, TOK, 128), BF), ((3, TOK, 128), BF),
            ((1, 2, 12 * TOK, 128), F32), ((384, 128), F32),
        ],
    )(
        *bufs, bias, next_bias, cbias, fgain, fine_qkv, fine_proj, merge_gain.reshape(4, 192),
        merge_weight, coarse_gain.reshape(1, 384), coarse_qkv, coarse_proj,
    )
    lat_recv = shifted(latp, (0, 1, 0), -1)
    lon_recv = shifted(lonp, (0, 0, 1), -1)
    corner_recv = shifted(lonp, (0, 1, 1), -1)
    csums = total(cpack, everywhere)
    ctab_sum = total(ctab, "lon")
    coarse_pieces = []
    for s, t, u in CORNERS:
        b = cout[HALF * s : HALF * s + HALF]
        coarse_pieces.append(shifted(b, (s, t, u), -1) if s + t + u else b)
    fg, fpack, ftab = call(
        back_kernel,
        [((2, 4 * HALF, 192), BF), ((FINE_ROWS, 384), BF), ((2, 6, POS), BF)],
        [
            ((4, TOK, 192), F32), ((3, 192, 192), F32), ((192, 192), F32), ((1, 192), F32),
            ((2, 2, 6 * TOK, 128), F32), ((192, 128), F32),
        ],
    )(x, gfo.reshape(4 * TOK, 192), lat_recv, lon_recv, corner_recv, bias, fgain, fine_qkv, fine_proj)
    fsums = total(fpack, everywhere)
    ftab_sum = total(ftab, "lon")
    fine_pieces = []
    for s, t, u in CORNERS:
        b = fg[s].reshape(2, 2, HALF, 192)
        b = (b[1:] if t else b)
        b = (b[:, 1:] if u else b)
        b = b.reshape(-1, 192)
        fine_pieces.append(shifted(b, (s, t, u), -1) if s + t + u else b)
    field_grad, coarse_out = call(
        place_kernel, [((2, 12, 24, 192), BF), ((2, 6, 12, 384), BF)]
    )(*fine_pieces, *coarse_pieces)
    levels, rows, cols = 2 * rep, 12 * lat, 24 * lon
    fine_scale = (levels * rows * cols) ** -0.5
    coarse_scale = (levels * rows * cols // 4) ** -0.5
    fine_table_scale = (cols // 12) ** -0.5
    coarse_table_scale = (cols // 24) ** -0.5
    mgain_g, mw_g, cgain_g, cqkv_g, cproj_g, ctab_g = call(
        lambda a, b, *o: coarse_unpack_kernel(coarse_scale, a, b, coarse_table_scale, *o),
        [((1, 768), F32), ((768, 384), F32), ((1, 384), F32), ((384, 1152), F32), ((384, 384), F32), ((1, 12, POS), F32)],
    )(csums, ctab_sum)
    fgain_g, fqkv_g, fproj_g, ftab_g = call(
        lambda a, b, *o: fine_unpack_kernel(fine_scale, a, b, fine_table_scale, *o),
        [((1, 192), F32), ((192, 576), F32), ((192, 192), F32), ((1, 2, 6, POS), F32)],
    )(fsums, ftab_sum)
    return (
        coarse_out, field_grad, fgain_g.reshape(192), fqkv_g, fproj_g, ftab_g,
        mgain_g.reshape(768), mw_g, cgain_g.reshape(384), cqkv_g, cproj_g, ctab_g.reshape(1, 1, 12, POS),
    )


def solution(mesh):
    tokens, tables = P("rep", "lat", "lon", None), P("rep", "lat", None, None)
    return jax.shard_map(
        body,
        mesh=mesh,
        in_specs=(tokens, P(), P(), P(), tables, P(), P(), P(), P(), P(), tables, tokens),
        out_specs=(tokens, tokens, P(), P(), P(), tables, P(), P(), P(), P(), P(), tables),
        check_vma=False,
    )
```

```python
import numpy as np
import jax
import jax.numpy as jnp
from jax import lax
from jax.experimental import pallas as pl
from jax.experimental.pallas import tpu as pltpu
from jax.sharding import PartitionSpec as P

F32, BF = jnp.float32, jnp.bfloat16
EPS = 1e-05
TOK, HALF, LANES = 144, 72, 256
POS, DIAG = 3312, 23
RUN = 6 * DIAG
HEAD = 32
NEG = -1e30
COARSE, FINE, TAB = 432, 80, 64
GRAIN = COARSE + FINE
WIDE = 3328
VMEM_LIMIT = 56 * 1024 * 1024


def dot(a, b, ca, cb):
    return lax.dot_general(a, b, (((ca,), (cb,)), ((), ())), preferred_element_type=F32)


def mm(a, b):
    return dot(a, b, 1, 0)


def mm_t(a, b):
    return dot(a, b, 1, 1)


def t_mm(a, b):
    return dot(a, b, 0, 0)


def low(x):
    return x.astype(BF)


def split3(x):
    hi = low(x)
    rest = x - hi.astype(F32)
    mid = low(rest)
    return hi, mid, low(rest - mid.astype(F32))


def iota(shape, dim):
    return lax.broadcasted_iota(jnp.int32, shape, dim)


def div_const(x, n):
    return lax.shift_right_logical(x * (65536 // n + 1), 16)


def one_hot(target, count):
    return jnp.where(iota((target.shape[0], count), 1) == target, 1.0, 0.0).astype(BF)


def window_index(rows):
    r = iota((rows, 1), 0)
    z = div_const(r, 72)
    r = r - z * 72
    w = div_const(r, 6)
    return z, r - w * 6, w


def pad_keys(x):
    gap = jnp.zeros((128 - HALF, x.shape[1]), F32)
    return low(jnp.concatenate([x[:HALF], gap, x[HALF:], gap], axis=0))


def unpad_keys(x):
    return jnp.concatenate([x[:HALF], x[128 : 128 + HALF]], axis=0)


def norm(x):
    width = sum(p.shape[1] for p in x)
    mean = sum(jnp.sum(p, axis=1, keepdims=True) for p in x) * (1.0 / width)
    shifted = [p - mean for p in x]
    var = sum(jnp.sum(p * p, axis=1, keepdims=True) for p in shifted) * (1.0 / width)
    inv = lax.rsqrt(var + EPS)
    return [p * inv for p in shifted], inv


def norm_back(grad, gain, hat, inv):
    width = sum(p.shape[1] for p in grad)
    scaled = [g * a for g, a in zip(grad, gain)]
    first = sum(jnp.sum(s, axis=1, keepdims=True) for s in scaled) * (1.0 / width)
    second = sum(jnp.sum(s * n, axis=1, keepdims=True) for s, n in zip(scaled, hat)) * (1.0 / width)
    gains = [jnp.sum(g * n, axis=0, keepdims=True) for g, n in zip(grad, hat)]
    return [inv * (s - first - n * second) for s, n in zip(scaled, hat)], gains


def load_bias(ref, kind, rows):
    return jnp.concatenate([ref[kind, 0, rows], ref[kind, 1, rows]], axis=1)


def head_mask(width, slot):
    lane = iota((1, width), 1)
    return (lane >= slot * HEAD) & (lane < (slot + 1) * HEAD)


def only_head(x, slot):
    return x * jnp.where(head_mask(x.shape[1], slot), 1.0, 0.0).astype(BF)


def by_head(x, slots):
    return jnp.concatenate([only_head(x, slot) for slot in range(slots)], axis=0)


def own_columns(x, slots):
    out = x[:TOK]
    for slot in range(1, slots):
        out = jnp.where(head_mask(x.shape[1], slot), x[slot * TOK : (slot + 1) * TOK], out)
    return out


def probabilities(q_stack, keys, bias):
    e = jnp.exp(mm_t(q_stack, keys) + bias)
    return e * (1.0 / jnp.sum(e, axis=1, keepdims=True))


def tile_forward(q, keys, values, bias, slots):
    p = probabilities(by_head(q, slots), keys, bias)
    return own_columns(mm(low(p), values), slots)


def tile_both(q, keys, values, gmix, bias, bias_grad_to, slots):
    q_stack, g_stack = by_head(q, slots), by_head(gmix, slots)
    p = probabilities(q_stack, keys, bias)
    p_low = low(p)
    mixed = own_columns(mm(p_low, values), slots)
    gp = mm_t(g_stack, values)
    gs = p * (gp - jnp.sum(p * gp, axis=1, keepdims=True))
    bias_grad_to(gs)
    gs_low = low(gs)
    gq = own_columns(mm(gs_low, keys), slots)
    return mixed, gq, t_mm(gs_low, q_stack), t_mm(p_low, g_stack)


def put(ref, grain, start, value, place=lambda chunk: chunk):
    at = 0
    while at < value.shape[0]:
        chunk, row = divmod(start + at, grain)
        n = min(grain - row, value.shape[0] - at)
        ref[place(chunk), row : row + n] = value[at : at + n]
        at += n


def place_of(chunk):
    return chunk % 8 * 2 + chunk // 8


def get_chunk(sums, chunk, rows):
    mine, other, core = sums
    return jnp.where(core == chunk // 8, mine[chunk % 8, rows].astype(F32), other[chunk % 8, rows].astype(F32))


def get(sums, grain, base, start, count):
    parts, at = [], 0
    while at < count:
        chunk, row = divmod(start + at, grain)
        n = min(grain - row, count - at)
        parts.append(get_chunk(sums, chunk, slice(base + row, base + row + n)))
        at += n
    return parts[0] if len(parts) == 1 else jnp.concatenate(parts, axis=0)


def gain_rows(pieces):
    line = pieces[0] if len(pieces) == 1 else jnp.concatenate(pieces, axis=1)
    width = line.shape[1]
    if width % 128:
        line = jnp.concatenate([line, jnp.zeros((1, 128 - width % 128), F32)], axis=1)
    rows = [line[:, 128 * i : 128 * i + 128] for i in range(line.shape[1] // 128)]
    rows.append(jnp.zeros((16 - len(rows), 128), F32))
    return low(jnp.concatenate(rows, axis=0))


def diagonal_select(first):
    lane = iota((1, 256), 1)
    wq = first + lax.shift_right_logical(lane, 7)
    lane = lane & 127
    wk = div_const(lane, 6)
    hk = lane - wk * 6
    diagonal = wq - wk + 11
    low_half = jnp.where((lane < HALF) & (hk < 3), hk * DIAG + diagonal, -1)
    high_half = jnp.where((lane < HALF) & (hk >= 3), (hk - 3) * DIAG + diagonal + 128, -1)
    target = jnp.maximum(low_half, high_half)
    return jnp.where(iota((256, 256), 0) == target, 1.0, 0.0).astype(BF)


HALF_RUN = 3 * DIAG


def table_groups():
    return [(g, (g // 12) * 16 + ((g // 6) % 2) * 8 + g % 6) for g in range(24)]


def table_slice(table, start):
    n = min(128, POS - start)
    part = table[:, start : start + n]
    if n < 128:
        part = jnp.concatenate([part, jnp.zeros((part.shape[0], 128 - n), F32)], axis=1)
    return part


def expand_tables(at_end, kinds, u_ref):
    lane, sub = iota((8, 128), 1), iota((8, 128), 0)
    column = div_const(lane, 6)
    crossing = (sub >= 3) != (lane - column * 6 >= 3)
    outside = jnp.where(lane >= HALF, NEG, 0.0)
    lev_term = jnp.where(at_end[0], NEG, 0.0)
    lat_term = jnp.where(crossing, jnp.where(at_end[1], NEG, 0.0), 0.0)
    u_ref[...] = jnp.zeros(u_ref.shape, F32)
    base = 0
    for table, _, _ in kinds:
        heads = table.shape[0]
        for g, row in table_groups():
            for half in range(2):
                u_ref[half, pl.ds(base + row, heads, stride=32)] = table_slice(table, g * RUN + half * HALF_RUN)
        base += heads * 32
    u = jnp.concatenate([u_ref[0], u_ref[1]], axis=1)
    hi = low(u)
    mid = low(u - hi.astype(F32))
    for first in range(0, 12, 2):
        sel = diagonal_select(first)
        x = mm(hi, sel) + mm(mid, sel)
        base = 0
        for table, may_end, out_ref in kinds:
            same = outside + lat_term if may_end else outside
            terms = same, same + lev_term
            for n in range(table.shape[0]):
                for zq in range(2):
                    for zk in range(2):
                        at = base + zq * 16 + zk * 8
                        for k in range(2):
                            to = n * TOK + zq * HALF + (first + k) * 6
                            part = x[at : at + 8, 128 * k : 128 * k + 128]
                            out_ref[zk, to : to + 6] = (part + terms[zq != zk])[:6]
                base += 32


def fold_tables(types, heads, grad_ref, y_ref, acc_ref, out_to):
    y_ref[...] = jnp.zeros(y_ref.shape, F32)
    for t in range(types):
        acc = None
        for first in range(0, 12, 2):
            sel = diagonal_select(first)
            for n in range(heads):
                for zq in range(2):
                    for zk in range(2):
                        at = n * 32 + zq * 16 + zk * 8
                        for k in range(2):
                            to = n * TOK + zq * HALF + (first + k) * 6
                            y_ref[at : at + 6, 128 * k : 128 * k + 128] = grad_ref[t, zk, to : to + 6]
            y = y_ref[...]
            hi = low(y)
            part = mm_t(hi, sel) + mm_t(low(y - hi.astype(F32)), sel)
            acc = part if acc is None else acc + part
        for half in range(2):
            acc_ref[half] = acc[:, 128 * half : 128 * half + 128]
        for g, row in table_groups():
            for half in range(2):
                out_to(t, g * RUN + half * HALF_RUN, acc_ref[half, pl.ds(row, heads, stride=32)][:, :HALF_RUN])


def bias_kernel(fine_ref, next_ref, coarse_ref, fine_out, coarse_out, u_ref):
    at_end = [lax.axis_index(name) == lax.axis_size(name) - 1 for name in ("rep", "lat")]
    kinds = [
        (fine_ref[:, 0, :], False, fine_out.at[0]),
        (fine_ref[:, 1, :], True, fine_out.at[1]),
        (next_ref[:, 0, :], False, fine_out.at[2]),
        (coarse_ref[:, 0, :], True, coarse_out.at[0]),
    ]
    expand_tables(at_end, kinds, u_ref)


def pack_kernel(field_ref, cot_ref, *outs):
    for s in range(2):
        for t in range(2):
            out = outs[2 * s + t]
            lev = 1 - s
            row, crow = (3, 3) if t == 0 else (0, 0)
            for h in range(9):
                out[h * 24 : h * 24 + 24] = field_ref[lev, row + h]
            for h in range(3):
                part = cot_ref[crow + h, :, lev, :].astype(F32)
                both = jnp.concatenate([part[:, :192], part[:, 192:]], axis=0)
                out[216 + h * 24 : 240 + h * 24] = low(both)


def fine_weights(qkv_ref):
    w = qkv_ref[...]
    return w[:, :192], w[:, 192:384], w[:, 384:]


FINE_TILES = ((0, 128, 4), (128, 64, 2))


def tile_rows(start, slots):
    return slice(start // HEAD * TOK, (start // HEAD + slots) * TOK)


def store_keys(ref, x):
    gap = jnp.zeros((128 - HALF, x.shape[1]), F32)
    for n in range(ref.shape[0]):
        part = x[n * TOK : (n + 1) * TOK]
        for z in range(2):
            ref[n, 128 * z : 128 * z + 128] = low(jnp.concatenate([part[HALF * z : HALF * z + HALF], gap], axis=0))


def main_kernel(
    b000, b001, b010, b011, b100, b101, b110, b111,
    bias_ref, cbias_ref,
    fgain_ref, fqkv_ref, fproj_ref, mgain_ref, mw_ref, cgain_ref, cqkv_ref, cproj_ref,
    x_out, gfo_out, latp_out, lonp_out, cin_out, gy_out, xc_out, mnorm_out, gci_out, mix_ref, g_ref, gb_ref, gains_out,
    x_ref, fo_ref, fq_ref, fk_ref, fv_ref, fm_ref,
    q_ref, k_ref, v_ref, gm_ref,
):
    bufs = ((b000, b001), (b010, b011)), ((b100, b101), (b110, b111))
    _, hh, ww = window_index(HALF)
    seen = set()
    for t in range(2):
        for u in range(2):
            hots = []
            for wr in (t, t + 1):
                for wc in (u, u + 1):
                    lat = 6 * wr + hh - 9 * t
                    lon = 12 * wc + ww - 18 * u
                    good = (lat >= 0) & (lat < 9) & (lon >= 0) & (lon < 18)
                    hots.append(one_hot(jnp.where(good, lat * 24 + lon + (6 if u == 0 else 0), -1), 216))
            hot = jnp.concatenate(hots, axis=0)
            for z in range(2):
                part = mm(hot, bufs[z][t][u][:216])
                for n in range(4):
                    place = 3 * (t + n // 2) + u + n % 2, slice(z * HALF, (z + 1) * HALF)
                    value = part[n * HALF : (n + 1) * HALF]
                    if (place[0], z) in seen:
                        value = value + x_ref[place]
                    seen.add((place[0], z))
                    x_ref[place] = value
    for wr in range(2):
        for wc in range(2):
            x_out[2 * wr + wc] = low(x_ref[3 * wr + wc])
    wq, wk, wv = fine_weights(fqkv_ref)
    x = x_ref[...].reshape(9 * TOK, 192)
    (hat,), _ = norm([x])
    xn = low(hat * fgain_ref[...].reshape(1, 192))
    fq_ref[...] = low(mm(xn, wq) * HEAD**-0.5).reshape(9, TOK, 192)
    store_keys(fk_ref, mm(xn, wk))
    store_keys(fv_ref, mm(xn, wv))

    def fine_window(w, table_ref, wr):
        for start, width, slots in FINE_TILES:
            lanes = slice(start, start + width)

            bias = load_bias(table_ref, wr, tile_rows(start, slots))
            fm_ref[w, :, lanes] = low(
                tile_forward(fq_ref[w, :, lanes], fk_ref[w, :, lanes], fv_ref[w, :, lanes], bias, slots)
            )

    @pl.loop(0, 9)
    def _(w):
        fine_window(w, bias_ref, div_const(w, 3))

    out = low(mm(fm_ref[...].reshape(9 * TOK, 192), fproj_ref[...])).astype(F32)
    fo_ref[...] = low(x_ref[...].reshape(9 * TOK, 192) + out)

    z, i, j = window_index(TOK)
    hots = []
    for p in range(4):
        lat = 3 + 2 * i + p // 2
        lon = 6 + 2 * j + p % 2
        wr, wc = div_const(lat, 6), div_const(lon, 12)
        target = (3 * wr + wc) * TOK + z * HALF + (lon - 12 * wc) * 6 + lat - 6 * wr
        hots.append(one_hot(target, 9 * TOK))
    merged = mm(jnp.concatenate(hots, axis=0), fo_ref[...])
    merged = [merged[p * TOK : (p + 1) * TOK] for p in range(4)]
    mhat, minv = norm(merged)
    mgain = mgain_ref[...].reshape(1, 768)
    mgain = [mgain[:, 192 * p : 192 * p + 192] for p in range(4)]
    mnorm = [low(h * g) for h, g in zip(mhat, mgain)]
    mweight = [mw_ref[192 * p : 192 * p + 192] for p in range(4)]
    cin = low(sum(mm(n, w) for n, w in zip(mnorm, mweight))).astype(F32)
    (chat,), cinv = norm([cin])
    cgain = cgain_ref[...].reshape(1, 384)
    xc = low(chat * cgain)
    _, ci, cj = window_index(HALF)
    cot_rows = [None, None]
    for t in range(2):
        for u in range(2):
            lat, lon = ci - 3 * t, cj - 6 * u
            good = (lat >= 0) & (lat < 3) & (lon >= 0) & (lon < 6)
            col = lat * 24 + lon + (6 if u == 0 else 0)
            hot = jnp.concatenate([one_hot(jnp.where(good, col + 12 * half, -1), HALF) for half in range(2)], axis=0)
            for s in range(2):
                part = mm(hot, bufs[s][t][u][216:])
                cot_rows[s] = part if cot_rows[s] is None else cot_rows[s] + part
    cot_rows = [jnp.concatenate([c[:HALF], c[HALF:]], axis=1) for c in cot_rows]
    cot = jnp.concatenate(cot_rows, axis=0)
    gy = low(cot)
    gmix = low(mm_t(gy, cproj_ref[...]))
    for tile in range(3):
        lanes = slice(128 * tile, 128 * tile + 128)
        q_ref[tile] = low(mm(xc, cqkv_ref[:, lanes]) * HEAD**-0.5)
        k_ref[tile] = pad_keys(mm(xc, cqkv_ref[:, 384 + 128 * tile : 512 + 128 * tile]))
        v_ref[tile] = pad_keys(mm(xc, cqkv_ref[:, 768 + 128 * tile : 896 + 128 * tile]))
        gm_ref[tile] = gmix[:, lanes]

    def coarse_tile(tile, carry):
        rows = pl.ds(pl.multiple_of(tile * 4 * TOK, 64), 4 * TOK)

        def bias_grad_to(gs):
            gb_ref[0, 0, rows] = gs[:, :128]
            gb_ref[0, 1, rows] = gs[:, 128:]

        mixed, gq, gk, gv = tile_both(
            q_ref[tile], k_ref[tile], v_ref[tile], gm_ref[tile], load_bias(cbias_ref, 0, rows), bias_grad_to, 4
        )
        mix_ref[tile] = low(mixed)
        g_ref[0, tile] = low(gq * HEAD**-0.5)
        g_ref[1, tile] = low(unpad_keys(gk))
        g_ref[2, tile] = low(unpad_keys(gv))
        return carry

    lax.fori_loop(0, 3, coarse_tile, 0)
    grolled = None
    for tile in range(3):
        for m in range(3):
            wcols = slice(384 * m + 128 * tile, 384 * m + 128 * tile + 128)
            part = mm_t(g_ref[m, tile], cqkv_ref[:, wcols])
            grolled = part if grolled is None else grolled + part
    cin_out[...] = low(cin)
    gy_out[...] = gy
    xc_out[...] = xc
    (gci,), (cgain_grad,) = norm_back([low(grolled).astype(F32)], [cgain], [chat], cinv)
    gci = low(cot + gci)
    gml = []
    gci_out[...] = gci
    for p in range(4):
        mnorm_out[p] = mnorm[p]
        gml.append(low(mm_t(gci, mweight[p])).astype(F32))
    gmerged, mgain_grad = norm_back(gml, mgain, mhat, minv)
    gains_out[...] = gain_rows(list(mgain_grad) + [cgain_grad])
    r48 = iota((48, 1), 0)
    zi = div_const(r48, 24)
    rest = r48 - 24 * zi
    lat_hot = one_hot(zi * HALF + lax.shift_right_logical(rest, 1) * 6 + 4 + (rest & 1), TOK)
    r40 = iota((40, 1), 0)
    zi = jnp.where(r40 >= 18, 1, 0)
    lon_hot = one_hot(jnp.where(r40 < 36, zi * HALF + 54 + r40 - 18 * zi, -1), TOK)
    hot = jnp.concatenate([lat_hot, lon_hot], axis=0)
    for p in range(4):
        g = low(gmerged[p])
        gfo_out[p] = g
        part = low(mm(hot, g))
        latp_out[48 * p : 48 * p + 48] = part[:48]
        lonp_out[40 * p : 40 * p + 40] = part[48:]


def side_kernel(
    cin_ref, gy_ref, xc_ref, mnorm_ref, gci_ref, mix_ref, g_ref, gb_ref, cproj_ref,
    cout_out, pack_out, ctab_out, y_ref, acc_ref,
):
    gy, xc, gci = gy_ref[...], xc_ref[...], gci_ref[...]
    out = None
    for tile in range(3):
        lanes = slice(128 * tile, 128 * tile + 128)
        part = mm(mix_ref[tile], cproj_ref[lanes])
        out = part if out is None else out + part
        dproj = low(t_mm(mix_ref[tile], gy))
        for c in range(3):
            start = 5760 + 384 * c + 128 * tile
            put(pack_out, COARSE, start, dproj[:, 128 * c : 128 * c + 128])
    cout_out[...] = low(cin_ref[...].astype(F32) + low(out).astype(F32))
    for m in range(3):
        dqkv = low(t_mm(xc, jnp.concatenate([g_ref[m, tile] for tile in range(3)], axis=1)))
        for tile in range(3):
            start = 2304 + 384 * (3 * m + tile)
            put(pack_out, COARSE, start, dqkv[:, 128 * tile : 128 * tile + 128])
    for p in range(4):
        dmw = low(t_mm(mnorm_ref[p], gci))
        for c in range(3):
            start = 768 * c + 192 * p
            put(pack_out, COARSE, start, dmw[:, 128 * c : 128 * c + 128])
    ctab_out[...] = jnp.zeros(ctab_out.shape, F32)

    def ctab(t, start, rows):
        ctab_out[:12, start : start + HALF_RUN] = rows

    fold_tables(1, 12, gb_ref, y_ref, acc_ref, ctab)


QUARTERS = ((0, 0), (1, 0), (0, 1), (1, 1))
FINE_PAD = (176, 64, 64, 32)
PIECE = tuple(n + 48 for n in FINE_PAD)


def fine_rows_of(s, t, u):
    r = iota((FINE_PAD[QUARTERS.index((t, u))], 1), 0)
    width, height = 6 if u else 18, 3 if t else 9
    row = div_const(r, width)
    lat, lon = row + 9 * t, r - row * width + 18 * u
    wr, wc = div_const(lat, 6), div_const(lon, 12)
    target = (2 * wr + wc) * TOK + s * HALF + (lon - 12 * wc) * 6 + lat - 6 * wr
    return jnp.where(row < height, target, -1)


def coarse_rows_of(s, t, u):
    r = iota((24, 1), 0)
    row = div_const(r, 6)
    return jnp.where(row < 3, s * HALF + (r - row * 6 + 6 * u) * 6 + row + 3 * t, -1)


def back_kernel(
    x_in, gfo_ref, latp_ref, lonp_ref, corner_ref, bias_ref, fgain_ref, fqkv_ref, fproj_ref, ctab_ref, gains_ref, cout_ref,
    p000, p010, p001, p011, p100, p110, p101, p111, pack_out,
    src_ref, fq_ref, fk_ref, fv_ref, fm_ref, gm_ref, g_ref, gb_ref, y_ref, acc_ref, tab_ref,
):
    src_ref[:576] = gfo_ref[...]
    src_ref[576:768] = latp_ref[...]
    src_ref[768:928] = lonp_ref[...]
    src_ref[928:] = corner_ref[...]
    z, h, w = window_index(TOK)
    hots = []
    for wr in range(2):
        for wc in range(2):
            lat, lon = 6 * wr + h, 12 * wc + w
            behind, before = lat < 3, lon < 6
            lat = jnp.where(behind, lat + 9, lat - 3)
            lon = jnp.where(before, lon + 18, lon - 6)
            p = 2 * (lat & 1) + (lon & 1)
            i, j = lax.shift_right_logical(lat, 1), lax.shift_right_logical(lon, 1)
            own = p * TOK + z * HALF + j * 6 + i
            from_lat = 576 + p * 48 + z * 24 + j * 2 + i - 4
            from_lon = 768 + p * 40 + z * 18 + (j - 9) * 6 + i
            target = jnp.where(before, from_lon + jnp.where(behind, 160, 0), jnp.where(behind, from_lat, own))
            hots.append(one_hot(target, 1088))
    gy = low(mm(jnp.concatenate(hots, axis=0), src_ref[...]))
    gy32 = gy.astype(F32)
    gb_ref[...] = jnp.zeros(gb_ref.shape, F32)
    weights = fine_weights(fqkv_ref)
    gain = fgain_ref[...].reshape(1, 192)
    x = x_in[...].reshape(4 * TOK, 192).astype(F32)
    (hat,), inv = norm([x])
    xn = low(hat * gain)
    fq_ref[...] = low(mm(xn, weights[0]) * HEAD**-0.5).reshape(4, TOK, 192)
    store_keys(fk_ref, mm(xn, weights[1]))
    store_keys(fv_ref, mm(xn, weights[2]))
    gm_ref[...] = low(mm_t(gy, fproj_ref[...])).reshape(4, TOK, 192)

    @pl.loop(0, 4)
    def _(n):
        wr = lax.shift_right_logical(n, 1)
        for start, width, slots in FINE_TILES:
            lanes = slice(start, start + width)

            rows = tile_rows(start, slots)

            def bias_grad_to(gs):
                gb_ref[wr, 0, rows] += gs[:, :128]
                gb_ref[wr, 1, rows] += gs[:, 128:]

            mixed, gq, gk, gv = tile_both(
                fq_ref[n, :, lanes], fk_ref[n, :, lanes], fv_ref[n, :, lanes], gm_ref[n, :, lanes],
                load_bias(bias_ref, wr, rows), bias_grad_to, slots,
            )
            fm_ref[n, :, lanes] = low(mixed)
            g_ref[0, n, :, lanes] = low(gq * HEAD**-0.5)
            g_ref[1, n, :, lanes] = low(unpad_keys(gk))
            g_ref[2, n, :, lanes] = low(unpad_keys(gv))

    dproj = t_mm(fm_ref[...].reshape(4 * TOK, 192), gy)
    grads = [g_ref[m].reshape(4 * TOK, 192) for m in range(3)]
    dqkv = [t_mm(xn, g) for g in grads]
    grolled = sum(mm_t(g, w) for g, w in zip(grads, weights))
    (gx,), (ggain,) = norm_back([low(grolled).astype(F32)], [gain], [hat], inv)
    fg = low(gy32 + gx)
    cout = cout_ref[...]
    for s, outs in enumerate(((p000, p010, p001, p011), (p100, p110, p101, p111))):
        hots, coarse_hots = [], []
        for t, u in QUARTERS:
            hots.append(one_hot(fine_rows_of(s, t, u), 4 * TOK))
            coarse_hots.append(one_hot(coarse_rows_of(s, t, u), TOK))
        fine = low(mm(jnp.concatenate(hots, axis=0), fg))
        coarse = low(mm(jnp.concatenate(coarse_hots, axis=0), cout))
        at = 0
        for n, ((t, u), out) in enumerate(zip(QUARTERS, outs)):
            rows = FINE_PAD[n]
            out[:rows] = fine[at : at + rows]
            out[rows : rows + 24] = coarse[24 * n : 24 * n + 24, :192]
            out[rows + 24 :] = coarse[24 * n : 24 * n + 24, 192:]
            at += rows
    first = low(jnp.concatenate([dqkv[0], dqkv[1]], axis=1))
    second = low(jnp.concatenate([dqkv[2], dproj], axis=1))
    for c in range(3):
        put(pack_out, FINE, 192 * c, first[:, 128 * c : 128 * c + 128], place_of)
        put(pack_out, FINE, 576 + 192 * c, second[:, 128 * c : 128 * c + 128], place_of)
    put(pack_out, FINE, 1152, gain_rows([ggain]), place_of)
    put(pack_out, FINE, 1168, gains_ref[...], place_of)
    put(pack_out, FINE, 1184, jnp.zeros((96, 128), BF), place_of)
    tab_ref[...] = jnp.zeros(tab_ref.shape, F32)
    tab_ref[16:32] = ctab_ref[...]

    def ftab(t, start, rows):
        tab_ref[8 * t : 8 * t + 6, start : start + HALF_RUN] = rows

    fold_tables(2, 6, gb_ref, y_ref, acc_ref, ftab)
    for c in range(13):
        for half in range(2):
            lanes = slice(256 * c + 128 * half, 256 * c + 128 * half + 128)
            pack_out[place_of(c), FINE + 32 * half : FINE + 32 * half + 32] = low(tab_ref[:, lanes])
    for c in range(13, 16):
        pack_out[place_of(c), FINE:] = jnp.zeros((TAB, 128), BF)


def place_kernel(*refs):
    field_out, coarse_out, src_ref = refs[8:]
    base = [sum(PIECE[:n]) for n in range(4)]

    def chosen(later_row, later_col, values):
        near = jnp.where(later_row, values[1], values[0])
        return jnp.where(later_col, jnp.where(later_row, values[3], values[2]), near)

    r = iota((288, 1), 0)
    lat = div_const(r, 24)
    col = r - lat * 24
    later_row, later_col = lat < 3, col < 6
    row = jnp.where(later_row, lat, lat - 3)
    inside = jnp.where(later_col, row * 6 + col, row * 18 + col - 6)
    hots = [one_hot(chosen(later_row, later_col, base) + inside, sum(PIECE))]
    r = iota((HALF, 1), 0)
    lat = div_const(r, 12)
    col = r - lat * 12
    later_row, later_col = lat < 3, col < 6
    inside = jnp.where(later_row, lat, lat - 3) * 6 + jnp.where(later_col, col, col - 6)
    inside = inside + chosen(later_row, later_col, [b + n for b, n in zip(base, FINE_PAD)])
    hots += [one_hot(inside, sum(PIECE)), one_hot(inside + 24, sum(PIECE))]
    hot = jnp.concatenate(hots, axis=0)
    for s in range(2):
        for n in range(4):
            src_ref[base[n] : base[n] + PIECE[n]] = refs[4 * s + n][...]
        out = low(mm(hot, src_ref[...]))
        for h in range(12):
            field_out[1 - s, h] = out[24 * h : 24 * h + 24]
        coarse = jnp.concatenate([out[288:360], out[360:]], axis=1)
        for h in range(6):
            coarse_out[h, :, 1 - s, :] = coarse[12 * h : 12 * h + 12]


def unpack_kernel(fine_scale, coarse_scale, fine_table_scale, coarse_table_scale, mine_ref, other_ref, *outs):
    sums = mine_ref, other_ref, lax.axis_index("lon") % 2
    fgain_out, qkv_out, proj_out, ftab_out, mgain_out, mw_out, cgain_out, cqkv_out, cproj_out, ctab_out = outs
    def coarse_get(start, count):
        return get(sums, COARSE, 0, start, count) * coarse_scale

    def fine_get(start, count, scale):
        return get(sums, FINE, COARSE, start, count) * scale

    for c in range(3):
        lanes = slice(128 * c, 128 * c + 128)
        mw_out[:, lanes] = coarse_get(768 * c, 768)
        cproj_out[:, lanes] = coarse_get(5760 + 384 * c, 384)
        qkv_out[:, lanes] = fine_get(192 * c, 192, fine_scale)
    for c in range(9):
        cqkv_out[:, 128 * c : 128 * c + 128] = coarse_get(2304 + 384 * c, 384)
    second = [fine_get(576 + 192 * c, 192, fine_scale) for c in range(3)]
    qkv_out[:, 384:512] = second[0]
    qkv_out[:, 512:] = second[1][:, :64]
    proj_out[...] = jnp.concatenate([second[1][:, 64:], second[2]], axis=1)
    gains = fine_get(1168, 16, coarse_scale)
    for c in range(6):
        mgain_out[pl.ds(128 * c, 128)] = gains[c]
    for c in range(3):
        cgain_out[pl.ds(128 * c, 128)] = gains[6 + c]
    gains = fine_get(1152, 16, fine_scale)
    fgain_out[pl.ds(0, 128)] = gains[0]
    fgain_out[pl.ds(128, 64)] = gains[1, :64]
    for c in range(13):
        for half in range(2):
            start = 256 * c + 128 * half
            n = min(128, POS - start)
            block = get_chunk(sums, c, slice(GRAIN + 32 * half, GRAIN + 32 * half + 32))[:, :n]
            for t in range(2):
                ftab_out[:, t, start : start + n] = block[8 * t : 8 * t + 6] * fine_table_scale
            ctab_out[:, 0, start : start + n] = block[16:28] * coarse_table_scale


def call(kernel, out_shapes, scratch=(), smem=0, flops=0, moved=0):
    def run(*args):
        specs = [pl.BlockSpec(memory_space=pltpu.SMEM)] * smem
        specs += [pl.BlockSpec(memory_space=pltpu.VMEM)] * (len(args) - smem)
        return pl.pallas_call(
            kernel,
            out_shape=[jax.ShapeDtypeStruct(s, d) for s, d in out_shapes],
            in_specs=specs,
            out_specs=[pl.BlockSpec(memory_space=pltpu.VMEM)] * len(out_shapes),
            scratch_shapes=[pltpu.VMEM(s, d) for s, d in scratch],
            compiler_params=pltpu.CompilerParams(vmem_limit_bytes=VMEM_LIMIT),
            cost_estimate=pl.CostEstimate(flops=flops, bytes_accessed=moved, transcendentals=0),
        )(*args)

    return run


def shifted(x, offset, sign):
    names = [n for n, o in zip(("lon", "lat", "rep"), offset[::-1]) if o]
    sizes = [lax.axis_size(n) for n in names]
    pairs = []
    for place in np.ndindex(*sizes):
        target = [(p - sign) % s for p, s in zip(place, sizes)]
        pairs.append((int(np.ravel_multi_index(place, sizes)), int(np.ravel_multi_index(target, sizes))))
    return lax.ppermute(x, tuple(names), pairs)


CORNERS = [(s, t, u) for s in range(2) for t in range(2) for u in range(2)]


def exchange(x, axes):
    return lax.all_to_all(lax.optimization_barrier(x), axes, 0, 0, tiled=True)


def summed(x):
    return jnp.sum(x.astype(F32), axis=0, keepdims=True).astype(BF)


def spread(x, count):
    return jnp.broadcast_to(x, (count,) + x.shape[1:])


def sibling(x):
    return lax.ppermute(x, "lon", [(i, i ^ 1) for i in range(lax.axis_size("lon"))])


def exchange_columns(x):
    size = lax.axis_size("lon")
    groups = [list(range(core, size, 2)) for core in range(2)]
    return lax.all_to_all(lax.optimization_barrier(x), "lon", 0, 0, axis_index_groups=groups, tiled=True)


def reduce_coarse(coarse):
    core = lax.axis_index("lon") % 2
    keep, send = (lax.dynamic_slice_in_dim(coarse, 8 * c, 8) for c in (core, 1 - core))
    both = (keep.astype(F32) + sibling(send).astype(F32)).astype(BF)
    return exchange_columns(both)


def reduce_everywhere(got, pack, beside):
    rest = lax.axis_size("lat") * lax.axis_size("rep")
    got, pack = lax.optimization_barrier((got, pack))
    pack, beside = lax.optimization_barrier((exchange(pack, "lon"), beside))
    got, pack = summed(got), summed(pack)
    part = jnp.concatenate([got, pack[:, :FINE]], axis=1).reshape(rest, -1, 128)
    part = summed(exchange(part, ("lat", "rep")))
    part = exchange(spread(part, rest), ("lat", "rep")).reshape(1, GRAIN, 128)
    mine = jnp.concatenate([part, pack[:, FINE:]], axis=1)
    mine = exchange_columns(spread(mine, lax.axis_size("lon") // 2))
    return (mine, sibling(mine)), beside


def body(
    fine_field, fine_gain, fine_qkv, fine_proj, fine_table, merge_gain, merge_weight,
    coarse_gain, coarse_qkv, coarse_proj, coarse_table, cotangent,
):
    rep, lat, lon = (lax.axis_size(n) for n in ("rep", "lat", "lon"))
    packs = call(pack_kernel, [((288, 192), BF)] * 4)(fine_field, cotangent.transpose(1, 2, 0, 3))
    bufs = []
    for s, t, u in CORNERS:
        b = packs[2 * s + t]
        bufs.append(shifted(b, (s, t, u), 1) if s + t + u else b)
    table = fine_table[0].transpose(1, 0, 2)
    bias, cbias = call(
        bias_kernel,
        [((3, 2, 6 * TOK, 128), F32), ((1, 2, 12 * TOK, 128), F32)],
        [((2, 30 * 32, 128), F32)],
        flops=1 << 32,
    )(table, shifted(fine_table, (0, 1, 0), 1)[0].transpose(1, 0, 2), coarse_table[0].transpose(1, 0, 2))
    x, gfo, latp, lonp, *coarse, cgains = call(
        main_kernel,
        [
            ((4, TOK, 192), BF), ((4, TOK, 192), BF), ((192, 192), BF), ((160, 192), BF),
            ((TOK, 384), BF), ((TOK, 384), BF), ((TOK, 384), BF), ((4, TOK, 192), BF), ((TOK, 384), BF),
            ((3, TOK, 128), BF), ((3, 3, TOK, 128), BF), ((1, 2, 12 * TOK, 128), F32), ((16, 128), BF),
        ],
        [
            ((9, TOK, 192), F32), ((9 * TOK, 192), BF),
            ((9, TOK, 192), BF), ((9, LANES, 192), BF), ((9, LANES, 192), BF), ((9, TOK, 192), BF),
            ((3, TOK, 128), BF), ((3, LANES, 128), BF), ((3, LANES, 128), BF), ((3, TOK, 128), BF),
        ],
        flops=1 << 34,
    )(
        *bufs, bias, cbias, fine_gain, fine_qkv, fine_proj, merge_gain,
        merge_weight, coarse_gain, coarse_qkv, coarse_proj,
    )
    lat_recv = shifted(latp, (0, 1, 0), -1)
    lon_recv = shifted(lonp, (0, 0, 1), -1)
    corner_recv = shifted(lonp, (0, 1, 1), -1)
    cout, cpack, ctab = call(
        side_kernel,
        [((TOK, 384), BF), ((16, COARSE, 128), BF), ((16, WIDE), F32)],
        [((384, 256), F32), ((2, 384, 128), F32)],
        flops=1 << 32,
    )(*coarse, coarse_proj)
    got = reduce_coarse(cpack)
    *pieces, pack = call(
        back_kernel,
        [((n, 192), BF) for n in PIECE + PIECE] + [((16, FINE + TAB, 128), BF)],
        [
            ((1088, 192), BF), ((4, TOK, 192), BF), ((4, LANES, 192), BF), ((4, LANES, 192), BF),
            ((4, TOK, 192), BF), ((4, TOK, 192), BF), ((3, 4, TOK, 192), BF),
            ((2, 2, 6 * TOK, 128), F32), ((192, 256), F32), ((2, 192, 128), F32), ((32, WIDE), F32),
        ],
        flops=1 << 33,
    )(x, gfo.reshape(4 * TOK, 192), lat_recv, lon_recv, corner_recv, bias, fine_gain, fine_qkv, fine_proj, ctab, cgains, cout)
    places = [(s, t, u) for s in range(2) for t, u in QUARTERS]
    pieces = [shifted(b, place, -1) if any(place) else b for b, place in zip(pieces, places)]
    sums, pieces = reduce_everywhere(got, pack, pieces)
    field_grad, coarse_out = call(
        place_kernel, [((2, 12, 24, 192), BF), ((6, 12, 2, 384), BF)], [((sum(PIECE), 192), BF)]
    )(*pieces)
    levels, rows, cols = 2 * rep, 12 * lat, 24 * lon
    fine_scale = (levels * rows * cols) ** -0.5
    coarse_scale = (levels * rows * cols // 4) ** -0.5
    fine_table_scale = (cols // 12) ** -0.5
    coarse_table_scale = (cols // 24) ** -0.5
    fgain_g, fqkv_g, fproj_g, ftab_g, mgain_g, mw_g, cgain_g, cqkv_g, cproj_g, ctab_g = call(
        lambda *refs: unpack_kernel(fine_scale, coarse_scale, fine_table_scale, coarse_table_scale, *refs),
        [
            ((192,), F32), ((192, 576), F32), ((192, 192), F32), ((6, 2, POS), F32), ((768,), F32),
            ((768, 384), F32), ((384,), F32), ((384, 1152), F32), ((384, 384), F32), ((12, 1, POS), F32),
        ],
    )(*sums)
    return (
        coarse_out.transpose(2, 0, 1, 3), field_grad, fgain_g, fqkv_g, fproj_g, ftab_g.transpose(1, 0, 2)[None],
        mgain_g, mw_g, cgain_g, cqkv_g, cproj_g, ctab_g.transpose(1, 0, 2)[None],
    )


def solution(mesh):
    tokens, tables = P("rep", "lat", "lon", None), P("rep", "lat", None, None)
    return jax.shard_map(
        body,
        mesh=mesh,
        in_specs=(tokens, P(), P(), P(), tables, P(), P(), P(), P(), P(), tables, tokens),
        out_specs=(tokens, tokens, P(), P(), P(), tables, P(), P(), P(), P(), P(), tables),
        check_vma=False,
    )
```

```python
import numpy as np
import jax
import jax.numpy as jnp
from jax import lax
from jax.experimental import pallas as pl
from jax.experimental.pallas import tpu as pltpu
from jax.sharding import PartitionSpec as P

F32, BF = jnp.float32, jnp.bfloat16
EPS = 1e-05
TOK, HALF, LANES = 144, 72, 256
POS, DIAG = 3312, 23
RUN = 6 * DIAG
HEAD = 32
NEG = -1e30
COARSE, FINE, TAB = 432, 80, 64
GRAIN = COARSE + FINE
WIDE = 3456
FINE_ROWS, COARSE_ROWS = 6 * TOK + 8, 12 * TOK + 8
VMEM_LIMIT = 24 * 1024 * 1024


def dot(a, b, ca, cb):
    return lax.dot_general(a, b, (((ca,), (cb,)), ((), ())), preferred_element_type=F32)


def mm(a, b):
    return dot(a, b, 1, 0)


def mm_t(a, b):
    return dot(a, b, 1, 1)


def t_mm(a, b):
    return dot(a, b, 0, 0)


def low(x):
    return x.astype(BF)


def split3(x):
    hi = low(x)
    rest = x - hi.astype(F32)
    mid = low(rest)
    return hi, mid, low(rest - mid.astype(F32))


def iota(shape, dim):
    return lax.broadcasted_iota(jnp.int32, shape, dim)


def div_const(x, n):
    return lax.shift_right_logical(x * (65536 // n + 1), 16)


def one_hot(target, count):
    return jnp.where(iota((target.shape[0], count), 1) == target, 1.0, 0.0).astype(BF)


def window_index(rows):
    r = iota((rows, 1), 0)
    z = div_const(r, 72)
    r = r - z * 72
    w = div_const(r, 6)
    return z, r - w * 6, w


def pad_keys(x):
    gap = jnp.zeros((128 - HALF, x.shape[1]), F32)
    return low(jnp.concatenate([x[:HALF], gap, x[HALF:], gap], axis=0))


def unpad_keys(x):
    return jnp.concatenate([x[:HALF], x[128 : 128 + HALF]], axis=0)


def norm(x):
    width = sum(p.shape[1] for p in x)
    mean = sum(jnp.sum(p, axis=1, keepdims=True) for p in x) * (1.0 / width)
    shifted = [p - mean for p in x]
    var = sum(jnp.sum(p * p, axis=1, keepdims=True) for p in shifted) * (1.0 / width)
    inv = lax.rsqrt(var + EPS)
    return [p * inv for p in shifted], inv


def norm_back(grad, gain, hat, inv):
    width = sum(p.shape[1] for p in grad)
    scaled = [g * a for g, a in zip(grad, gain)]
    first = sum(jnp.sum(s, axis=1, keepdims=True) for s in scaled) * (1.0 / width)
    second = sum(jnp.sum(s * n, axis=1, keepdims=True) for s, n in zip(scaled, hat)) * (1.0 / width)
    gains = [jnp.sum(g * n, axis=0, keepdims=True) for g, n in zip(grad, hat)]
    return [inv * (s - first - n * second) for s, n in zip(scaled, hat)], gains


def load_bias(ref, kind, rows):
    return jnp.concatenate([ref[kind, 0, rows], ref[kind, 1, rows]], axis=1)


def head_mask(width, slot):
    lane = iota((1, width), 1)
    return (lane >= slot * HEAD) & (lane < (slot + 1) * HEAD)


def only_head(x, slot):
    return x * jnp.where(head_mask(x.shape[1], slot), 1.0, 0.0).astype(BF)


def by_head(x, slots):
    return jnp.concatenate([only_head(x, slot) for slot in range(slots)], axis=0)


def own_columns(x, slots):
    out = x[:TOK]
    for slot in range(1, slots):
        out = jnp.where(head_mask(x.shape[1], slot), x[slot * TOK : (slot + 1) * TOK], out)
    return out


def probabilities(q_stack, keys, bias):
    e = jnp.exp(mm_t(q_stack, keys) + bias)
    return e * (1.0 / jnp.sum(e, axis=1, keepdims=True))


def tile_forward(q, keys, values, bias, slots):
    p = probabilities(by_head(q, slots), keys, bias)
    return own_columns(mm(low(p), values), slots)


def tile_both(q, keys, values, gmix, bias, bias_grad_to, slots):
    q_stack, g_stack = by_head(q, slots), by_head(gmix, slots)
    p = probabilities(q_stack, keys, bias)
    p_low = low(p)
    mixed = own_columns(mm(p_low, values), slots)
    gp = mm_t(g_stack, values)
    gs = p * (gp - jnp.sum(p * gp, axis=1, keepdims=True))
    bias_grad_to(gs)
    gs_low = low(gs)
    gq = own_columns(mm(gs_low, keys), slots)
    return mixed, gq, t_mm(gs_low, q_stack), t_mm(p_low, g_stack)


def put(ref, grain, start, value, place=lambda chunk: chunk):
    at = 0
    while at < value.shape[0]:
        chunk, row = divmod(start + at, grain)
        n = min(grain - row, value.shape[0] - at)
        ref[place(chunk), row : row + n] = value[at : at + n]
        at += n


def place_of(chunk):
    return chunk % 8 * 2 + chunk // 8


def get_chunk(sums, chunk, rows):
    mine, other, core = sums
    return jnp.where(core == chunk // 8, mine[chunk % 8, rows].astype(F32), other[chunk % 8, rows].astype(F32))


def get(sums, grain, base, start, count):
    parts, at = [], 0
    while at < count:
        chunk, row = divmod(start + at, grain)
        n = min(grain - row, count - at)
        parts.append(get_chunk(sums, chunk, slice(base + row, base + row + n)))
        at += n
    return parts[0] if len(parts) == 1 else jnp.concatenate(parts, axis=0)


def gain_rows(pieces):
    line = pieces[0] if len(pieces) == 1 else jnp.concatenate(pieces, axis=1)
    width = line.shape[1]
    if width % 128:
        line = jnp.concatenate([line, jnp.zeros((1, 128 - width % 128), F32)], axis=1)
    rows = [line[:, 128 * i : 128 * i + 128] for i in range(line.shape[1] // 128)]
    rows.append(jnp.zeros((16 - len(rows), 128), F32))
    return low(jnp.concatenate(rows, axis=0))


def diagonal_select(first):
    lane = iota((1, 256), 1)
    wq = first + lax.shift_right_logical(lane, 7)
    lane = lane & 127
    wk = div_const(lane, 6)
    hk = lane - wk * 6
    diagonal = wq - wk + 11
    low_half = jnp.where((lane < HALF) & (hk < 3), hk * DIAG + diagonal, -1)
    high_half = jnp.where((lane < HALF) & (hk >= 3), (hk - 3) * DIAG + diagonal + 128, -1)
    target = jnp.maximum(low_half, high_half)
    return jnp.where(iota((256, 256), 0) == target, 1.0, 0.0).astype(BF)


HALF_RUN = 3 * DIAG


def table_groups():
    return [(g, (g // 12) * 16 + ((g // 6) % 2) * 8 + g % 6) for g in range(24)]


def table_slice(table, start):
    n = min(128, POS - start)
    part = table[:, start : start + n]
    if n < 128:
        part = jnp.concatenate([part, jnp.zeros((part.shape[0], 128 - n), F32)], axis=1)
    return part


def expand_tables(at_end, kinds, u_ref):
    lane, sub = iota((8, 128), 1), iota((8, 128), 0)
    column = div_const(lane, 6)
    crossing = (sub >= 3) != (lane - column * 6 >= 3)
    outside = jnp.where(lane >= HALF, NEG, 0.0)
    lev_term = jnp.where(at_end[0], NEG, 0.0)
    lat_term = jnp.where(crossing, jnp.where(at_end[1], NEG, 0.0), 0.0)
    u_ref[...] = jnp.zeros(u_ref.shape, F32)
    base = 0
    for table, _, _ in kinds:
        heads = table.shape[0]
        for g, row in table_groups():
            for half in range(2):
                u_ref[half, pl.ds(base + row, heads, stride=32)] = table_slice(table, g * RUN + half * HALF_RUN)
        base += heads * 32
    u = jnp.concatenate([u_ref[0, :base], u_ref[1, :base]], axis=1)
    hi = low(u)
    mid = low(u - hi.astype(F32))
    for first in range(0, 12, 2):
        sel = diagonal_select(first)
        x = mm(hi, sel) + mm(mid, sel)
        base = 0
        for table, may_end, out_ref in kinds:
            same = outside + lat_term if may_end else outside
            terms = same, same + lev_term
            for n in range(table.shape[0]):
                for zq in range(2):
                    for zk in range(2):
                        at = base + zq * 16 + zk * 8
                        for k in range(2):
                            to = n * TOK + zq * HALF + (first + k) * 6
                            part = x[at : at + 8, 128 * k : 128 * k + 128]
                            out_ref[zk, to : to + 6] = (part + terms[zq != zk])[:6]
                base += 32


def fold_tables(types, heads, grad_ref, y_ref, acc_ref, out_to):
    y_ref[...] = jnp.zeros(y_ref.shape, F32)
    for t in range(types):
        acc = None
        for first in range(0, 12, 2):
            sel = diagonal_select(first)
            for n in range(heads):
                for zq in range(2):
                    for zk in range(2):
                        at = n * 32 + zq * 16 + zk * 8
                        for k in range(2):
                            to = n * TOK + zq * HALF + (first + k) * 6
                            y_ref[at : at + 6, 128 * k : 128 * k + 128] = grad_ref[t, zk, to : to + 6]
            y = y_ref[...]
            hi = low(y)
            part = mm_t(hi, sel) + mm_t(low(y - hi.astype(F32)), sel)
            acc = part if acc is None else acc + part
        for half in range(2):
            acc_ref[half, : heads * 32] = acc[:, 128 * half : 128 * half + 128]
        for g, row in table_groups():
            for half in range(2):
                out_to(t, g * RUN + half * HALF_RUN, acc_ref[half, pl.ds(row, heads, stride=32)][:, :HALF_RUN])


def bias_kernel(fine_ref, next_ref, coarse_ref, fine_out, coarse_out, u_ref):
    at_end = [lax.axis_index(name) == lax.axis_size(name) - 1 for name in ("rep", "lat")]
    own, later, coarse = fine_ref[...], next_ref[...], coarse_ref[...]
    kinds = [
        (own[:, 0, :], False, fine_out.at[0]),
        (own[:, 1, :], True, fine_out.at[1]),
        (later[:, 0, :], False, fine_out.at[2]),
        (coarse[:, 0, :], True, coarse_out.at[0]),
    ]
    expand_tables(at_end, kinds, u_ref)


FIELD_PAD, COT_PAD = 176, 24
MESSAGE = FIELD_PAD + FIELD_PAD // 2 + 3 * COT_PAD


def pack_kernel(field_ref, cot_ref, *outs):
    r = iota((FIELD_PAD, 1), 0)
    row = div_const(r, 18)
    rc = iota((COT_PAD, 1), 0)
    crow = div_const(rc, 6)
    hots, cot_hots = [], []
    for t in range(2):
        for u in range(2):
            target = (row + (0 if t else 3)) * 24 + r - row * 18 + (0 if u else 6)
            hots.append(one_hot(jnp.where(r < 162, target, -1), 288))
    hot = jnp.concatenate(hots, axis=0)
    for s in range(2):
        for t in range(2):
            for u in range(2):
                target = (crow + (0 if t else 3)) * 12 + rc - crow * 6 + (0 if u else 6)
                cot_hots.append(one_hot(jnp.where(rc < 18, target * 2 + 1 - s, -1), TOK))
    cot = mm(jnp.concatenate(cot_hots, axis=0), low(cot_ref[...].astype(F32).reshape(TOK, 384)))
    half = FIELD_PAD // 2
    for s in range(2):
        rows = mm(hot, low(field_ref[1 - s].astype(F32).reshape(288, 192)))
        for n in range(4):
            out = outs[4 * s + n]
            part = rows[n * FIELD_PAD : (n + 1) * FIELD_PAD]
            out[:FIELD_PAD] = low(part[:, :128])
            rest = [low(jnp.concatenate([part[:half, 128:], part[half:, 128:]], axis=1))]
            first = (4 * s + n) * COT_PAD
            rest += [low(cot[first : first + COT_PAD, 128 * c : 128 * c + 128]) for c in range(3)]
            out[FIELD_PAD:] = jnp.concatenate([x.astype(F32) for x in rest], axis=0).astype(BF)


def field_of(ref):
    half = FIELD_PAD // 2
    rest = ref[FIELD_PAD : FIELD_PAD + half].astype(F32)
    rest = jnp.concatenate([rest[:, :64], rest[:, 64:]], axis=0)
    return low(jnp.concatenate([ref[:FIELD_PAD].astype(F32), rest], axis=1))


def cot_of(ref):
    rows = ref[FIELD_PAD:].astype(F32)[FIELD_PAD // 2 :]
    return low(jnp.concatenate([rows[COT_PAD * c : COT_PAD * c + COT_PAD] for c in range(3)], axis=1))


def fine_weights(qkv_ref):
    w = qkv_ref[...]
    return w[:, :192], w[:, 192:384], w[:, 384:]


FINE_TILES = ((0, 128, 4), (128, 64, 2))


def tile_rows(start, slots):
    return slice(start // HEAD * TOK, (start // HEAD + slots) * TOK)


def store_keys(ref, x):
    gap = jnp.zeros((128 - HALF, x.shape[1]), F32)
    for n in range(ref.shape[0]):
        part = x[n * TOK : (n + 1) * TOK]
        for z in range(2):
            ref[n, 128 * z : 128 * z + 128] = low(jnp.concatenate([part[HALF * z : HALF * z + HALF], gap], axis=0))


def main_kernel(
    b000, b001, b010, b011, b100, b101, b110, b111,
    bias_ref, cbias_ref,
    fgain_ref, fqkv_ref, fproj_ref, mgain_ref, mw_ref, cgain_ref, cqkv_ref, cproj_ref,
    x_out, gfo_out, latp_out, lonp_out, cin_out, gy_out, xc_out, mnorm_out, gci_out, mix_ref, g_ref, gb_ref, gains_out,
    x_ref, fo_ref, fq_ref, fk_ref, fv_ref, fm_ref,
    q_ref, k_ref, v_ref, gm_ref,
):
    bufs = ((b000, b001), (b010, b011)), ((b100, b101), (b110, b111))
    _, hh, ww = window_index(HALF)
    seen = set()
    for t in range(2):
        for u in range(2):
            hots = []
            for wr in (t, t + 1):
                for wc in (u, u + 1):
                    lat = 6 * wr + hh - 9 * t
                    lon = 12 * wc + ww - 18 * u
                    good = (lat >= 0) & (lat < 9) & (lon >= 0) & (lon < 18)
                    hots.append(one_hot(jnp.where(good, lat * 18 + lon, -1), FIELD_PAD))
            hot = jnp.concatenate(hots, axis=0)
            for z in range(2):
                part = mm(hot, field_of(bufs[z][t][u]))
                for n in range(4):
                    place = 3 * (t + n // 2) + u + n % 2, slice(z * HALF, (z + 1) * HALF)
                    value = part[n * HALF : (n + 1) * HALF]
                    if (place[0], z) in seen:
                        value = value + x_ref[place]
                    seen.add((place[0], z))
                    x_ref[place] = value
    for wr in range(2):
        for wc in range(2):
            x_out[2 * wr + wc] = low(x_ref[3 * wr + wc])
    wq, wk, wv = fine_weights(fqkv_ref)
    x = x_ref[...].reshape(9 * TOK, 192)
    (hat,), _ = norm([x])
    xn = low(hat * fgain_ref[...].reshape(1, 192))
    fq_ref[...] = low(mm(xn, wq) * HEAD**-0.5).reshape(9, TOK, 192)
    store_keys(fk_ref, mm(xn, wk))
    store_keys(fv_ref, mm(xn, wv))

    def fine_window(w, table_ref, wr):
        for start, width, slots in FINE_TILES:
            lanes = slice(start, start + width)

            bias = load_bias(table_ref, wr, tile_rows(start, slots))
            fm_ref[w, :, lanes] = low(
                tile_forward(fq_ref[w, :, lanes], fk_ref[w, :, lanes], fv_ref[w, :, lanes], bias, slots)
            )

    @pl.loop(0, 9)
    def _(w):
        fine_window(w, bias_ref, div_const(w, 3))

    out = low(mm(fm_ref[...].reshape(9 * TOK, 192), fproj_ref[...])).astype(F32)
    fo_ref[...] = low(x_ref[...].reshape(9 * TOK, 192) + out)

    z, i, j = window_index(TOK)
    hots = []
    for p in range(4):
        lat = 3 + 2 * i + p // 2
        lon = 6 + 2 * j + p % 2
        wr, wc = div_const(lat, 6), div_const(lon, 12)
        target = (3 * wr + wc) * TOK + z * HALF + (lon - 12 * wc) * 6 + lat - 6 * wr
        hots.append(one_hot(target, 9 * TOK))
    merged = mm(jnp.concatenate(hots, axis=0), fo_ref[...])
    merged = [merged[p * TOK : (p + 1) * TOK] for p in range(4)]
    mhat, minv = norm(merged)
    mgain = mgain_ref[...].reshape(1, 768)
    mgain = [mgain[:, 192 * p : 192 * p + 192] for p in range(4)]
    mnorm = [low(h * g) for h, g in zip(mhat, mgain)]
    mweight = [mw_ref[192 * p : 192 * p + 192] for p in range(4)]
    cin = low(sum(mm(n, w) for n, w in zip(mnorm, mweight))).astype(F32)
    (chat,), cinv = norm([cin])
    cgain = cgain_ref[...].reshape(1, 384)
    xc = low(chat * cgain)
    _, ci, cj = window_index(HALF)
    cot_rows = [None, None]
    for t in range(2):
        for u in range(2):
            lat, lon = ci - 3 * t, cj - 6 * u
            good = (lat >= 0) & (lat < 3) & (lon >= 0) & (lon < 6)
            hot = one_hot(jnp.where(good, lat * 6 + lon, -1), COT_PAD)
            for s in range(2):
                part = mm(hot, cot_of(bufs[s][t][u]))
                cot_rows[s] = part if cot_rows[s] is None else cot_rows[s] + part
    cot = jnp.concatenate(cot_rows, axis=0)
    gy = low(cot)
    gmix = low(mm_t(gy, cproj_ref[...]))
    for tile in range(3):
        lanes = slice(128 * tile, 128 * tile + 128)
        q_ref[tile] = low(mm(xc, cqkv_ref[:, lanes]) * HEAD**-0.5)
        k_ref[tile] = pad_keys(mm(xc, cqkv_ref[:, 384 + 128 * tile : 512 + 128 * tile]))
        v_ref[tile] = pad_keys(mm(xc, cqkv_ref[:, 768 + 128 * tile : 896 + 128 * tile]))
        gm_ref[tile] = gmix[:, lanes]

    def coarse_tile(tile, carry):
        rows = pl.ds(pl.multiple_of(tile * 4 * TOK, 64), 4 * TOK)

        def bias_grad_to(gs):
            gb_ref[0, 0, rows] = gs[:, :128]
            gb_ref[0, 1, rows] = gs[:, 128:]

        mixed, gq, gk, gv = tile_both(
            q_ref[tile], k_ref[tile], v_ref[tile], gm_ref[tile], load_bias(cbias_ref, 0, rows), bias_grad_to, 4
        )
        mix_ref[tile] = low(mixed)
        g_ref[0, tile] = low(gq * HEAD**-0.5)
        g_ref[1, tile] = low(unpad_keys(gk))
        g_ref[2, tile] = low(unpad_keys(gv))
        return carry

    lax.fori_loop(0, 3, coarse_tile, 0)
    grolled = None
    for tile in range(3):
        for m in range(3):
            wcols = slice(384 * m + 128 * tile, 384 * m + 128 * tile + 128)
            part = mm_t(g_ref[m, tile], cqkv_ref[:, wcols])
            grolled = part if grolled is None else grolled + part
    cin_out[...] = low(cin)
    gy_out[...] = gy
    xc_out[...] = xc
    (gci,), (cgain_grad,) = norm_back([low(grolled).astype(F32)], [cgain], [chat], cinv)
    gci = low(cot + gci)
    gml = []
    gci_out[...] = gci
    for p in range(4):
        mnorm_out[p] = mnorm[p]
        gml.append(low(mm_t(gci, mweight[p])).astype(F32))
    gmerged, mgain_grad = norm_back(gml, mgain, mhat, minv)
    gains_out[...] = gain_rows(list(mgain_grad) + [cgain_grad])
    r48 = iota((48, 1), 0)
    zi = div_const(r48, 24)
    rest = r48 - 24 * zi
    lat_hot = one_hot(zi * HALF + lax.shift_right_logical(rest, 1) * 6 + 4 + (rest & 1), TOK)
    r40 = iota((40, 1), 0)
    zi = jnp.where(r40 >= 18, 1, 0)
    lon_hot = one_hot(jnp.where(r40 < 36, zi * HALF + 54 + r40 - 18 * zi, -1), TOK)
    hot = jnp.concatenate([lat_hot, lon_hot], axis=0)
    for p in range(4):
        g = low(gmerged[p])
        gfo_out[p] = g
        part = low(mm(hot, g))
        latp_out[48 * p : 48 * p + 48] = part[:48]
        lonp_out[40 * p : 40 * p + 40] = part[48:]


def side_kernel(
    cin_ref, gy_ref, xc_ref, mnorm_ref, gci_ref, mix_ref, g_ref, gb_ref, cproj_ref,
    cout_out, pack_out, ctab_out, y_ref, acc_ref,
):
    gy, xc, gci = gy_ref[...], xc_ref[...], gci_ref[...]
    out = None
    for tile in range(3):
        lanes = slice(128 * tile, 128 * tile + 128)
        part = mm(mix_ref[tile], cproj_ref[lanes])
        out = part if out is None else out + part
        dproj = low(t_mm(mix_ref[tile], gy))
        for c in range(3):
            start = 5760 + 384 * c + 128 * tile
            put(pack_out, COARSE, start, dproj[:, 128 * c : 128 * c + 128])
    cout_out[...] = low(cin_ref[...].astype(F32) + low(out).astype(F32))
    for m in range(3):
        dqkv = low(t_mm(xc, jnp.concatenate([g_ref[m, tile] for tile in range(3)], axis=1)))
        for tile in range(3):
            start = 2304 + 384 * (3 * m + tile)
            put(pack_out, COARSE, start, dqkv[:, 128 * tile : 128 * tile + 128])
    for p in range(4):
        dmw = low(t_mm(mnorm_ref[p], gci))
        for c in range(3):
            start = 768 * c + 192 * p
            put(pack_out, COARSE, start, dmw[:, 128 * c : 128 * c + 128])
    ctab_out[...] = jnp.zeros(ctab_out.shape, F32)

    def ctab(t, start, rows):
        ctab_out[:12, start : start + HALF_RUN] = rows

    fold_tables(1, 12, gb_ref, y_ref, acc_ref, ctab)


QUARTERS = ((0, 0), (0, 1), (1, 1), (1, 0))
FINE_PAD = (176, 64, 32, 64)
PIECE = tuple(n + 48 for n in FINE_PAD)
BASE = tuple(sum(PIECE[:n]) for n in range(5))


def fine_rows_of(s, t, u):
    r = iota((FINE_PAD[QUARTERS.index((t, u))], 1), 0)
    width, height = 6 if u else 18, 3 if t else 9
    row = div_const(r, width)
    lat, lon = row + 9 * t, r - row * width + 18 * u
    wr, wc = div_const(lat, 6), div_const(lon, 12)
    target = (2 * wr + wc) * TOK + s * HALF + (lon - 12 * wc) * 6 + lat - 6 * wr
    return jnp.where(row < height, target, -1)


def coarse_rows_of(s, t, u):
    r = iota((24, 1), 0)
    row = div_const(r, 6)
    return jnp.where(row < 3, s * HALF + (r - row * 6 + 6 * u) * 6 + row + 3 * t, -1)


def back_kernel(
    x_in, gfo_ref, latp_ref, lonp_ref, corner_ref, bias_ref, fgain_ref, fqkv_ref, fproj_ref, ctab_ref, gains_ref, cout_ref,
    level0_out, level1_out, pack_out,
    src_ref, fq_ref, fk_ref, fv_ref, fm_ref, gm_ref, g_ref, gb_ref, y_ref, acc_ref, tab_ref,
):
    src_ref[:576] = gfo_ref[...]
    src_ref[576:768] = latp_ref[...]
    src_ref[768:928] = lonp_ref[...]
    src_ref[928:] = corner_ref[...]
    z, h, w = window_index(TOK)
    hots = []
    for wr in range(2):
        for wc in range(2):
            lat, lon = 6 * wr + h, 12 * wc + w
            behind, before = lat < 3, lon < 6
            lat = jnp.where(behind, lat + 9, lat - 3)
            lon = jnp.where(before, lon + 18, lon - 6)
            p = 2 * (lat & 1) + (lon & 1)
            i, j = lax.shift_right_logical(lat, 1), lax.shift_right_logical(lon, 1)
            own = p * TOK + z * HALF + j * 6 + i
            from_lat = 576 + p * 48 + z * 24 + j * 2 + i - 4
            from_lon = 768 + p * 40 + z * 18 + (j - 9) * 6 + i
            target = jnp.where(before, from_lon + jnp.where(behind, 160, 0), jnp.where(behind, from_lat, own))
            hots.append(one_hot(target, 1088))
    gy = low(mm(jnp.concatenate(hots, axis=0), src_ref[...]))
    gy32 = gy.astype(F32)
    gb_ref[...] = jnp.zeros(gb_ref.shape, F32)
    weights = fine_weights(fqkv_ref)
    gain = fgain_ref[...].reshape(1, 192)
    x = x_in[...].reshape(4 * TOK, 192).astype(F32)
    (hat,), inv = norm([x])
    xn = low(hat * gain)
    fq_ref[...] = low(mm(xn, weights[0]) * HEAD**-0.5).reshape(4, TOK, 192)
    store_keys(fk_ref, mm(xn, weights[1]))
    store_keys(fv_ref, mm(xn, weights[2]))
    gm_ref[...] = low(mm_t(gy, fproj_ref[...])).reshape(4, TOK, 192)

    @pl.loop(0, 4)
    def _(n):
        wr = lax.shift_right_logical(n, 1)
        for start, width, slots in FINE_TILES:
            lanes = slice(start, start + width)

            rows = tile_rows(start, slots)

            def bias_grad_to(gs):
                gb_ref[wr, 0, rows] += gs[:, :128]
                gb_ref[wr, 1, rows] += gs[:, 128:]

            mixed, gq, gk, gv = tile_both(
                fq_ref[n, :, lanes], fk_ref[n, :, lanes], fv_ref[n, :, lanes], gm_ref[n, :, lanes],
                load_bias(bias_ref, wr, rows), bias_grad_to, slots,
            )
            fm_ref[n, :, lanes] = low(mixed)
            g_ref[0, n, :, lanes] = low(gq * HEAD**-0.5)
            g_ref[1, n, :, lanes] = low(unpad_keys(gk))
            g_ref[2, n, :, lanes] = low(unpad_keys(gv))

    dproj = t_mm(fm_ref[...].reshape(4 * TOK, 192), gy)
    grads = [g_ref[m].reshape(4 * TOK, 192) for m in range(3)]
    dqkv = [t_mm(xn, g) for g in grads]
    grolled = sum(mm_t(g, w) for g, w in zip(grads, weights))
    (gx,), (ggain,) = norm_back([low(grolled).astype(F32)], [gain], [hat], inv)
    fg = low(gy32 + gx)
    cout = cout_ref[...]
    for s, out in enumerate((level0_out, level1_out)):
        hots, coarse_hots = [], []
        for t, u in QUARTERS:
            hots.append(one_hot(fine_rows_of(s, t, u), 4 * TOK))
            coarse_hots.append(one_hot(coarse_rows_of(s, t, u), TOK))
        fine = low(mm(jnp.concatenate(hots, axis=0), fg))
        coarse = low(mm(jnp.concatenate(coarse_hots, axis=0), cout))
        at = 0
        for n, rows in enumerate(FINE_PAD):
            to = BASE[n]
            out[to : to + rows] = fine[at : at + rows]
            out[to + rows : to + rows + 24] = coarse[24 * n : 24 * n + 24, :192]
            out[to + rows + 24 : to + rows + 48] = coarse[24 * n : 24 * n + 24, 192:]
            at += rows
    first = low(jnp.concatenate([dqkv[0], dqkv[1]], axis=1))
    second = low(jnp.concatenate([dqkv[2], dproj], axis=1))
    for c in range(3):
        put(pack_out, FINE, 192 * c, first[:, 128 * c : 128 * c + 128], place_of)
        put(pack_out, FINE, 576 + 192 * c, second[:, 128 * c : 128 * c + 128], place_of)
    put(pack_out, FINE, 1152, gain_rows([ggain]), place_of)
    put(pack_out, FINE, 1168, gains_ref[...], place_of)
    put(pack_out, FINE, 1184, jnp.zeros((96, 128), BF), place_of)
    tab_ref[...] = jnp.zeros(tab_ref.shape, F32)
    tab_ref[16:32] = ctab_ref[...]

    def ftab(t, start, rows):
        tab_ref[8 * t : 8 * t + 6, start : start + HALF_RUN] = rows

    fold_tables(2, 6, gb_ref, y_ref, acc_ref, ftab)
    for c in range(13):
        for half in range(2):
            lanes = slice(256 * c + 128 * half, 256 * c + 128 * half + 128)
            pack_out[place_of(c), FINE + 32 * half : FINE + 32 * half + 32] = low(tab_ref[:, lanes])
    for c in range(13, 16):
        pack_out[place_of(c), FINE:] = jnp.zeros((TAB, 128), BF)


def place_kernel(level0_ref, level1_ref, lat_ref, lon_ref, field_out, coarse_out, src_ref):
    def chosen(later_row, later_col, values):
        value = dict(zip(QUARTERS, values))
        near = jnp.where(later_row, value[1, 0], value[0, 0])
        return jnp.where(later_col, jnp.where(later_row, value[1, 1], value[0, 1]), near)

    base = BASE[:4]
    r = iota((288, 1), 0)
    lat = div_const(r, 24)
    col = r - lat * 24
    later_row, later_col = lat < 3, col < 6
    row = jnp.where(later_row, lat, lat - 3)
    inside = jnp.where(later_col, row * 6 + col, row * 18 + col - 6)
    hots = [one_hot(chosen(later_row, later_col, base) + inside, sum(PIECE))]
    r = iota((HALF, 1), 0)
    lat = div_const(r, 12)
    col = r - lat * 12
    later_row, later_col = lat < 3, col < 6
    inside = jnp.where(later_row, lat, lat - 3) * 6 + jnp.where(later_col, col, col - 6)
    inside = inside + chosen(later_row, later_col, [b + n for b, n in zip(base, FINE_PAD)])
    hots += [one_hot(inside, sum(PIECE)), one_hot(inside + 24, sum(PIECE))]
    hot = jnp.concatenate(hots, axis=0)
    placed = []
    for s in range(2):
        src_ref[: BASE[1]] = (level0_ref, level1_ref)[s][: BASE[1]]
        src_ref[BASE[1] : BASE[3]] = lon_ref[s]
        src_ref[BASE[3] :] = lat_ref[s, PIECE[2] :]
        out = low(mm(hot, src_ref[...]))
        for h in range(12):
            field_out[1 - s, h] = out[24 * h : 24 * h + 24]
        coarse = jnp.concatenate([out[288:360], out[360:]], axis=1).astype(F32)
        placed.append(coarse)
    for h in range(6):
        rows = slice(12 * h, 12 * h + 12)
        coarse_out[h] = low(jnp.stack([placed[1][rows], placed[0][rows]], axis=1))


def unpack_kernel(fine_scale, coarse_scale, fine_table_scale, coarse_table_scale, mine_ref, other_ref, *outs):
    sums = mine_ref, other_ref, lax.axis_index("lon") % 2
    fgain_out, qkv_out, proj_out, ftab_out, mgain_out, mw_out, cgain_out, cqkv_out, cproj_out, ctab_out = outs
    def coarse_get(start, count):
        return get(sums, COARSE, 0, start, count) * coarse_scale

    def fine_get(start, count, scale):
        return get(sums, FINE, COARSE, start, count) * scale

    for c in range(3):
        lanes = slice(128 * c, 128 * c + 128)
        mw_out[:, lanes] = coarse_get(768 * c, 768)
        cproj_out[:, lanes] = coarse_get(5760 + 384 * c, 384)
        qkv_out[:, lanes] = fine_get(192 * c, 192, fine_scale)
    for c in range(9):
        cqkv_out[:, 128 * c : 128 * c + 128] = coarse_get(2304 + 384 * c, 384)
    second = [fine_get(576 + 192 * c, 192, fine_scale) for c in range(3)]
    qkv_out[:, 384:512] = second[0]
    qkv_out[:, 512:] = second[1][:, :64]
    proj_out[...] = jnp.concatenate([second[1][:, 64:], second[2]], axis=1)
    gains = fine_get(1168, 16, coarse_scale)
    for c in range(6):
        mgain_out[pl.ds(128 * c, 128)] = gains[c]
    for c in range(3):
        cgain_out[pl.ds(128 * c, 128)] = gains[6 + c]
    gains = fine_get(1152, 16, fine_scale)
    fgain_out[...] = jnp.concatenate([gains[:1], gains[1:2, :64]], axis=1).reshape(192)
    for c in range(13):
        for half in range(2):
            start = 256 * c + 128 * half
            n = min(128, POS - start)
            block = get_chunk(sums, c, slice(GRAIN + 32 * half, GRAIN + 32 * half + 32))[:, :n]
            both = jnp.stack([block[:6], block[8:14]], axis=1)
            ftab_out[:, :, start : start + n] = both * fine_table_scale
            ctab_out[:, 0, start : start + n] = block[16:28] * coarse_table_scale


def call(kernel, out_shapes, scratch=(), smem=0, flops=0, moved=0, vmem=VMEM_LIMIT):
    def run(*args):
        specs = [pl.BlockSpec(memory_space=pltpu.SMEM)] * smem
        specs += [pl.BlockSpec(memory_space=pltpu.VMEM)] * (len(args) - smem)
        return pl.pallas_call(
            kernel,
            out_shape=[jax.ShapeDtypeStruct(s, d) for s, d in out_shapes],
            in_specs=specs,
            out_specs=[pl.BlockSpec(memory_space=pltpu.VMEM)] * len(out_shapes),
            scratch_shapes=[pltpu.VMEM(s, d) for s, d in scratch],
            compiler_params=pltpu.CompilerParams(vmem_limit_bytes=vmem),
            cost_estimate=pl.CostEstimate(flops=flops, bytes_accessed=moved, transcendentals=0),
        )(*args)

    return run


def shifted(x, offset, sign):
    names = [n for n, o in zip(("lon", "lat", "rep"), offset[::-1]) if o]
    sizes = [lax.axis_size(n) for n in names]
    pairs = []
    for place in np.ndindex(*sizes):
        target = [(p - sign) % s for p, s in zip(place, sizes)]
        pairs.append((int(np.ravel_multi_index(place, sizes)), int(np.ravel_multi_index(target, sizes))))
    return lax.ppermute(x, tuple(names), pairs)


CORNERS = [(s, t, u) for s in range(2) for t in range(2) for u in range(2)]


def exchange(x, axes):
    return lax.all_to_all(lax.optimization_barrier(x), axes, 0, 0, tiled=True)


def summed(x):
    return jnp.sum(x.astype(F32), axis=0, keepdims=True).astype(BF)


def spread(x, count):
    return jnp.broadcast_to(x, (count,) + x.shape[1:])


def sibling(x):
    return lax.ppermute(x, "lon", [(i, i ^ 1) for i in range(lax.axis_size("lon"))])


def exchange_columns(x):
    size = lax.axis_size("lon")
    groups = [list(range(core, size, 2)) for core in range(2)]
    return lax.all_to_all(lax.optimization_barrier(x), "lon", 0, 0, axis_index_groups=groups, tiled=True)


def reduce_coarse(coarse):
    core = lax.axis_index("lon") % 2
    keep, send = (lax.dynamic_slice_in_dim(coarse, 8 * c, 8) for c in (core, 1 - core))
    both = (keep.astype(F32) + sibling(send).astype(F32)).astype(BF)
    return exchange_columns(both)


def reduce_everywhere(got, pack, level0, level1):
    rest = lax.axis_size("lat") * lax.axis_size("rep")
    got, pack = lax.optimization_barrier((got, pack))
    pack, level1 = lax.optimization_barrier((exchange(pack, "lon"), shifted(level1, (1, 0, 0), -1)))
    got, pack = summed(got), summed(pack)
    part = jnp.concatenate([got, pack[:, :FINE]], axis=1).reshape(rest, -1, 128)
    later = shifted(jnp.stack([level0[BASE[2] :], level1[BASE[2] :]]), (0, 1, 0), -1)
    part, later = lax.optimization_barrier((exchange(part, ("lat", "rep")), later))
    part = spread(summed(part), rest)
    corner = later[:, : PIECE[2]]
    column = [jnp.concatenate([x[BASE[1] : BASE[2]], c]) for x, c in zip((level0, level1), corner)]
    column = shifted(jnp.stack(column), (0, 0, 1), -1)
    part, column = lax.optimization_barrier((exchange(part, ("lat", "rep")), column))
    mine = jnp.concatenate([part.reshape(1, GRAIN, 128), pack[:, FINE:]], axis=1)
    mine = exchange_columns(spread(mine, lax.axis_size("lon") // 2))
    return (mine, sibling(mine)), (level0, level1, later, column)


def body(
    fine_field, fine_gain, fine_qkv, fine_proj, fine_table, merge_gain, merge_weight,
    coarse_gain, coarse_qkv, coarse_proj, coarse_table, cotangent,
):
    rep, lat, lon = (lax.axis_size(n) for n in ("rep", "lat", "lon"))
    packs = call(pack_kernel, [((MESSAGE, 128), BF)] * 8)(fine_field, cotangent.transpose(1, 2, 0, 3))
    bufs = [shifted(b, place, 1) if any(place) else b for b, place in zip(packs, CORNERS)]
    table = fine_table[0].transpose(1, 0, 2)
    bias, cbias = call(
        bias_kernel,
        [((3, 2, FINE_ROWS, 128), F32), ((1, 2, COARSE_ROWS, 128), F32)],
        [((2, 34 * 32, 128), F32)],
        flops=1 << 32,
    )(table, shifted(fine_table, (0, 1, 0), 1)[0].transpose(1, 0, 2), coarse_table[0].transpose(1, 0, 2))
    x, gfo, latp, lonp, *coarse, cgains = call(
        main_kernel,
        [
            ((4, TOK, 192), BF), ((4, TOK, 192), BF), ((192, 192), BF), ((160, 192), BF),
            ((TOK, 384), BF), ((TOK, 384), BF), ((TOK, 384), BF), ((4, TOK, 192), BF), ((TOK, 384), BF),
            ((3, TOK, 128), BF), ((3, 3, TOK, 128), BF), ((1, 2, COARSE_ROWS, 128), F32), ((16, 128), BF),
        ],
        [
            ((9, TOK, 192), F32), ((9 * TOK, 192), BF),
            ((9, TOK, 192), BF), ((9, LANES, 192), BF), ((9, LANES, 192), BF), ((9, TOK, 192), BF),
            ((3, TOK, 128), BF), ((3, LANES, 128), BF), ((3, LANES, 128), BF), ((3, TOK, 128), BF),
        ],
        flops=1 << 34,
    )(
        *bufs, bias, cbias, fine_gain, fine_qkv, fine_proj, merge_gain,
        merge_weight, coarse_gain, coarse_qkv, coarse_proj,
    )
    lat_recv = shifted(latp, (0, 1, 0), -1)
    lon_recv = shifted(lonp, (0, 0, 1), -1)
    corner_recv = shifted(lonp, (0, 1, 1), -1)
    cout, cpack, ctab = call(
        side_kernel,
        [((TOK, 384), BF), ((16, COARSE, 128), BF), ((16, WIDE), F32)],
        [((384, 256), F32), ((2, 512, 128), F32)],
        flops=1 << 32,
    )(*coarse, coarse_proj)
    got = reduce_coarse(cpack)
    level0, level1, pack = call(
        back_kernel,
        [((BASE[4], 192), BF), ((BASE[4], 192), BF), ((16, FINE + TAB, 128), BF)],
        [
            ((1088, 192), BF), ((4, TOK, 192), BF), ((4, LANES, 192), BF), ((4, LANES, 192), BF),
            ((4, TOK, 192), BF), ((4, TOK, 192), BF), ((3, 4, TOK, 192), BF),
            ((2, 2, FINE_ROWS, 128), F32), ((192, 256), F32), ((2, 256, 128), F32), ((32, WIDE), F32),
        ],
        flops=1 << 33,
    )(x, gfo.reshape(4 * TOK, 192), lat_recv, lon_recv, corner_recv, bias, fine_gain, fine_qkv, fine_proj, ctab, cgains, cout)
    sums, back = reduce_everywhere(got, pack, level0, level1)
    field_grad, coarse_out = call(
        place_kernel, [((2, 12, 24, 192), BF), ((6, 12, 2, 384), BF)], [((sum(PIECE), 192), BF)]
    )(*back)
    levels, rows, cols = 2 * rep, 12 * lat, 24 * lon
    fine_scale = (levels * rows * cols) ** -0.5
    coarse_scale = (levels * rows * cols // 4) ** -0.5
    fine_table_scale = (cols // 12) ** -0.5
    coarse_table_scale = (cols // 24) ** -0.5
    fgain_g, fqkv_g, fproj_g, ftab_g, mgain_g, mw_g, cgain_g, cqkv_g, cproj_g, ctab_g = call(
        lambda *refs: unpack_kernel(fine_scale, coarse_scale, fine_table_scale, coarse_table_scale, *refs),
        [
            ((192,), F32), ((192, 576), F32), ((192, 192), F32), ((6, 2, POS), F32), ((768,), F32),
            ((768, 384), F32), ((384,), F32), ((384, 1152), F32), ((384, 384), F32), ((12, 1, POS), F32),
        ],
    )(*sums)
    return (
        coarse_out.transpose(2, 0, 1, 3), field_grad, fgain_g, fqkv_g, fproj_g, ftab_g.transpose(1, 0, 2)[None],
        mgain_g, mw_g, cgain_g, cqkv_g, cproj_g, ctab_g.transpose(1, 0, 2)[None],
    )


def solution(mesh):
    tokens, tables = P("rep", "lat", "lon", None), P("rep", "lat", None, None)
    return jax.shard_map(
        body,
        mesh=mesh,
        in_specs=(tokens, P(), P(), P(), tables, P(), P(), P(), P(), P(), tables, tokens),
        out_specs=(tokens, tokens, P(), P(), P(), tables, P(), P(), P(), P(), P(), tables),
        check_vma=False,
    )
```

```python
import numpy as np
import jax
import jax.numpy as jnp
from jax import lax
from jax.experimental import pallas as pl
from jax.experimental.pallas import tpu as pltpu
from jax.sharding import PartitionSpec as P

F32, BF = jnp.float32, jnp.bfloat16
EPS = 1e-05
TOK, HALF, LANES = 144, 72, 256
POS, DIAG = 3312, 23
RUN = 6 * DIAG
HEAD = 32
NEG = -1e30
COARSE, FINE, TAB = 432, 80, 64
GRAIN = COARSE + FINE
WIDE = 3456
FINE_ROWS, COARSE_ROWS = 6 * TOK + 8, 12 * TOK + 8
VMEM_LIMIT = 24 * 1024 * 1024


def dot(a, b, ca, cb):
    return lax.dot_general(a, b, (((ca,), (cb,)), ((), ())), preferred_element_type=F32)


def mm(a, b):
    return dot(a, b, 1, 0)


def mm_t(a, b):
    return dot(a, b, 1, 1)


def t_mm(a, b):
    return dot(a, b, 0, 0)


def low(x):
    return x.astype(BF)


def split3(x):
    hi = low(x)
    rest = x - hi.astype(F32)
    mid = low(rest)
    return hi, mid, low(rest - mid.astype(F32))


def iota(shape, dim):
    return lax.broadcasted_iota(jnp.int32, shape, dim)


def div_const(x, n):
    return lax.shift_right_logical(x * (65536 // n + 1), 16)


def one_hot(target, count):
    return jnp.where(iota((target.shape[0], count), 1) == target, 1.0, 0.0).astype(BF)


def window_index(rows):
    r = iota((rows, 1), 0)
    z = div_const(r, 72)
    r = r - z * 72
    w = div_const(r, 6)
    return z, r - w * 6, w


def pad_keys(x):
    gap = jnp.zeros((128 - HALF, x.shape[1]), F32)
    return low(jnp.concatenate([x[:HALF], gap, x[HALF:], gap], axis=0))


def unpad_keys(x):
    return jnp.concatenate([x[:HALF], x[128 : 128 + HALF]], axis=0)


def norm(x):
    width = sum(p.shape[1] for p in x)
    mean = sum(jnp.sum(p, axis=1, keepdims=True) for p in x) * (1.0 / width)
    shifted = [p - mean for p in x]
    var = sum(jnp.sum(p * p, axis=1, keepdims=True) for p in shifted) * (1.0 / width)
    inv = lax.rsqrt(var + EPS)
    return [p * inv for p in shifted], inv


def norm_back(grad, gain, hat, inv):
    width = sum(p.shape[1] for p in grad)
    scaled = [g * a for g, a in zip(grad, gain)]
    first = sum(jnp.sum(s, axis=1, keepdims=True) for s in scaled) * (1.0 / width)
    second = sum(jnp.sum(s * n, axis=1, keepdims=True) for s, n in zip(scaled, hat)) * (1.0 / width)
    gains = [jnp.sum(g * n, axis=0, keepdims=True) for g, n in zip(grad, hat)]
    return [inv * (s - first - n * second) for s, n in zip(scaled, hat)], gains


def load_bias(ref, kind, rows):
    return jnp.concatenate([ref[kind, 0, rows], ref[kind, 1, rows]], axis=1)


def head_mask(width, slot):
    lane = iota((1, width), 1)
    return (lane >= slot * HEAD) & (lane < (slot + 1) * HEAD)


def only_head(x, slot):
    return x * jnp.where(head_mask(x.shape[1], slot), 1.0, 0.0).astype(BF)


def by_head(x, slots):
    return jnp.concatenate([only_head(x, slot) for slot in range(slots)], axis=0)


def own_columns(x, slots):
    out = x[:TOK]
    for slot in range(1, slots):
        out = jnp.where(head_mask(x.shape[1], slot), x[slot * TOK : (slot + 1) * TOK], out)
    return out


def probabilities(q_stack, keys, bias):
    e = jnp.exp(mm_t(q_stack, keys) + bias)
    return e * (1.0 / jnp.sum(e, axis=1, keepdims=True))


def tile_forward(q, keys, values, bias, slots):
    p = probabilities(by_head(q, slots), keys, bias)
    return own_columns(mm(low(p), values), slots)


def tile_both(q, keys, values, gmix, bias, bias_grad_to, slots):
    q_stack, g_stack = by_head(q, slots), by_head(gmix, slots)
    p = probabilities(q_stack, keys, bias)
    p_low = low(p)
    mixed = own_columns(mm(p_low, values), slots)
    gp = mm_t(g_stack, values)
    gs = p * (gp - jnp.sum(p * gp, axis=1, keepdims=True))
    bias_grad_to(gs)
    gs_low = low(gs)
    gq = own_columns(mm(gs_low, keys), slots)
    return mixed, gq, t_mm(gs_low, q_stack), t_mm(p_low, g_stack)


def put(ref, grain, start, value):
    at = 0
    while at < value.shape[0]:
        chunk, row = divmod(start + at, grain)
        n = min(grain - row, value.shape[0] - at)
        ref[chunk, row : row + n] = value[at : at + n]
        at += n


def split_halves(pack_ref, keep_ref, send_ref):
    core = lax.axis_index("lon") % 2
    for own in range(2):

        @pl.when(core == own)
        def _():
            keep_ref[...] = pack_ref[8 * own : 8 * own + 8]
            send_ref[...] = pack_ref[8 - 8 * own : 16 - 8 * own]


def get_chunk(sums, chunk, rows):
    mine, other, core = sums
    return jnp.where(core == chunk // 8, mine[chunk % 8, rows].astype(F32), other[chunk % 8, rows].astype(F32))


def get(sums, grain, base, start, count):
    parts, at = [], 0
    while at < count:
        chunk, row = divmod(start + at, grain)
        n = min(grain - row, count - at)
        parts.append(get_chunk(sums, chunk, slice(base + row, base + row + n)))
        at += n
    return parts[0] if len(parts) == 1 else jnp.concatenate(parts, axis=0)


def gain_rows(pieces):
    line = pieces[0] if len(pieces) == 1 else jnp.concatenate(pieces, axis=1)
    width = line.shape[1]
    if width % 128:
        line = jnp.concatenate([line, jnp.zeros((1, 128 - width % 128), F32)], axis=1)
    rows = [line[:, 128 * i : 128 * i + 128] for i in range(line.shape[1] // 128)]
    rows.append(jnp.zeros((16 - len(rows), 128), F32))
    return low(jnp.concatenate(rows, axis=0))


def diagonal_select(first):
    lane = iota((1, 256), 1)
    wq = first + lax.shift_right_logical(lane, 7)
    lane = lane & 127
    wk = div_const(lane, 6)
    hk = lane - wk * 6
    diagonal = wq - wk + 11
    low_half = jnp.where((lane < HALF) & (hk < 3), hk * DIAG + diagonal, -1)
    high_half = jnp.where((lane < HALF) & (hk >= 3), (hk - 3) * DIAG + diagonal + 128, -1)
    target = jnp.maximum(low_half, high_half)
    return jnp.where(iota((256, 256), 0) == target, 1.0, 0.0).astype(BF)


HALF_RUN = 3 * DIAG


def table_groups():
    return [(g, (g // 12) * 16 + ((g // 6) % 2) * 8 + g % 6) for g in range(24)]


def table_slice(table, start):
    n = min(128, POS - start)
    part = table[:, start : start + n]
    if n < 128:
        part = jnp.concatenate([part, jnp.zeros((part.shape[0], 128 - n), F32)], axis=1)
    return part


def expand_tables(at_end, kinds, u_ref):
    lane, sub = iota((8, 128), 1), iota((8, 128), 0)
    column = div_const(lane, 6)
    crossing = (sub >= 3) != (lane - column * 6 >= 3)
    outside = jnp.where(lane >= HALF, NEG, 0.0)
    lev_term = jnp.where(at_end[0], NEG, 0.0)
    lat_term = jnp.where(crossing, jnp.where(at_end[1], NEG, 0.0), 0.0)
    u_ref[...] = jnp.zeros(u_ref.shape, F32)
    base = 0
    for table, _, _ in kinds:
        heads = table.shape[0]
        for g, row in table_groups():
            for half in range(2):
                u_ref[half, pl.ds(base + row, heads, stride=32)] = table_slice(table, g * RUN + half * HALF_RUN)
        base += heads * 32
    u = jnp.concatenate([u_ref[0, :base], u_ref[1, :base]], axis=1)
    hi = low(u)
    mid = low(u - hi.astype(F32))
    for first in range(0, 12, 2):
        sel = diagonal_select(first)
        x = mm(hi, sel) + mm(mid, sel)
        base = 0
        for table, may_end, out_ref in kinds:
            same = outside + lat_term if may_end else outside
            terms = same, same + lev_term
            for n in range(table.shape[0]):
                for zq in range(2):
                    for zk in range(2):
                        at = base + zq * 16 + zk * 8
                        for k in range(2):
                            to = n * TOK + zq * HALF + (first + k) * 6
                            part = x[at : at + 8, 128 * k : 128 * k + 128]
                            out_ref[zk, to : to + 6] = (part + terms[zq != zk])[:6]
                base += 32


def fold_tables(types, heads, grad_ref, y_ref, acc_ref, out_to):
    y_ref[...] = jnp.zeros(y_ref.shape, F32)
    for t in range(types):
        acc = None
        for first in range(0, 12, 2):
            sel = diagonal_select(first)
            for n in range(heads):
                for zq in range(2):
                    for zk in range(2):
                        at = n * 32 + zq * 16 + zk * 8
                        for k in range(2):
                            to = n * TOK + zq * HALF + (first + k) * 6
                            y_ref[at : at + 6, 128 * k : 128 * k + 128] = grad_ref[t, zk, to : to + 6]
            y = y_ref[...]
            hi = low(y)
            part = mm_t(hi, sel) + mm_t(low(y - hi.astype(F32)), sel)
            acc = part if acc is None else acc + part
        for half in range(2):
            acc_ref[half, : heads * 32] = acc[:, 128 * half : 128 * half + 128]
        for g, row in table_groups():
            for half in range(2):
                out_to(t, g * RUN + half * HALF_RUN, acc_ref[half, pl.ds(row, heads, stride=32)][:, :HALF_RUN])


def bias_kernel(fine_ref, next_ref, coarse_ref, fine_out, coarse_out, u_ref):
    at_end = [lax.axis_index(name) == lax.axis_size(name) - 1 for name in ("rep", "lat")]
    own, later, coarse = fine_ref[...], next_ref[...], coarse_ref[...]
    kinds = [
        (own[:, 0, :], False, fine_out.at[0]),
        (own[:, 1, :], True, fine_out.at[1]),
        (later[:, 0, :], False, fine_out.at[2]),
        (coarse[:, 0, :], True, coarse_out.at[0]),
    ]
    expand_tables(at_end, kinds, u_ref)


FIELD_PAD, COT_PAD = 176, 24
MESSAGE = FIELD_PAD + FIELD_PAD // 2 + 3 * COT_PAD


def pack_kernel(field_ref, cot_ref, *outs):
    r = iota((FIELD_PAD, 1), 0)
    row = div_const(r, 18)
    rc = iota((COT_PAD, 1), 0)
    crow = div_const(rc, 6)
    hots, cot_hots = [], []
    for t in range(2):
        for u in range(2):
            target = (row + (0 if t else 3)) * 24 + r - row * 18 + (0 if u else 6)
            hots.append(one_hot(jnp.where(r < 162, target, -1), 288))
    hot = jnp.concatenate(hots, axis=0)
    for s in range(2):
        for t in range(2):
            for u in range(2):
                target = (crow + (0 if t else 3)) * 12 + rc - crow * 6 + (0 if u else 6)
                cot_hots.append(one_hot(jnp.where(rc < 18, target * 2 + 1 - s, -1), TOK))
    cot = mm(jnp.concatenate(cot_hots, axis=0), low(cot_ref[...].astype(F32).reshape(TOK, 384)))
    half = FIELD_PAD // 2
    for s in range(2):
        rows = mm(hot, low(field_ref[1 - s].astype(F32).reshape(288, 192)))
        for n in range(4):
            out = outs[4 * s + n]
            part = rows[n * FIELD_PAD : (n + 1) * FIELD_PAD]
            out[:FIELD_PAD] = low(part[:, :128])
            rest = [low(jnp.concatenate([part[:half, 128:], part[half:, 128:]], axis=1))]
            first = (4 * s + n) * COT_PAD
            rest += [low(cot[first : first + COT_PAD, 128 * c : 128 * c + 128]) for c in range(3)]
            out[FIELD_PAD:] = jnp.concatenate([x.astype(F32) for x in rest], axis=0).astype(BF)


def field_of(ref):
    half = FIELD_PAD // 2
    rest = ref[FIELD_PAD : FIELD_PAD + half].astype(F32)
    rest = jnp.concatenate([rest[:, :64], rest[:, 64:]], axis=0)
    return low(jnp.concatenate([ref[:FIELD_PAD].astype(F32), rest], axis=1))


def cot_of(ref):
    rows = ref[FIELD_PAD:].astype(F32)[FIELD_PAD // 2 :]
    return low(jnp.concatenate([rows[COT_PAD * c : COT_PAD * c + COT_PAD] for c in range(3)], axis=1))


def fine_weights(qkv_ref):
    w = qkv_ref[...]
    return w[:, :192], w[:, 192:384], w[:, 384:]


FINE_TILES = ((0, 128, 4), (128, 64, 2))


def tile_rows(start, slots):
    return slice(start // HEAD * TOK, (start // HEAD + slots) * TOK)


def store_keys(ref, x):
    gap = jnp.zeros((128 - HALF, x.shape[1]), F32)
    for n in range(ref.shape[0]):
        part = x[n * TOK : (n + 1) * TOK]
        for z in range(2):
            ref[n, 128 * z : 128 * z + 128] = low(jnp.concatenate([part[HALF * z : HALF * z + HALF], gap], axis=0))


def main_kernel(
    b000, b001, b010, b011, b100, b101, b110, b111,
    bias_ref, cbias_ref,
    fgain_ref, fqkv_ref, fproj_ref, mgain_ref, mw_ref, cgain_ref, cqkv_ref, cproj_ref,
    x_out, gfo_out, latp_out, lonp_out, cin_out, gy_out, xc_out, mnorm_out, gci_out, mix_ref, g_ref, gb_ref, gains_out,
    x_ref, fo_ref, fq_ref, fk_ref, fv_ref, fm_ref,
    q_ref, k_ref, v_ref, gm_ref,
):
    bufs = ((b000, b001), (b010, b011)), ((b100, b101), (b110, b111))
    _, hh, ww = window_index(HALF)
    seen = set()
    for t in range(2):
        for u in range(2):
            hots = []
            for wr in (t, t + 1):
                for wc in (u, u + 1):
                    lat = 6 * wr + hh - 9 * t
                    lon = 12 * wc + ww - 18 * u
                    good = (lat >= 0) & (lat < 9) & (lon >= 0) & (lon < 18)
                    hots.append(one_hot(jnp.where(good, lat * 18 + lon, -1), FIELD_PAD))
            hot = jnp.concatenate(hots, axis=0)
            for z in range(2):
                part = mm(hot, field_of(bufs[z][t][u]))
                for n in range(4):
                    place = 3 * (t + n // 2) + u + n % 2, slice(z * HALF, (z + 1) * HALF)
                    value = part[n * HALF : (n + 1) * HALF]
                    if (place[0], z) in seen:
                        value = value + x_ref[place]
                    seen.add((place[0], z))
                    x_ref[place] = value
    for wr in range(2):
        for wc in range(2):
            x_out[2 * wr + wc] = low(x_ref[3 * wr + wc])
    wq, wk, wv = fine_weights(fqkv_ref)
    x = x_ref[...].reshape(9 * TOK, 192)
    (hat,), _ = norm([x])
    xn = low(hat * fgain_ref[...].reshape(1, 192))
    fq_ref[...] = low(mm(xn, wq) * HEAD**-0.5).reshape(9, TOK, 192)
    store_keys(fk_ref, mm(xn, wk))
    store_keys(fv_ref, mm(xn, wv))

    def fine_window(w, table_ref, wr):
        for start, width, slots in FINE_TILES:
            lanes = slice(start, start + width)

            bias = load_bias(table_ref, wr, tile_rows(start, slots))
            fm_ref[w, :, lanes] = low(
                tile_forward(fq_ref[w, :, lanes], fk_ref[w, :, lanes], fv_ref[w, :, lanes], bias, slots)
            )

    @pl.loop(0, 9, unroll=9)
    def _(w):
        fine_window(w, bias_ref, div_const(w, 3))

    out = low(mm(fm_ref[...].reshape(9 * TOK, 192), fproj_ref[...])).astype(F32)
    fo_ref[...] = low(x_ref[...].reshape(9 * TOK, 192) + out)

    z, i, j = window_index(TOK)
    hots = []
    for p in range(4):
        lat = 3 + 2 * i + p // 2
        lon = 6 + 2 * j + p % 2
        wr, wc = div_const(lat, 6), div_const(lon, 12)
        target = (3 * wr + wc) * TOK + z * HALF + (lon - 12 * wc) * 6 + lat - 6 * wr
        hots.append(one_hot(target, 9 * TOK))
    merged = mm(jnp.concatenate(hots, axis=0), fo_ref[...])
    merged = [merged[p * TOK : (p + 1) * TOK] for p in range(4)]
    mhat, minv = norm(merged)
    mgain = mgain_ref[...].reshape(1, 768)
    mgain = [mgain[:, 192 * p : 192 * p + 192] for p in range(4)]
    mnorm = [low(h * g) for h, g in zip(mhat, mgain)]
    mweight = [mw_ref[192 * p : 192 * p + 192] for p in range(4)]
    cin = low(sum(mm(n, w) for n, w in zip(mnorm, mweight))).astype(F32)
    (chat,), cinv = norm([cin])
    cgain = cgain_ref[...].reshape(1, 384)
    xc = low(chat * cgain)
    _, ci, cj = window_index(HALF)
    cot_rows = [None, None]
    for t in range(2):
        for u in range(2):
            lat, lon = ci - 3 * t, cj - 6 * u
            good = (lat >= 0) & (lat < 3) & (lon >= 0) & (lon < 6)
            hot = one_hot(jnp.where(good, lat * 6 + lon, -1), COT_PAD)
            for s in range(2):
                part = mm(hot, cot_of(bufs[s][t][u]))
                cot_rows[s] = part if cot_rows[s] is None else cot_rows[s] + part
    cot = jnp.concatenate(cot_rows, axis=0)
    gy = low(cot)
    gmix = low(mm_t(gy, cproj_ref[...]))
    for tile in range(3):
        lanes = slice(128 * tile, 128 * tile + 128)
        q_ref[tile] = low(mm(xc, cqkv_ref[:, lanes]) * HEAD**-0.5)
        k_ref[tile] = pad_keys(mm(xc, cqkv_ref[:, 384 + 128 * tile : 512 + 128 * tile]))
        v_ref[tile] = pad_keys(mm(xc, cqkv_ref[:, 768 + 128 * tile : 896 + 128 * tile]))
        gm_ref[tile] = gmix[:, lanes]

    def coarse_tile(tile, carry):
        rows = pl.ds(pl.multiple_of(tile * 4 * TOK, 64), 4 * TOK)

        def bias_grad_to(gs):
            gb_ref[0, 0, rows] = gs[:, :128]
            gb_ref[0, 1, rows] = gs[:, 128:]

        mixed, gq, gk, gv = tile_both(
            q_ref[tile], k_ref[tile], v_ref[tile], gm_ref[tile], load_bias(cbias_ref, 0, rows), bias_grad_to, 4
        )
        mix_ref[tile] = low(mixed)
        g_ref[0, tile] = low(gq * HEAD**-0.5)
        g_ref[1, tile] = low(unpad_keys(gk))
        g_ref[2, tile] = low(unpad_keys(gv))
        return carry

    lax.fori_loop(0, 3, coarse_tile, 0, unroll=True)
    grolled = None
    for tile in range(3):
        for m in range(3):
            wcols = slice(384 * m + 128 * tile, 384 * m + 128 * tile + 128)
            part = mm_t(g_ref[m, tile], cqkv_ref[:, wcols])
            grolled = part if grolled is None else grolled + part
    cin_out[...] = low(cin)
    gy_out[...] = gy
    xc_out[...] = xc
    (gci,), (cgain_grad,) = norm_back([low(grolled).astype(F32)], [cgain], [chat], cinv)
    gci = low(cot + gci)
    gml = []
    gci_out[...] = gci
    for p in range(4):
        mnorm_out[p] = mnorm[p]
        gml.append(low(mm_t(gci, mweight[p])).astype(F32))
    gmerged, mgain_grad = norm_back(gml, mgain, mhat, minv)
    gains_out[...] = gain_rows(list(mgain_grad) + [cgain_grad])
    r48 = iota((48, 1), 0)
    zi = div_const(r48, 24)
    rest = r48 - 24 * zi
    lat_hot = one_hot(zi * HALF + lax.shift_right_logical(rest, 1) * 6 + 4 + (rest & 1), TOK)
    r40 = iota((40, 1), 0)
    zi = jnp.where(r40 >= 18, 1, 0)
    lon_hot = one_hot(jnp.where(r40 < 36, zi * HALF + 54 + r40 - 18 * zi, -1), TOK)
    hot = jnp.concatenate([lat_hot, lon_hot], axis=0)
    for p in range(4):
        g = low(gmerged[p])
        gfo_out[p] = g
        part = low(mm(hot, g))
        latp_out[48 * p : 48 * p + 48] = part[:48]
        lonp_out[40 * p : 40 * p + 40] = part[48:]


def side_kernel(
    cin_ref, gy_ref, xc_ref, mnorm_ref, gci_ref, mix_ref, g_ref, gb_ref, cproj_ref,
    cout_out, keep_out, send_out, ctab_out, y_ref, acc_ref, pack_out,
):
    gy, xc, gci = gy_ref[...], xc_ref[...], gci_ref[...]
    out = None
    for tile in range(3):
        lanes = slice(128 * tile, 128 * tile + 128)
        part = mm(mix_ref[tile], cproj_ref[lanes])
        out = part if out is None else out + part
        dproj = low(t_mm(mix_ref[tile], gy))
        for c in range(3):
            start = 5760 + 384 * c + 128 * tile
            put(pack_out, COARSE, start, dproj[:, 128 * c : 128 * c + 128])
    cout_out[...] = low(cin_ref[...].astype(F32) + low(out).astype(F32))
    for m in range(3):
        dqkv = low(t_mm(xc, jnp.concatenate([g_ref[m, tile] for tile in range(3)], axis=1)))
        for tile in range(3):
            start = 2304 + 384 * (3 * m + tile)
            put(pack_out, COARSE, start, dqkv[:, 128 * tile : 128 * tile + 128])
    for p in range(4):
        dmw = low(t_mm(mnorm_ref[p], gci))
        for c in range(3):
            start = 768 * c + 192 * p
            put(pack_out, COARSE, start, dmw[:, 128 * c : 128 * c + 128])
    split_halves(pack_out, keep_out, send_out)
    ctab_out[...] = jnp.zeros(ctab_out.shape, F32)

    def ctab(t, start, rows):
        ctab_out[:12, start : start + HALF_RUN] = rows

    fold_tables(1, 12, gb_ref, y_ref, acc_ref, ctab)


QUARTERS = ((0, 0), (0, 1), (1, 1), (1, 0))
FINE_PAD = (176, 64, 32, 64)
PIECE = tuple(n + 48 for n in FINE_PAD)
BASE = tuple(sum(PIECE[:n]) for n in range(5))


def fine_rows_of(s, t, u):
    r = iota((FINE_PAD[QUARTERS.index((t, u))], 1), 0)
    width, height = 6 if u else 18, 3 if t else 9
    row = div_const(r, width)
    lat, lon = row + 9 * t, r - row * width + 18 * u
    wr, wc = div_const(lat, 6), div_const(lon, 12)
    target = (2 * wr + wc) * TOK + s * HALF + (lon - 12 * wc) * 6 + lat - 6 * wr
    return jnp.where(row < height, target, -1)


def coarse_rows_of(s, t, u):
    r = iota((24, 1), 0)
    row = div_const(r, 6)
    return jnp.where(row < 3, s * HALF + (r - row * 6 + 6 * u) * 6 + row + 3 * t, -1)


def back_kernel(
    x_in, gfo_ref, latp_ref, lonp_ref, corner_ref, bias_ref, fgain_ref, fqkv_ref, fproj_ref, ctab_ref, gains_ref, cout_ref,
    near0_out, later0_out, near1_out, later1_out, keep_out, send_out,
    src_ref, fq_ref, fk_ref, fv_ref, fm_ref, gm_ref, g_ref, gb_ref, y_ref, acc_ref, tab_ref, pack_out,
):
    src_ref[:576] = gfo_ref[...]
    src_ref[576:768] = latp_ref[...]
    src_ref[768:928] = lonp_ref[...]
    src_ref[928:] = corner_ref[...]
    z, h, w = window_index(TOK)
    hots = []
    for wr in range(2):
        for wc in range(2):
            lat, lon = 6 * wr + h, 12 * wc + w
            behind, before = lat < 3, lon < 6
            lat = jnp.where(behind, lat + 9, lat - 3)
            lon = jnp.where(before, lon + 18, lon - 6)
            p = 2 * (lat & 1) + (lon & 1)
            i, j = lax.shift_right_logical(lat, 1), lax.shift_right_logical(lon, 1)
            own = p * TOK + z * HALF + j * 6 + i
            from_lat = 576 + p * 48 + z * 24 + j * 2 + i - 4
            from_lon = 768 + p * 40 + z * 18 + (j - 9) * 6 + i
            target = jnp.where(before, from_lon + jnp.where(behind, 160, 0), jnp.where(behind, from_lat, own))
            hots.append(one_hot(target, 1088))
    gy = low(mm(jnp.concatenate(hots, axis=0), src_ref[...]))
    gy32 = gy.astype(F32)
    gb_ref[...] = jnp.zeros(gb_ref.shape, F32)
    weights = fine_weights(fqkv_ref)
    gain = fgain_ref[...].reshape(1, 192)
    x = x_in[...].reshape(4 * TOK, 192).astype(F32)
    (hat,), inv = norm([x])
    xn = low(hat * gain)
    fq_ref[...] = low(mm(xn, weights[0]) * HEAD**-0.5).reshape(4, TOK, 192)
    store_keys(fk_ref, mm(xn, weights[1]))
    store_keys(fv_ref, mm(xn, weights[2]))
    gm_ref[...] = low(mm_t(gy, fproj_ref[...])).reshape(4, TOK, 192)

    @pl.loop(0, 4, unroll=4)
    def _(n):
        wr = lax.shift_right_logical(n, 1)
        for start, width, slots in FINE_TILES:
            lanes = slice(start, start + width)

            rows = tile_rows(start, slots)

            def bias_grad_to(gs):
                gb_ref[wr, 0, rows] += gs[:, :128]
                gb_ref[wr, 1, rows] += gs[:, 128:]

            mixed, gq, gk, gv = tile_both(
                fq_ref[n, :, lanes], fk_ref[n, :, lanes], fv_ref[n, :, lanes], gm_ref[n, :, lanes],
                load_bias(bias_ref, wr, rows), bias_grad_to, slots,
            )
            fm_ref[n, :, lanes] = low(mixed)
            g_ref[0, n, :, lanes] = low(gq * HEAD**-0.5)
            g_ref[1, n, :, lanes] = low(unpad_keys(gk))
            g_ref[2, n, :, lanes] = low(unpad_keys(gv))

    dproj = t_mm(fm_ref[...].reshape(4 * TOK, 192), gy)
    grads = [g_ref[m].reshape(4 * TOK, 192) for m in range(3)]
    dqkv = [t_mm(xn, g) for g in grads]
    grolled = sum(mm_t(g, w) for g, w in zip(grads, weights))
    (gx,), (ggain,) = norm_back([low(grolled).astype(F32)], [gain], [hat], inv)
    fg = low(gy32 + gx)
    cout = cout_ref[...]
    for s, outs in enumerate(((near0_out, later0_out), (near1_out, later1_out))):
        hots, coarse_hots = [], []
        for t, u in QUARTERS:
            hots.append(one_hot(fine_rows_of(s, t, u), 4 * TOK))
            coarse_hots.append(one_hot(coarse_rows_of(s, t, u), TOK))
        fine = low(mm(jnp.concatenate(hots, axis=0), fg))
        coarse = low(mm(jnp.concatenate(coarse_hots, axis=0), cout))
        at = 0
        for n, rows in enumerate(FINE_PAD):
            out, to = outs[n // 2], BASE[n] - BASE[n // 2 * 2]
            out[to : to + rows] = fine[at : at + rows]
            out[to + rows : to + rows + 24] = coarse[24 * n : 24 * n + 24, :192]
            out[to + rows + 24 : to + rows + 48] = coarse[24 * n : 24 * n + 24, 192:]
            at += rows
    first = low(jnp.concatenate([dqkv[0], dqkv[1]], axis=1))
    second = low(jnp.concatenate([dqkv[2], dproj], axis=1))
    for c in range(3):
        put(pack_out, FINE, 192 * c, first[:, 128 * c : 128 * c + 128])
        put(pack_out, FINE, 576 + 192 * c, second[:, 128 * c : 128 * c + 128])
    put(pack_out, FINE, 1152, gain_rows([ggain]))
    put(pack_out, FINE, 1168, gains_ref[...])
    put(pack_out, FINE, 1184, jnp.zeros((96, 128), BF))
    tab_ref[...] = jnp.zeros(tab_ref.shape, F32)
    tab_ref[16:32] = ctab_ref[...]

    def ftab(t, start, rows):
        tab_ref[8 * t : 8 * t + 6, start : start + HALF_RUN] = rows

    fold_tables(2, 6, gb_ref, y_ref, acc_ref, ftab)
    for c in range(13):
        for half in range(2):
            lanes = slice(256 * c + 128 * half, 256 * c + 128 * half + 128)
            pack_out[c, FINE + 32 * half : FINE + 32 * half + 32] = low(tab_ref[:, lanes])
    for c in range(13, 16):
        pack_out[c, FINE:] = jnp.zeros((TAB, 128), BF)
    split_halves(pack_out, keep_out, send_out)


def place_kernel(near0_ref, near1_ref, later0_ref, later1_ref, lon_ref, field_out, coarse_out, src_ref):
    def chosen(later_row, later_col, values):
        value = dict(zip(QUARTERS, values))
        near = jnp.where(later_row, value[1, 0], value[0, 0])
        return jnp.where(later_col, jnp.where(later_row, value[1, 1], value[0, 1]), near)

    base = BASE[:4]
    r = iota((288, 1), 0)
    lat = div_const(r, 24)
    col = r - lat * 24
    later_row, later_col = lat < 3, col < 6
    row = jnp.where(later_row, lat, lat - 3)
    inside = jnp.where(later_col, row * 6 + col, row * 18 + col - 6)
    hots = [one_hot(chosen(later_row, later_col, base) + inside, sum(PIECE))]
    r = iota((HALF, 1), 0)
    lat = div_const(r, 12)
    col = r - lat * 12
    later_row, later_col = lat < 3, col < 6
    inside = jnp.where(later_row, lat, lat - 3) * 6 + jnp.where(later_col, col, col - 6)
    inside = inside + chosen(later_row, later_col, [b + n for b, n in zip(base, FINE_PAD)])
    hots += [one_hot(inside, sum(PIECE)), one_hot(inside + 24, sum(PIECE))]
    hot = jnp.concatenate(hots, axis=0)
    placed = []
    for s in range(2):
        src_ref[: BASE[1]] = (near0_ref, near1_ref)[s][: BASE[1]]
        src_ref[BASE[1] : BASE[3]] = lon_ref[s]
        src_ref[BASE[3] :] = (later0_ref, later1_ref)[s][PIECE[2] :]
        out = low(mm(hot, src_ref[...]))
        for h in range(12):
            field_out[1 - s, h] = out[24 * h : 24 * h + 24]
        coarse = jnp.concatenate([out[288:360], out[360:]], axis=1).astype(F32)
        placed.append(coarse)
    for h in range(6):
        rows = slice(12 * h, 12 * h + 12)
        coarse_out[h] = low(jnp.stack([placed[1][rows], placed[0][rows]], axis=1))


def unpack_kernel(fine_scale, coarse_scale, fine_table_scale, coarse_table_scale, mine_ref, other_ref, *outs):
    sums = mine_ref, other_ref, lax.axis_index("lon") % 2
    fgain_out, qkv_out, proj_out, ftab_out, mgain_out, mw_out, cgain_out, cqkv_out, cproj_out, ctab_out = outs
    def coarse_get(start, count):
        return get(sums, COARSE, 0, start, count) * coarse_scale

    def fine_get(start, count, scale):
        return get(sums, FINE, COARSE, start, count) * scale

    for c in range(3):
        lanes = slice(128 * c, 128 * c + 128)
        mw_out[:, lanes] = coarse_get(768 * c, 768)
        cproj_out[:, lanes] = coarse_get(5760 + 384 * c, 384)
        qkv_out[:, lanes] = fine_get(192 * c, 192, fine_scale)
    for c in range(9):
        cqkv_out[:, 128 * c : 128 * c + 128] = coarse_get(2304 + 384 * c, 384)
    second = [fine_get(576 + 192 * c, 192, fine_scale) for c in range(3)]
    qkv_out[:, 384:512] = second[0]
    qkv_out[:, 512:] = second[1][:, :64]
    proj_out[...] = jnp.concatenate([second[1][:, 64:], second[2]], axis=1)
    gains = fine_get(1168, 16, coarse_scale)
    for c in range(6):
        mgain_out[pl.ds(128 * c, 128)] = gains[c]
    for c in range(3):
        cgain_out[pl.ds(128 * c, 128)] = gains[6 + c]
    gains = fine_get(1152, 16, fine_scale)
    fgain_out[...] = jnp.concatenate([gains[:1], gains[1:2, :64]], axis=1).reshape(192)
    for c in range(13):
        for half in range(2):
            start = 256 * c + 128 * half
            n = min(128, POS - start)
            block = get_chunk(sums, c, slice(GRAIN + 32 * half, GRAIN + 32 * half + 32))[:, :n]
            both = jnp.stack([block[:6], block[8:14]], axis=1)
            ftab_out[:, :, start : start + n] = both * fine_table_scale
            ctab_out[:, 0, start : start + n] = block[16:28] * coarse_table_scale


def call(kernel, out_shapes, scratch=(), smem=0, flops=0, moved=0, vmem=VMEM_LIMIT):
    def run(*args):
        specs = [pl.BlockSpec(memory_space=pltpu.SMEM)] * smem
        specs += [pl.BlockSpec(memory_space=pltpu.VMEM)] * (len(args) - smem)
        return pl.pallas_call(
            kernel,
            out_shape=[jax.ShapeDtypeStruct(s, d) for s, d in out_shapes],
            in_specs=specs,
            out_specs=[pl.BlockSpec(memory_space=pltpu.VMEM)] * len(out_shapes),
            scratch_shapes=[pltpu.VMEM(s, d) for s, d in scratch],
            compiler_params=pltpu.CompilerParams(vmem_limit_bytes=vmem),
            cost_estimate=pl.CostEstimate(flops=flops, bytes_accessed=moved, transcendentals=0),
        )(*args)

    return run


def shifted(x, offset, sign):
    names = [n for n, o in zip(("lon", "lat", "rep"), offset[::-1]) if o]
    sizes = [lax.axis_size(n) for n in names]
    pairs = []
    for place in np.ndindex(*sizes):
        target = [(p - sign) % s for p, s in zip(place, sizes)]
        pairs.append((int(np.ravel_multi_index(place, sizes)), int(np.ravel_multi_index(target, sizes))))
    return lax.ppermute(x, tuple(names), pairs)


CORNERS = [(s, t, u) for s in range(2) for t in range(2) for u in range(2)]


def exchange(x, axes):
    return lax.all_to_all(lax.optimization_barrier(x), axes, 0, 0, tiled=True)


def summed(x):
    return jnp.sum(x.astype(F32), axis=0, keepdims=True).astype(BF)


def spread(x, count):
    return jnp.broadcast_to(x, (count,) + x.shape[1:])


def sibling(x):
    return lax.ppermute(x, "lon", [(i, i ^ 1) for i in range(lax.axis_size("lon"))])


def exchange_columns(x):
    size = lax.axis_size("lon")
    groups = [list(range(core, size, 2)) for core in range(2)]
    return lax.all_to_all(lax.optimization_barrier(x), "lon", 0, 0, axis_index_groups=groups, tiled=True)


def reduce_everywhere(keep, other, near0, later0, near1, later1):
    rest = lax.axis_size("lat") * lax.axis_size("rep")
    keep, other = lax.optimization_barrier((keep, other))
    pair = [(a.astype(F32) + b.astype(F32)).astype(BF) for a, b in zip(keep, other)]
    pack = exchange_columns(jnp.concatenate(pair, axis=1))
    pack = summed(pack)
    part = pack[:, :GRAIN].reshape(rest, -1, 128)
    near1, later0, later1 = (
        shifted(x, place, -1) for x, place in ((near1, (1, 0, 0)), (later0, (0, 1, 0)), (later1, (1, 1, 0)))
    )
    part = exchange(part, ("lat", "rep"))
    part, near1, later0, later1 = lax.optimization_barrier((part, near1, later0, later1))
    part = spread(summed(part), rest)
    column = [jnp.concatenate([x[BASE[1] :], y[: PIECE[2]]]) for x, y in ((near0, later0), (near1, later1))]
    column = shifted(jnp.stack(column), (0, 0, 1), -1)
    part, column = lax.optimization_barrier((exchange(part, ("lat", "rep")), column))
    mine = jnp.concatenate([part.reshape(1, GRAIN, 128), pack[:, GRAIN:]], axis=1)
    mine = exchange_columns(spread(mine, lax.axis_size("lon") // 2))
    return (mine, sibling(mine)), (near0, near1, later0, later1, column)


def body(
    fine_field, fine_gain, fine_qkv, fine_proj, fine_table, merge_gain, merge_weight,
    coarse_gain, coarse_qkv, coarse_proj, coarse_table, cotangent,
):
    rep, lat, lon = (lax.axis_size(n) for n in ("rep", "lat", "lon"))
    packs = call(pack_kernel, [((MESSAGE, 128), BF)] * 8)(fine_field, cotangent.transpose(1, 2, 0, 3))
    bufs = [shifted(b, place, 1) if any(place) else b for b, place in zip(packs, CORNERS)]
    table = fine_table[0].transpose(1, 0, 2)
    bias, cbias = call(
        bias_kernel,
        [((3, 2, FINE_ROWS, 128), F32), ((1, 2, COARSE_ROWS, 128), F32)],
        [((2, 34 * 32, 128), F32)],
        flops=1 << 32,
    )(table, shifted(fine_table, (0, 1, 0), 1)[0].transpose(1, 0, 2), coarse_table[0].transpose(1, 0, 2))
    x, gfo, latp, lonp, *coarse, cgains = call(
        main_kernel,
        [
            ((4, TOK, 192), BF), ((4, TOK, 192), BF), ((192, 192), BF), ((160, 192), BF),
            ((TOK, 384), BF), ((TOK, 384), BF), ((TOK, 384), BF), ((4, TOK, 192), BF), ((TOK, 384), BF),
            ((3, TOK, 128), BF), ((3, 3, TOK, 128), BF), ((1, 2, COARSE_ROWS, 128), F32), ((16, 128), BF),
        ],
        [
            ((9, TOK, 192), F32), ((9 * TOK, 192), BF),
            ((9, TOK, 192), BF), ((9, LANES, 192), BF), ((9, LANES, 192), BF), ((9, TOK, 192), BF),
            ((3, TOK, 128), BF), ((3, LANES, 128), BF), ((3, LANES, 128), BF), ((3, TOK, 128), BF),
        ],
        flops=1 << 34,
    )(
        *bufs, bias, cbias, fine_gain, fine_qkv, fine_proj, merge_gain,
        merge_weight, coarse_gain, coarse_qkv, coarse_proj,
    )
    lat_recv = shifted(latp, (0, 1, 0), -1)
    lon_recv = shifted(lonp, (0, 0, 1), -1)
    corner_recv = shifted(lonp, (0, 1, 1), -1)
    cout, ckeep, csend, ctab = call(
        side_kernel,
        [((TOK, 384), BF), ((8, COARSE, 128), BF), ((8, COARSE, 128), BF), ((16, WIDE), F32)],
        [((384, 256), F32), ((2, 512, 128), F32), ((16, COARSE, 128), BF)],
        flops=1 << 35,
    )(*coarse, coarse_proj)
    cother = sibling(csend)
    near0, later0, near1, later1, fkeep, fsend = call(
        back_kernel,
        [((BASE[2], 192), BF), ((BASE[4] - BASE[2], 192), BF),
         ((BASE[2], 192), BF), ((BASE[4] - BASE[2], 192), BF), ((8, FINE + TAB, 128), BF), ((8, FINE + TAB, 128), BF)],
        [
            ((1088, 192), BF), ((4, TOK, 192), BF), ((4, LANES, 192), BF), ((4, LANES, 192), BF),
            ((4, TOK, 192), BF), ((4, TOK, 192), BF), ((3, 4, TOK, 192), BF),
            ((2, 2, FINE_ROWS, 128), F32), ((192, 256), F32), ((2, 256, 128), F32), ((32, WIDE), F32), ((16, FINE + TAB, 128), BF),
        ],
        flops=1 << 33,
    )(x, gfo.reshape(4 * TOK, 192), lat_recv, lon_recv, corner_recv, bias, fine_gain, fine_qkv, fine_proj, ctab, cgains, cout)
    sums, back = reduce_everywhere((ckeep, fkeep), (cother, sibling(fsend)), near0, later0, near1, later1)
    field_grad, coarse_out = call(
        place_kernel, [((2, 12, 24, 192), BF), ((6, 12, 2, 384), BF)], [((sum(PIECE), 192), BF)]
    )(*back)
    levels, rows, cols = 2 * rep, 12 * lat, 24 * lon
    fine_scale = (levels * rows * cols) ** -0.5
    coarse_scale = (levels * rows * cols // 4) ** -0.5
    fine_table_scale = (cols // 12) ** -0.5
    coarse_table_scale = (cols // 24) ** -0.5
    fgain_g, fqkv_g, fproj_g, ftab_g, mgain_g, mw_g, cgain_g, cqkv_g, cproj_g, ctab_g = call(
        lambda *refs: unpack_kernel(fine_scale, coarse_scale, fine_table_scale, coarse_table_scale, *refs),
        [
            ((192,), F32), ((192, 576), F32), ((192, 192), F32), ((6, 2, POS), F32), ((768,), F32),
            ((768, 384), F32), ((384,), F32), ((384, 1152), F32), ((384, 384), F32), ((12, 1, POS), F32),
        ],
    )(*sums)
    return (
        coarse_out.transpose(2, 0, 1, 3), field_grad, fgain_g, fqkv_g, fproj_g, ftab_g.transpose(1, 0, 2)[None],
        mgain_g, mw_g, cgain_g, cqkv_g, cproj_g, ctab_g.transpose(1, 0, 2)[None],
    )


def solution(mesh):
    tokens, tables = P("rep", "lat", "lon", None), P("rep", "lat", None, None)
    return jax.shard_map(
        body,
        mesh=mesh,
        in_specs=(tokens, P(), P(), P(), tables, P(), P(), P(), P(), P(), tables, tokens),
        out_specs=(tokens, tokens, P(), P(), P(), tables, P(), P(), P(), P(), P(), tables),
        check_vma=False,
    )
```

```python
import numpy as np
import jax
import jax.numpy as jnp
from jax import lax
from jax.experimental import pallas as pl
from jax.experimental.pallas import tpu as pltpu
from jax.sharding import PartitionSpec as P

F32, BF = jnp.float32, jnp.bfloat16
EPS = 1e-05
TOK, HALF, LANES = 144, 72, 256
POS, DIAG = 3312, 23
RUN = 6 * DIAG
HEAD = 32
NEG = -1e30
COARSE, FINE, TAB = 432, 80, 64
GRAIN = COARSE + FINE
WIDE = 3456
FINE_ROWS, COARSE_ROWS = 6 * TOK + 8, 12 * TOK + 8
VMEM_LIMIT = 24 * 1024 * 1024


def dot(a, b, ca, cb):
    return lax.dot_general(a, b, (((ca,), (cb,)), ((), ())), preferred_element_type=F32)


def mm(a, b):
    return dot(a, b, 1, 0)


def mm_t(a, b):
    return dot(a, b, 1, 1)


def t_mm(a, b):
    return dot(a, b, 0, 0)


def low(x):
    return x.astype(BF)


def split3(x):
    hi = low(x)
    rest = x - hi.astype(F32)
    mid = low(rest)
    return hi, mid, low(rest - mid.astype(F32))


def iota(shape, dim):
    return lax.broadcasted_iota(jnp.int32, shape, dim)


def div_const(x, n):
    return lax.shift_right_logical(x * (65536 // n + 1), 16)


def one_hot(target, count):
    return jnp.where(iota((target.shape[0], count), 1) == target, 1.0, 0.0).astype(BF)


def window_index(rows):
    r = iota((rows, 1), 0)
    z = div_const(r, 72)
    r = r - z * 72
    w = div_const(r, 6)
    return z, r - w * 6, w


def pad_keys(x):
    gap = jnp.zeros((128 - HALF, x.shape[1]), F32)
    return low(jnp.concatenate([x[:HALF], gap, x[HALF:], gap], axis=0))


def unpad_keys(x):
    return jnp.concatenate([x[:HALF], x[128 : 128 + HALF]], axis=0)


def norm(x):
    width = sum(p.shape[1] for p in x)
    mean = sum(jnp.sum(p, axis=1, keepdims=True) for p in x) * (1.0 / width)
    shifted = [p - mean for p in x]
    var = sum(jnp.sum(p * p, axis=1, keepdims=True) for p in shifted) * (1.0 / width)
    inv = lax.rsqrt(var + EPS)
    return [p * inv for p in shifted], inv


def norm_back(grad, gain, hat, inv):
    width = sum(p.shape[1] for p in grad)
    scaled = [g * a for g, a in zip(grad, gain)]
    first = sum(jnp.sum(s, axis=1, keepdims=True) for s in scaled) * (1.0 / width)
    second = sum(jnp.sum(s * n, axis=1, keepdims=True) for s, n in zip(scaled, hat)) * (1.0 / width)
    gains = [jnp.sum(g * n, axis=0, keepdims=True) for g, n in zip(grad, hat)]
    return [inv * (s - first - n * second) for s, n in zip(scaled, hat)], gains


def load_bias(ref, kind, rows):
    return jnp.concatenate([ref[kind, 0, rows], ref[kind, 1, rows]], axis=1)


def head_mask(width, slot):
    lane = iota((1, width), 1)
    return (lane >= slot * HEAD) & (lane < (slot + 1) * HEAD)


def only_head(x, slot):
    return x * jnp.where(head_mask(x.shape[1], slot), 1.0, 0.0).astype(BF)


def by_head(x, slots):
    return jnp.concatenate([only_head(x, slot) for slot in range(slots)], axis=0)


def own_columns(x, slots):
    out = x[:TOK]
    for slot in range(1, slots):
        out = jnp.where(head_mask(x.shape[1], slot), x[slot * TOK : (slot + 1) * TOK], out)
    return out


def probabilities(q_stack, keys, bias):
    e = jnp.exp(mm_t(q_stack, keys) + bias)
    return e * (1.0 / jnp.sum(e, axis=1, keepdims=True))


def tile_forward(q, keys, values, bias, slots):
    p = probabilities(by_head(q, slots), keys, bias)
    return own_columns(mm(low(p), values), slots)


def tile_both(q, keys, values, gmix, bias, bias_grad_to, slots):
    q_stack, g_stack = by_head(q, slots), by_head(gmix, slots)
    p = probabilities(q_stack, keys, bias)
    p_low = low(p)
    mixed = own_columns(mm(p_low, values), slots)
    gp = mm_t(g_stack, values)
    gs = p * (gp - jnp.sum(p * gp, axis=1, keepdims=True))
    bias_grad_to(gs)
    gs_low = low(gs)
    gq = own_columns(mm(gs_low, keys), slots)
    return mixed, gq, t_mm(gs_low, q_stack), t_mm(p_low, g_stack)


def put(ref, grain, start, value):
    at = 0
    while at < value.shape[0]:
        chunk, row = divmod(start + at, grain)
        n = min(grain - row, value.shape[0] - at)
        ref[chunk, row : row + n] = value[at : at + n]
        at += n


def split_halves(pack_ref, keep_ref, send_ref):
    core = lax.axis_index("lon") % 2
    for own in range(2):

        @pl.when(core == own)
        def _():
            keep_ref[...] = pack_ref[8 * own : 8 * own + 8]
            send_ref[...] = pack_ref[8 - 8 * own : 16 - 8 * own]


def get_chunk(sums, chunk, rows):
    mine, other, core = sums
    return jnp.where(core == chunk // 8, mine[chunk % 8, rows].astype(F32), other[chunk % 8, rows].astype(F32))


def get(sums, grain, base, start, count):
    parts, at = [], 0
    while at < count:
        chunk, row = divmod(start + at, grain)
        n = min(grain - row, count - at)
        parts.append(get_chunk(sums, chunk, slice(base + row, base + row + n)))
        at += n
    return parts[0] if len(parts) == 1 else jnp.concatenate(parts, axis=0)


def gain_rows(pieces):
    line = pieces[0] if len(pieces) == 1 else jnp.concatenate(pieces, axis=1)
    width = line.shape[1]
    if width % 128:
        line = jnp.concatenate([line, jnp.zeros((1, 128 - width % 128), F32)], axis=1)
    rows = [line[:, 128 * i : 128 * i + 128] for i in range(line.shape[1] // 128)]
    rows.append(jnp.zeros((16 - len(rows), 128), F32))
    return low(jnp.concatenate(rows, axis=0))


def diagonal_select(first):
    lane = iota((1, 256), 1)
    wq = first + lax.shift_right_logical(lane, 7)
    lane = lane & 127
    wk = div_const(lane, 6)
    hk = lane - wk * 6
    diagonal = wq - wk + 11
    low_half = jnp.where((lane < HALF) & (hk < 3), hk * DIAG + diagonal, -1)
    high_half = jnp.where((lane < HALF) & (hk >= 3), (hk - 3) * DIAG + diagonal + 128, -1)
    target = jnp.maximum(low_half, high_half)
    return jnp.where(iota((256, 256), 0) == target, 1.0, 0.0).astype(BF)


HALF_RUN = 3 * DIAG


def table_groups():
    return [(g, (g // 12) * 16 + ((g // 6) % 2) * 8 + g % 6) for g in range(24)]


def table_slice(table, start):
    n = min(128, POS - start)
    part = table[:, start : start + n]
    if n < 128:
        part = jnp.concatenate([part, jnp.zeros((part.shape[0], 128 - n), F32)], axis=1)
    return part


def expand_tables(at_end, kinds, u_ref):
    lane, sub = iota((8, 128), 1), iota((8, 128), 0)
    column = div_const(lane, 6)
    crossing = (sub >= 3) != (lane - column * 6 >= 3)
    outside = jnp.where(lane >= HALF, NEG, 0.0)
    lev_term = jnp.where(at_end[0], NEG, 0.0)
    lat_term = jnp.where(crossing, jnp.where(at_end[1], NEG, 0.0), 0.0)
    u_ref[...] = jnp.zeros(u_ref.shape, F32)
    base = 0
    for table, _, _ in kinds:
        heads = table.shape[0]
        for g, row in table_groups():
            for half in range(2):
                u_ref[half, pl.ds(base + row, heads, stride=32)] = table_slice(table, g * RUN + half * HALF_RUN)
        base += heads * 32
    u = jnp.concatenate([u_ref[0, :base], u_ref[1, :base]], axis=1)
    hi = low(u)
    mid = low(u - hi.astype(F32))
    for first in range(0, 12, 2):
        sel = diagonal_select(first)
        x = mm(hi, sel) + mm(mid, sel)
        base = 0
        for table, may_end, out_ref in kinds:
            same = outside + lat_term if may_end else outside
            terms = same, same + lev_term
            for n in range(table.shape[0]):
                for zq in range(2):
                    for zk in range(2):
                        at = base + zq * 16 + zk * 8
                        for k in range(2):
                            to = n * TOK + zq * HALF + (first + k) * 6
                            part = x[at : at + 8, 128 * k : 128 * k + 128]
                            out_ref[zk, to : to + 6] = (part + terms[zq != zk])[:6]
                base += 32


def fold_tables(types, heads, grad_ref, y_ref, acc_ref, out_to):
    y_ref[...] = jnp.zeros(y_ref.shape, F32)
    for t in range(types):
        acc = None
        for first in range(0, 12, 2):
            sel = diagonal_select(first)
            for n in range(heads):
                for zq in range(2):
                    for zk in range(2):
                        at = n * 32 + zq * 16 + zk * 8
                        for k in range(2):
                            to = n * TOK + zq * HALF + (first + k) * 6
                            y_ref[at : at + 6, 128 * k : 128 * k + 128] = grad_ref[t, zk, to : to + 6]
            y = y_ref[...]
            hi = low(y)
            part = mm_t(hi, sel) + mm_t(low(y - hi.astype(F32)), sel)
            acc = part if acc is None else acc + part
        for half in range(2):
            acc_ref[half, : heads * 32] = acc[:, 128 * half : 128 * half + 128]
        for g, row in table_groups():
            for half in range(2):
                out_to(t, g * RUN + half * HALF_RUN, acc_ref[half, pl.ds(row, heads, stride=32)][:, :HALF_RUN])


def bias_kernel(fine_ref, next_ref, coarse_ref, fine_out, coarse_out, u_ref):
    at_end = [lax.axis_index(name) == lax.axis_size(name) - 1 for name in ("rep", "lat")]
    own, later, coarse = fine_ref[...], next_ref[...], coarse_ref[...]
    kinds = [
        (own[:, 0, :], False, fine_out.at[0]),
        (own[:, 1, :], True, fine_out.at[1]),
        (later[:, 0, :], False, fine_out.at[2]),
        (coarse[:, 0, :], True, coarse_out.at[0]),
    ]
    expand_tables(at_end, kinds, u_ref)


FIELD_PAD, COT_PAD = 176, 24
MESSAGE = FIELD_PAD + FIELD_PAD // 2 + 3 * COT_PAD


def pack_kernel(field_ref, cot_ref, *outs):
    r = iota((FIELD_PAD, 1), 0)
    row = div_const(r, 18)
    rc = iota((COT_PAD, 1), 0)
    crow = div_const(rc, 6)
    hots, cot_hots = [], []
    for t in range(2):
        for u in range(2):
            target = (row + (0 if t else 3)) * 24 + r - row * 18 + (0 if u else 6)
            hots.append(one_hot(jnp.where(r < 162, target, -1), 288))
    hot = jnp.concatenate(hots, axis=0)
    for s in range(2):
        for t in range(2):
            for u in range(2):
                target = (crow + (0 if t else 3)) * 12 + rc - crow * 6 + (0 if u else 6)
                cot_hots.append(one_hot(jnp.where(rc < 18, target * 2 + 1 - s, -1), TOK))
    cot = mm(jnp.concatenate(cot_hots, axis=0), low(cot_ref[...].astype(F32).reshape(TOK, 384)))
    half = FIELD_PAD // 2
    for s in range(2):
        rows = mm(hot, low(field_ref[1 - s].astype(F32).reshape(288, 192)))
        for n in range(4):
            out = outs[4 * s + n]
            part = rows[n * FIELD_PAD : (n + 1) * FIELD_PAD]
            out[:FIELD_PAD] = low(part[:, :128])
            rest = [low(jnp.concatenate([part[:half, 128:], part[half:, 128:]], axis=1))]
            first = (4 * s + n) * COT_PAD
            rest += [low(cot[first : first + COT_PAD, 128 * c : 128 * c + 128]) for c in range(3)]
            out[FIELD_PAD:] = jnp.concatenate([x.astype(F32) for x in rest], axis=0).astype(BF)


def field_of(ref):
    half = FIELD_PAD // 2
    rest = ref[FIELD_PAD : FIELD_PAD + half].astype(F32)
    rest = jnp.concatenate([rest[:, :64], rest[:, 64:]], axis=0)
    return low(jnp.concatenate([ref[:FIELD_PAD].astype(F32), rest], axis=1))


def cot_of(ref):
    rows = ref[FIELD_PAD:].astype(F32)[FIELD_PAD // 2 :]
    return low(jnp.concatenate([rows[COT_PAD * c : COT_PAD * c + COT_PAD] for c in range(3)], axis=1))


def fine_weights(qkv_ref):
    w = qkv_ref[...]
    return w[:, :192], w[:, 192:384], w[:, 384:]


FINE_TILES = ((0, 128, 4), (128, 64, 2))


def tile_rows(start, slots):
    return slice(start // HEAD * TOK, (start // HEAD + slots) * TOK)


def store_keys(ref, x):
    gap = jnp.zeros((128 - HALF, x.shape[1]), F32)
    for n in range(ref.shape[0]):
        part = x[n * TOK : (n + 1) * TOK]
        for z in range(2):
            ref[n, 128 * z : 128 * z + 128] = low(jnp.concatenate([part[HALF * z : HALF * z + HALF], gap], axis=0))


def main_kernel(
    b000, b001, b010, b011, b100, b101, b110, b111,
    bias_ref, cbias_ref,
    fgain_ref, fqkv_ref, fproj_ref, mgain_ref, mw_ref, cgain_ref, cqkv_ref, cproj_ref,
    x_out, gfo_out, latp_out, lonp_out, cin_out, gy_out, xc_out, mnorm_out, gci_out, mix_ref, g_ref, gb_ref, gains_out,
    x_ref, fo_ref, fq_ref, fk_ref, fv_ref, fm_ref,
    q_ref, k_ref, v_ref, gm_ref,
):
    bufs = ((b000, b001), (b010, b011)), ((b100, b101), (b110, b111))
    _, hh, ww = window_index(HALF)
    seen = set()
    for t in range(2):
        for u in range(2):
            hots = []
            for wr in (t, t + 1):
                for wc in (u, u + 1):
                    lat = 6 * wr + hh - 9 * t
                    lon = 12 * wc + ww - 18 * u
                    good = (lat >= 0) & (lat < 9) & (lon >= 0) & (lon < 18)
                    hots.append(one_hot(jnp.where(good, lat * 18 + lon, -1), FIELD_PAD))
            hot = jnp.concatenate(hots, axis=0)
            for z in range(2):
                part = mm(hot, field_of(bufs[z][t][u]))
                for n in range(4):
                    place = 3 * (t + n // 2) + u + n % 2, slice(z * HALF, (z + 1) * HALF)
                    value = part[n * HALF : (n + 1) * HALF]
                    if (place[0], z) in seen:
                        value = value + x_ref[place]
                    seen.add((place[0], z))
                    x_ref[place] = value
    for wr in range(2):
        for wc in range(2):
            x_out[2 * wr + wc] = low(x_ref[3 * wr + wc])
    wq, wk, wv = fine_weights(fqkv_ref)
    x = x_ref[...].reshape(9 * TOK, 192)
    (hat,), _ = norm([x])
    xn = low(hat * fgain_ref[...].reshape(1, 192))
    fq_ref[...] = low(mm(xn, wq) * HEAD**-0.5).reshape(9, TOK, 192)
    store_keys(fk_ref, mm(xn, wk))
    store_keys(fv_ref, mm(xn, wv))

    def fine_window(w, table_ref, wr):
        for start, width, slots in FINE_TILES:
            lanes = slice(start, start + width)

            bias = load_bias(table_ref, wr, tile_rows(start, slots))
            fm_ref[w, :, lanes] = low(
                tile_forward(fq_ref[w, :, lanes], fk_ref[w, :, lanes], fv_ref[w, :, lanes], bias, slots)
            )

    @pl.loop(0, 9, unroll=3)
    def _(w):
        fine_window(w, bias_ref, div_const(w, 3))

    out = low(mm(fm_ref[...].reshape(9 * TOK, 192), fproj_ref[...])).astype(F32)
    fo_ref[...] = low(x_ref[...].reshape(9 * TOK, 192) + out)

    z, i, j = window_index(TOK)
    hots = []
    for p in range(4):
        lat = 3 + 2 * i + p // 2
        lon = 6 + 2 * j + p % 2
        wr, wc = div_const(lat, 6), div_const(lon, 12)
        target = (3 * wr + wc) * TOK + z * HALF + (lon - 12 * wc) * 6 + lat - 6 * wr
        hots.append(one_hot(target, 9 * TOK))
    merged = mm(jnp.concatenate(hots, axis=0), fo_ref[...])
    merged = [merged[p * TOK : (p + 1) * TOK] for p in range(4)]
    mhat, minv = norm(merged)
    mgain = mgain_ref[...].reshape(1, 768)
    mgain = [mgain[:, 192 * p : 192 * p + 192] for p in range(4)]
    mnorm = [low(h * g) for h, g in zip(mhat, mgain)]
    mweight = [mw_ref[192 * p : 192 * p + 192] for p in range(4)]
    cin = low(sum(mm(n, w) for n, w in zip(mnorm, mweight))).astype(F32)
    (chat,), cinv = norm([cin])
    cgain = cgain_ref[...].reshape(1, 384)
    xc = low(chat * cgain)
    _, ci, cj = window_index(HALF)
    cot_rows = [None, None]
    for t in range(2):
        for u in range(2):
            lat, lon = ci - 3 * t, cj - 6 * u
            good = (lat >= 0) & (lat < 3) & (lon >= 0) & (lon < 6)
            hot = one_hot(jnp.where(good, lat * 6 + lon, -1), COT_PAD)
            for s in range(2):
                part = mm(hot, cot_of(bufs[s][t][u]))
                cot_rows[s] = part if cot_rows[s] is None else cot_rows[s] + part
    cot = jnp.concatenate(cot_rows, axis=0)
    gy = low(cot)
    gmix = low(mm_t(gy, cproj_ref[...]))
    for tile in range(3):
        lanes = slice(128 * tile, 128 * tile + 128)
        q_ref[tile] = low(mm(xc, cqkv_ref[:, lanes]) * HEAD**-0.5)
        k_ref[tile] = pad_keys(mm(xc, cqkv_ref[:, 384 + 128 * tile : 512 + 128 * tile]))
        v_ref[tile] = pad_keys(mm(xc, cqkv_ref[:, 768 + 128 * tile : 896 + 128 * tile]))
        gm_ref[tile] = gmix[:, lanes]

    def coarse_tile(tile, carry):
        rows = pl.ds(pl.multiple_of(tile * 4 * TOK, 64), 4 * TOK)

        def bias_grad_to(gs):
            gb_ref[0, 0, rows] = gs[:, :128]
            gb_ref[0, 1, rows] = gs[:, 128:]

        mixed, gq, gk, gv = tile_both(
            q_ref[tile], k_ref[tile], v_ref[tile], gm_ref[tile], load_bias(cbias_ref, 0, rows), bias_grad_to, 4
        )
        mix_ref[tile] = low(mixed)
        g_ref[0, tile] = low(gq * HEAD**-0.5)
        g_ref[1, tile] = low(unpad_keys(gk))
        g_ref[2, tile] = low(unpad_keys(gv))
        return carry

    lax.fori_loop(0, 3, coarse_tile, 0, unroll=True)
    grolled = None
    for tile in range(3):
        for m in range(3):
            wcols = slice(384 * m + 128 * tile, 384 * m + 128 * tile + 128)
            part = mm_t(g_ref[m, tile], cqkv_ref[:, wcols])
            grolled = part if grolled is None else grolled + part
    cin_out[...] = low(cin)
    gy_out[...] = gy
    xc_out[...] = xc
    (gci,), (cgain_grad,) = norm_back([low(grolled).astype(F32)], [cgain], [chat], cinv)
    gci = low(cot + gci)
    gml = []
    gci_out[...] = gci
    for p in range(4):
        mnorm_out[p] = mnorm[p]
        gml.append(low(mm_t(gci, mweight[p])).astype(F32))
    gmerged, mgain_grad = norm_back(gml, mgain, mhat, minv)
    gains_out[...] = gain_rows(list(mgain_grad) + [cgain_grad])
    r48 = iota((48, 1), 0)
    zi = div_const(r48, 24)
    rest = r48 - 24 * zi
    lat_hot = one_hot(zi * HALF + lax.shift_right_logical(rest, 1) * 6 + 4 + (rest & 1), TOK)
    r40 = iota((40, 1), 0)
    zi = jnp.where(r40 >= 18, 1, 0)
    lon_hot = one_hot(jnp.where(r40 < 36, zi * HALF + 54 + r40 - 18 * zi, -1), TOK)
    hot = jnp.concatenate([lat_hot, lon_hot], axis=0)
    for p in range(4):
        g = low(gmerged[p])
        gfo_out[p] = g
        part = low(mm(hot, g))
        latp_out[48 * p : 48 * p + 48] = part[:48]
        lonp_out[40 * p : 40 * p + 40] = part[48:]


def side_kernel(
    cin_ref, gy_ref, xc_ref, mnorm_ref, gci_ref, mix_ref, g_ref, gb_ref, cproj_ref,
    cout_out, keep_out, send_out, ctab_out, y_ref, acc_ref, pack_out,
):
    gy, xc, gci = gy_ref[...], xc_ref[...], gci_ref[...]
    out = None
    for tile in range(3):
        lanes = slice(128 * tile, 128 * tile + 128)
        part = mm(mix_ref[tile], cproj_ref[lanes])
        out = part if out is None else out + part
        dproj = low(t_mm(mix_ref[tile], gy))
        for c in range(3):
            start = 5760 + 384 * c + 128 * tile
            put(pack_out, COARSE, start, dproj[:, 128 * c : 128 * c + 128])
    cout_out[...] = low(cin_ref[...].astype(F32) + low(out).astype(F32))
    for m in range(3):
        dqkv = low(t_mm(xc, jnp.concatenate([g_ref[m, tile] for tile in range(3)], axis=1)))
        for tile in range(3):
            start = 2304 + 384 * (3 * m + tile)
            put(pack_out, COARSE, start, dqkv[:, 128 * tile : 128 * tile + 128])
    for p in range(4):
        dmw = low(t_mm(mnorm_ref[p], gci))
        for c in range(3):
            start = 768 * c + 192 * p
            put(pack_out, COARSE, start, dmw[:, 128 * c : 128 * c + 128])
    split_halves(pack_out, keep_out, send_out)
    ctab_out[...] = jnp.zeros(ctab_out.shape, F32)

    def ctab(t, start, rows):
        ctab_out[:12, start : start + HALF_RUN] = rows

    fold_tables(1, 12, gb_ref, y_ref, acc_ref, ctab)


QUARTERS = ((0, 0), (0, 1), (1, 1), (1, 0))
FINE_PAD = (176, 64, 32, 64)
PIECE = tuple(n + 48 for n in FINE_PAD)
BASE = tuple(sum(PIECE[:n]) for n in range(5))


def fine_rows_of(s, t, u):
    r = iota((FINE_PAD[QUARTERS.index((t, u))], 1), 0)
    width, height = 6 if u else 18, 3 if t else 9
    row = div_const(r, width)
    lat, lon = row + 9 * t, r - row * width + 18 * u
    wr, wc = div_const(lat, 6), div_const(lon, 12)
    target = (2 * wr + wc) * TOK + s * HALF + (lon - 12 * wc) * 6 + lat - 6 * wr
    return jnp.where(row < height, target, -1)


def coarse_rows_of(s, t, u):
    r = iota((24, 1), 0)
    row = div_const(r, 6)
    return jnp.where(row < 3, s * HALF + (r - row * 6 + 6 * u) * 6 + row + 3 * t, -1)


def back_kernel(
    x_in, gfo_ref, latp_ref, lonp_ref, corner_ref, bias_ref, fgain_ref, fqkv_ref, fproj_ref, ctab_ref, gains_ref, cout_ref,
    near0_out, later0_out, near1_out, later1_out, keep_out, send_out,
    src_ref, fq_ref, fk_ref, fv_ref, fm_ref, gm_ref, g_ref, gb_ref, y_ref, acc_ref, tab_ref, pack_out,
):
    src_ref[:576] = gfo_ref[...]
    src_ref[576:768] = latp_ref[...]
    src_ref[768:928] = lonp_ref[...]
    src_ref[928:] = corner_ref[...]
    z, h, w = window_index(TOK)
    hots = []
    for wr in range(2):
        for wc in range(2):
            lat, lon = 6 * wr + h, 12 * wc + w
            behind, before = lat < 3, lon < 6
            lat = jnp.where(behind, lat + 9, lat - 3)
            lon = jnp.where(before, lon + 18, lon - 6)
            p = 2 * (lat & 1) + (lon & 1)
            i, j = lax.shift_right_logical(lat, 1), lax.shift_right_logical(lon, 1)
            own = p * TOK + z * HALF + j * 6 + i
            from_lat = 576 + p * 48 + z * 24 + j * 2 + i - 4
            from_lon = 768 + p * 40 + z * 18 + (j - 9) * 6 + i
            target = jnp.where(before, from_lon + jnp.where(behind, 160, 0), jnp.where(behind, from_lat, own))
            hots.append(one_hot(target, 1088))
    gy = low(mm(jnp.concatenate(hots, axis=0), src_ref[...]))
    gy32 = gy.astype(F32)
    gb_ref[...] = jnp.zeros(gb_ref.shape, F32)
    weights = fine_weights(fqkv_ref)
    gain = fgain_ref[...].reshape(1, 192)
    x = x_in[...].reshape(4 * TOK, 192).astype(F32)
    (hat,), inv = norm([x])
    xn = low(hat * gain)
    fq_ref[...] = low(mm(xn, weights[0]) * HEAD**-0.5).reshape(4, TOK, 192)
    store_keys(fk_ref, mm(xn, weights[1]))
    store_keys(fv_ref, mm(xn, weights[2]))
    gm_ref[...] = low(mm_t(gy, fproj_ref[...])).reshape(4, TOK, 192)

    @pl.loop(0, 4)
    def _(n):
        wr = lax.shift_right_logical(n, 1)
        for start, width, slots in FINE_TILES:
            lanes = slice(start, start + width)

            rows = tile_rows(start, slots)

            def bias_grad_to(gs):
                gb_ref[wr, 0, rows] += gs[:, :128]
                gb_ref[wr, 1, rows] += gs[:, 128:]

            mixed, gq, gk, gv = tile_both(
                fq_ref[n, :, lanes], fk_ref[n, :, lanes], fv_ref[n, :, lanes], gm_ref[n, :, lanes],
                load_bias(bias_ref, wr, rows), bias_grad_to, slots,
            )
            fm_ref[n, :, lanes] = low(mixed)
            g_ref[0, n, :, lanes] = low(gq * HEAD**-0.5)
            g_ref[1, n, :, lanes] = low(unpad_keys(gk))
            g_ref[2, n, :, lanes] = low(unpad_keys(gv))

    dproj = t_mm(fm_ref[...].reshape(4 * TOK, 192), gy)
    grads = [g_ref[m].reshape(4 * TOK, 192) for m in range(3)]
    dqkv = [t_mm(xn, g) for g in grads]
    grolled = sum(mm_t(g, w) for g, w in zip(grads, weights))
    (gx,), (ggain,) = norm_back([low(grolled).astype(F32)], [gain], [hat], inv)
    fg = low(gy32 + gx)
    cout = cout_ref[...]
    for s, outs in enumerate(((near0_out, later0_out), (near1_out, later1_out))):
        hots, coarse_hots = [], []
        for t, u in QUARTERS:
            hots.append(one_hot(fine_rows_of(s, t, u), 4 * TOK))
            coarse_hots.append(one_hot(coarse_rows_of(s, t, u), TOK))
        fine = low(mm(jnp.concatenate(hots, axis=0), fg))
        coarse = low(mm(jnp.concatenate(coarse_hots, axis=0), cout))
        at = 0
        for n, rows in enumerate(FINE_PAD):
            out, to = outs[n // 2], BASE[n] - BASE[n // 2 * 2]
            out[to : to + rows] = fine[at : at + rows]
            out[to + rows : to + rows + 24] = coarse[24 * n : 24 * n + 24, :192]
            out[to + rows + 24 : to + rows + 48] = coarse[24 * n : 24 * n + 24, 192:]
            at += rows
    first = low(jnp.concatenate([dqkv[0], dqkv[1]], axis=1))
    second = low(jnp.concatenate([dqkv[2], dproj], axis=1))
    for c in range(3):
        put(pack_out, FINE, 192 * c, first[:, 128 * c : 128 * c + 128])
        put(pack_out, FINE, 576 + 192 * c, second[:, 128 * c : 128 * c + 128])
    put(pack_out, FINE, 1152, gain_rows([ggain]))
    put(pack_out, FINE, 1168, gains_ref[...])
    put(pack_out, FINE, 1184, jnp.zeros((96, 128), BF))
    tab_ref[...] = jnp.zeros(tab_ref.shape, F32)
    tab_ref[16:32] = ctab_ref[...]

    def ftab(t, start, rows):
        tab_ref[8 * t : 8 * t + 6, start : start + HALF_RUN] = rows

    fold_tables(2, 6, gb_ref, y_ref, acc_ref, ftab)
    for c in range(13):
        for half in range(2):
            lanes = slice(256 * c + 128 * half, 256 * c + 128 * half + 128)
            pack_out[c, FINE + 32 * half : FINE + 32 * half + 32] = low(tab_ref[:, lanes])
    for c in range(13, 16):
        pack_out[c, FINE:] = jnp.zeros((TAB, 128), BF)
    split_halves(pack_out, keep_out, send_out)


def place_kernel(near0_ref, near1_ref, later0_ref, later1_ref, lon_ref, field_out, coarse_out, src_ref):
    def chosen(later_row, later_col, values):
        value = dict(zip(QUARTERS, values))
        near = jnp.where(later_row, value[1, 0], value[0, 0])
        return jnp.where(later_col, jnp.where(later_row, value[1, 1], value[0, 1]), near)

    base = BASE[:4]
    r = iota((288, 1), 0)
    lat = div_const(r, 24)
    col = r - lat * 24
    later_row, later_col = lat < 3, col < 6
    row = jnp.where(later_row, lat, lat - 3)
    inside = jnp.where(later_col, row * 6 + col, row * 18 + col - 6)
    hots = [one_hot(chosen(later_row, later_col, base) + inside, sum(PIECE))]
    r = iota((HALF, 1), 0)
    lat = div_const(r, 12)
    col = r - lat * 12
    later_row, later_col = lat < 3, col < 6
    inside = jnp.where(later_row, lat, lat - 3) * 6 + jnp.where(later_col, col, col - 6)
    inside = inside + chosen(later_row, later_col, [b + n for b, n in zip(base, FINE_PAD)])
    hots += [one_hot(inside, sum(PIECE)), one_hot(inside + 24, sum(PIECE))]
    hot = jnp.concatenate(hots, axis=0)
    placed = []
    for s in range(2):
        src_ref[: BASE[1]] = (near0_ref, near1_ref)[s][: BASE[1]]
        src_ref[BASE[1] : BASE[3]] = lon_ref[s]
        src_ref[BASE[3] :] = (later0_ref, later1_ref)[s][PIECE[2] :]
        out = low(mm(hot, src_ref[...]))
        for h in range(12):
            field_out[1 - s, h] = out[24 * h : 24 * h + 24]
        coarse = jnp.concatenate([out[288:360], out[360:]], axis=1).astype(F32)
        placed.append(coarse)
    for h in range(6):
        rows = slice(12 * h, 12 * h + 12)
        coarse_out[h] = low(jnp.stack([placed[1][rows], placed[0][rows]], axis=1))


def unpack_kernel(fine_scale, coarse_scale, fine_table_scale, coarse_table_scale, mine_ref, other_ref, *outs):
    sums = mine_ref, other_ref, lax.axis_index("lon") % 2
    fgain_out, qkv_out, proj_out, ftab_out, mgain_out, mw_out, cgain_out, cqkv_out, cproj_out, ctab_out = outs
    def coarse_get(start, count):
        return get(sums, COARSE, 0, start, count) * coarse_scale

    def fine_get(start, count, scale):
        return get(sums, FINE, COARSE, start, count) * scale

    for c in range(3):
        lanes = slice(128 * c, 128 * c + 128)
        mw_out[:, lanes] = coarse_get(768 * c, 768)
        cproj_out[:, lanes] = coarse_get(5760 + 384 * c, 384)
        qkv_out[:, lanes] = fine_get(192 * c, 192, fine_scale)
    for c in range(9):
        cqkv_out[:, 128 * c : 128 * c + 128] = coarse_get(2304 + 384 * c, 384)
    second = [fine_get(576 + 192 * c, 192, fine_scale) for c in range(3)]
    qkv_out[:, 384:512] = second[0]
    qkv_out[:, 512:] = second[1][:, :64]
    proj_out[...] = jnp.concatenate([second[1][:, 64:], second[2]], axis=1)
    gains = fine_get(1168, 16, coarse_scale)
    for c in range(6):
        mgain_out[pl.ds(128 * c, 128)] = gains[c]
    for c in range(3):
        cgain_out[pl.ds(128 * c, 128)] = gains[6 + c]
    gains = fine_get(1152, 16, fine_scale)
    fgain_out[...] = jnp.concatenate([gains[:1], gains[1:2, :64]], axis=1).reshape(192)
    for c in range(13):
        for half in range(2):
            start = 256 * c + 128 * half
            n = min(128, POS - start)
            block = get_chunk(sums, c, slice(GRAIN + 32 * half, GRAIN + 32 * half + 32))[:, :n]
            both = jnp.stack([block[:6], block[8:14]], axis=1)
            ftab_out[:, :, start : start + n] = both * fine_table_scale
            ctab_out[:, 0, start : start + n] = block[16:28] * coarse_table_scale


def call(kernel, out_shapes, scratch=(), smem=0, flops=0, moved=0, vmem=VMEM_LIMIT):
    def run(*args):
        specs = [pl.BlockSpec(memory_space=pltpu.SMEM)] * smem
        specs += [pl.BlockSpec(memory_space=pltpu.VMEM)] * (len(args) - smem)
        return pl.pallas_call(
            kernel,
            out_shape=[jax.ShapeDtypeStruct(s, d) for s, d in out_shapes],
            in_specs=specs,
            out_specs=[pl.BlockSpec(memory_space=pltpu.VMEM)] * len(out_shapes),
            scratch_shapes=[pltpu.VMEM(s, d) for s, d in scratch],
            compiler_params=pltpu.CompilerParams(vmem_limit_bytes=vmem),
            cost_estimate=pl.CostEstimate(flops=flops, bytes_accessed=moved, transcendentals=0),
        )(*args)

    return run


def shifted(x, offset, sign):
    names = [n for n, o in zip(("lon", "lat", "rep"), offset[::-1]) if o]
    sizes = [lax.axis_size(n) for n in names]
    pairs = []
    for place in np.ndindex(*sizes):
        target = [(p - sign) % s for p, s in zip(place, sizes)]
        pairs.append((int(np.ravel_multi_index(place, sizes)), int(np.ravel_multi_index(target, sizes))))
    return lax.ppermute(x, tuple(names), pairs)


CORNERS = [(s, t, u) for s in range(2) for t in range(2) for u in range(2)]


def exchange(x, axes):
    return lax.all_to_all(lax.optimization_barrier(x), axes, 0, 0, tiled=True)


def summed(x):
    return jnp.sum(x.astype(F32), axis=0, keepdims=True).astype(BF)


def spread(x, count):
    return jnp.broadcast_to(x, (count,) + x.shape[1:])


def sibling(x):
    return lax.ppermute(x, "lon", [(i, i ^ 1) for i in range(lax.axis_size("lon"))])


def exchange_columns(x):
    size = lax.axis_size("lon")
    groups = [list(range(core, size, 2)) for core in range(2)]
    return lax.all_to_all(lax.optimization_barrier(x), "lon", 0, 0, axis_index_groups=groups, tiled=True)


def reduce_everywhere(keep, other, near0, later0, near1, later1):
    rest = lax.axis_size("lat") * lax.axis_size("rep")
    keep, other = lax.optimization_barrier((keep, other))
    pair = [(a.astype(F32) + b.astype(F32)).astype(BF) for a, b in zip(keep, other)]
    pack = exchange_columns(jnp.concatenate(pair, axis=1))
    pack = summed(pack)
    part = pack[:, :GRAIN].reshape(rest, -1, 128)
    near1, later0, later1 = (
        shifted(x, place, -1) for x, place in ((near1, (1, 0, 0)), (later0, (0, 1, 0)), (later1, (1, 1, 0)))
    )
    part = exchange(part, ("lat", "rep"))
    part, near1, later0, later1 = lax.optimization_barrier((part, near1, later0, later1))
    part = spread(summed(part), rest)
    column = [jnp.concatenate([x[BASE[1] :], y[: PIECE[2]]]) for x, y in ((near0, later0), (near1, later1))]
    column = shifted(jnp.stack(column), (0, 0, 1), -1)
    part, column = lax.optimization_barrier((exchange(part, ("lat", "rep")), column))
    mine = jnp.concatenate([part.reshape(1, GRAIN, 128), pack[:, GRAIN:]], axis=1)
    mine = exchange_columns(spread(mine, lax.axis_size("lon") // 2))
    return (mine, sibling(mine)), (near0, near1, later0, later1, column)


def body(
    fine_field, fine_gain, fine_qkv, fine_proj, fine_table, merge_gain, merge_weight,
    coarse_gain, coarse_qkv, coarse_proj, coarse_table, cotangent,
):
    rep, lat, lon = (lax.axis_size(n) for n in ("rep", "lat", "lon"))
    packs = call(pack_kernel, [((MESSAGE, 128), BF)] * 8)(fine_field, cotangent.transpose(1, 2, 0, 3))
    bufs = [shifted(b, place, 1) if any(place) else b for b, place in zip(packs, CORNERS)]
    table = fine_table[0].transpose(1, 0, 2)
    bias, cbias = call(
        bias_kernel,
        [((3, 2, FINE_ROWS, 128), F32), ((1, 2, COARSE_ROWS, 128), F32)],
        [((2, 34 * 32, 128), F32)],
        flops=1 << 32,
    )(table, shifted(fine_table, (0, 1, 0), 1)[0].transpose(1, 0, 2), coarse_table[0].transpose(1, 0, 2))
    x, gfo, latp, lonp, *coarse, cgains = call(
        main_kernel,
        [
            ((4, TOK, 192), BF), ((4, TOK, 192), BF), ((192, 192), BF), ((160, 192), BF),
            ((TOK, 384), BF), ((TOK, 384), BF), ((TOK, 384), BF), ((4, TOK, 192), BF), ((TOK, 384), BF),
            ((3, TOK, 128), BF), ((3, 3, TOK, 128), BF), ((1, 2, COARSE_ROWS, 128), F32), ((16, 128), BF),
        ],
        [
            ((9, TOK, 192), F32), ((9 * TOK, 192), BF),
            ((9, TOK, 192), BF), ((9, LANES, 192), BF), ((9, LANES, 192), BF), ((9, TOK, 192), BF),
            ((3, TOK, 128), BF), ((3, LANES, 128), BF), ((3, LANES, 128), BF), ((3, TOK, 128), BF),
        ],
        flops=1 << 34,
    )(
        *bufs, bias, cbias, fine_gain, fine_qkv, fine_proj, merge_gain,
        merge_weight, coarse_gain, coarse_qkv, coarse_proj,
    )
    lat_recv = shifted(latp, (0, 1, 0), -1)
    lon_recv = shifted(lonp, (0, 0, 1), -1)
    corner_recv = shifted(lonp, (0, 1, 1), -1)
    cout, ckeep, csend, ctab = call(
        side_kernel,
        [((TOK, 384), BF), ((8, COARSE, 128), BF), ((8, COARSE, 128), BF), ((16, WIDE), F32)],
        [((384, 256), F32), ((2, 512, 128), F32), ((16, COARSE, 128), BF)],
        flops=1 << 35,
    )(*coarse, coarse_proj)
    cother = sibling(csend)
    near0, later0, near1, later1, fkeep, fsend = call(
        back_kernel,
        [((BASE[2], 192), BF), ((BASE[4] - BASE[2], 192), BF),
         ((BASE[2], 192), BF), ((BASE[4] - BASE[2], 192), BF), ((8, FINE + TAB, 128), BF), ((8, FINE + TAB, 128), BF)],
        [
            ((1088, 192), BF), ((4, TOK, 192), BF), ((4, LANES, 192), BF), ((4, LANES, 192), BF),
            ((4, TOK, 192), BF), ((4, TOK, 192), BF), ((3, 4, TOK, 192), BF),
            ((2, 2, FINE_ROWS, 128), F32), ((192, 256), F32), ((2, 256, 128), F32), ((32, WIDE), F32), ((16, FINE + TAB, 128), BF),
        ],
        flops=1 << 33,
    )(x, gfo.reshape(4 * TOK, 192), lat_recv, lon_recv, corner_recv, bias, fine_gain, fine_qkv, fine_proj, ctab, cgains, cout)
    sums, back = reduce_everywhere((ckeep, fkeep), (cother, sibling(fsend)), near0, later0, near1, later1)
    field_grad, coarse_out = call(
        place_kernel, [((2, 12, 24, 192), BF), ((6, 12, 2, 384), BF)], [((sum(PIECE), 192), BF)]
    )(*back)
    levels, rows, cols = 2 * rep, 12 * lat, 24 * lon
    fine_scale = (levels * rows * cols) ** -0.5
    coarse_scale = (levels * rows * cols // 4) ** -0.5
    fine_table_scale = (cols // 12) ** -0.5
    coarse_table_scale = (cols // 24) ** -0.5
    fgain_g, fqkv_g, fproj_g, ftab_g, mgain_g, mw_g, cgain_g, cqkv_g, cproj_g, ctab_g = call(
        lambda *refs: unpack_kernel(fine_scale, coarse_scale, fine_table_scale, coarse_table_scale, *refs),
        [
            ((192,), F32), ((192, 576), F32), ((192, 192), F32), ((6, 2, POS), F32), ((768,), F32),
            ((768, 384), F32), ((384,), F32), ((384, 1152), F32), ((384, 384), F32), ((12, 1, POS), F32),
        ],
    )(*sums)
    return (
        coarse_out.transpose(2, 0, 1, 3), field_grad, fgain_g, fqkv_g, fproj_g, ftab_g.transpose(1, 0, 2)[None],
        mgain_g, mw_g, cgain_g, cqkv_g, cproj_g, ctab_g.transpose(1, 0, 2)[None],
    )


def solution(mesh):
    tokens, tables = P("rep", "lat", "lon", None), P("rep", "lat", None, None)
    return jax.shard_map(
        body,
        mesh=mesh,
        in_specs=(tokens, P(), P(), P(), tables, P(), P(), P(), P(), P(), tables, tokens),
        out_specs=(tokens, tokens, P(), P(), P(), tables, P(), P(), P(), P(), P(), tables),
        check_vma=False,
    )
```

```python
import numpy as np
import jax
import jax.numpy as jnp
from jax import lax
from jax.experimental import pallas as pl
from jax.experimental.pallas import tpu as pltpu
from jax.sharding import PartitionSpec as P

F32, BF = jnp.float32, jnp.bfloat16
EPS = 1e-05
TOK, HALF, LANES = 144, 72, 256
POS, DIAG = 3312, 23
RUN = 6 * DIAG
HEAD = 32
NEG = -1e30
COARSE, FINE, TAB = 432, 80, 64
GRAIN = COARSE + FINE
WIDE = 3456
FINE_ROWS, COARSE_ROWS = 6 * TOK + 8, 12 * TOK + 8
VMEM_LIMIT = 24 * 1024 * 1024


def dot(a, b, ca, cb):
    return lax.dot_general(a, b, (((ca,), (cb,)), ((), ())), preferred_element_type=F32)


def mm(a, b):
    return dot(a, b, 1, 0)


def mm_t(a, b):
    return dot(a, b, 1, 1)


def t_mm(a, b):
    return dot(a, b, 0, 0)


def low(x):
    return x.astype(BF)


def split3(x):
    hi = low(x)
    rest = x - hi.astype(F32)
    mid = low(rest)
    return hi, mid, low(rest - mid.astype(F32))


def iota(shape, dim):
    return lax.broadcasted_iota(jnp.int32, shape, dim)


def div_const(x, n):
    return lax.shift_right_logical(x * (65536 // n + 1), 16)


def one_hot(target, count):
    return jnp.where(iota((target.shape[0], count), 1) == target, 1.0, 0.0).astype(BF)


def window_index(rows):
    r = iota((rows, 1), 0)
    z = div_const(r, 72)
    r = r - z * 72
    w = div_const(r, 6)
    return z, r - w * 6, w


def pad_keys(x):
    gap = jnp.zeros((128 - HALF, x.shape[1]), F32)
    return low(jnp.concatenate([x[:HALF], gap, x[HALF:], gap], axis=0))


def unpad_keys(x):
    return jnp.concatenate([x[:HALF], x[128 : 128 + HALF]], axis=0)


def norm(x):
    width = sum(p.shape[1] for p in x)
    mean = sum(jnp.sum(p, axis=1, keepdims=True) for p in x) * (1.0 / width)
    shifted = [p - mean for p in x]
    var = sum(jnp.sum(p * p, axis=1, keepdims=True) for p in shifted) * (1.0 / width)
    inv = lax.rsqrt(var + EPS)
    return [p * inv for p in shifted], inv


def norm_back(grad, gain, hat, inv):
    width = sum(p.shape[1] for p in grad)
    scaled = [g * a for g, a in zip(grad, gain)]
    first = sum(jnp.sum(s, axis=1, keepdims=True) for s in scaled) * (1.0 / width)
    second = sum(jnp.sum(s * n, axis=1, keepdims=True) for s, n in zip(scaled, hat)) * (1.0 / width)
    gains = [jnp.sum(g * n, axis=0, keepdims=True) for g, n in zip(grad, hat)]
    return [inv * (s - first - n * second) for s, n in zip(scaled, hat)], gains


def load_bias(ref, kind, rows):
    return jnp.concatenate([ref[kind, 0, rows], ref[kind, 1, rows]], axis=1)


def head_mask(width, slot):
    lane = iota((1, width), 1)
    return (lane >= slot * HEAD) & (lane < (slot + 1) * HEAD)


def only_head(x, slot):
    return x * jnp.where(head_mask(x.shape[1], slot), 1.0, 0.0).astype(BF)


def by_head(x, slots):
    return jnp.concatenate([only_head(x, slot) for slot in range(slots)], axis=0)


def own_columns(x, slots):
    out = x[:TOK]
    for slot in range(1, slots):
        out = jnp.where(head_mask(x.shape[1], slot), x[slot * TOK : (slot + 1) * TOK], out)
    return out


def probabilities(q_stack, keys, bias):
    e = jnp.exp(mm_t(q_stack, keys) + bias)
    return e * (1.0 / jnp.sum(e, axis=1, keepdims=True))


def tile_forward(q, keys, values, bias, slots):
    p = probabilities(by_head(q, slots), keys, bias)
    return own_columns(mm(low(p), values), slots)


def tile_both(q, keys, values, gmix, bias, bias_grad_to, slots):
    q_stack, g_stack = by_head(q, slots), by_head(gmix, slots)
    p = probabilities(q_stack, keys, bias)
    p_low = low(p)
    mixed = own_columns(mm(p_low, values), slots)
    gp = mm_t(g_stack, values)
    gs = p * (gp - jnp.sum(p * gp, axis=1, keepdims=True))
    bias_grad_to(gs)
    gs_low = low(gs)
    gq = own_columns(mm(gs_low, keys), slots)
    return mixed, gq, t_mm(gs_low, q_stack), t_mm(p_low, g_stack)


def put(ref, grain, start, value):
    at = 0
    while at < value.shape[0]:
        chunk, row = divmod(start + at, grain)
        n = min(grain - row, value.shape[0] - at)
        ref[chunk, row : row + n] = value[at : at + n]
        at += n


def split_halves(pack_ref, keep_ref, send_ref):
    core = lax.axis_index("lon") % 2
    for own in range(2):

        @pl.when(core == own)
        def _():
            keep_ref[...] = pack_ref[8 * own : 8 * own + 8]
            send_ref[...] = pack_ref[8 - 8 * own : 16 - 8 * own]


def get_chunk(sums, chunk, rows):
    mine, other, core = sums
    return jnp.where(core == chunk // 8, mine[chunk % 8, rows].astype(F32), other[chunk % 8, rows].astype(F32))


def get(sums, grain, base, start, count):
    parts, at = [], 0
    while at < count:
        chunk, row = divmod(start + at, grain)
        n = min(grain - row, count - at)
        parts.append(get_chunk(sums, chunk, slice(base + row, base + row + n)))
        at += n
    return parts[0] if len(parts) == 1 else jnp.concatenate(parts, axis=0)


def gain_rows(pieces):
    line = pieces[0] if len(pieces) == 1 else jnp.concatenate(pieces, axis=1)
    width = line.shape[1]
    if width % 128:
        line = jnp.concatenate([line, jnp.zeros((1, 128 - width % 128), F32)], axis=1)
    rows = [line[:, 128 * i : 128 * i + 128] for i in range(line.shape[1] // 128)]
    rows.append(jnp.zeros((16 - len(rows), 128), F32))
    return low(jnp.concatenate(rows, axis=0))


def diagonal_select(first):
    lane = iota((1, 256), 1)
    wq = first + lax.shift_right_logical(lane, 7)
    lane = lane & 127
    wk = div_const(lane, 6)
    hk = lane - wk * 6
    diagonal = wq - wk + 11
    low_half = jnp.where((lane < HALF) & (hk < 3), hk * DIAG + diagonal, -1)
    high_half = jnp.where((lane < HALF) & (hk >= 3), (hk - 3) * DIAG + diagonal + 128, -1)
    target = jnp.maximum(low_half, high_half)
    return jnp.where(iota((256, 256), 0) == target, 1.0, 0.0).astype(BF)


HALF_RUN = 3 * DIAG


def table_groups():
    return [(g, (g // 12) * 16 + ((g // 6) % 2) * 8 + g % 6) for g in range(24)]


def table_slice(table, start):
    n = min(128, POS - start)
    part = table[:, start : start + n]
    if n < 128:
        part = jnp.concatenate([part, jnp.zeros((part.shape[0], 128 - n), F32)], axis=1)
    return part


def expand_tables(at_end, kinds, u_ref):
    lane, sub = iota((8, 128), 1), iota((8, 128), 0)
    column = div_const(lane, 6)
    crossing = (sub >= 3) != (lane - column * 6 >= 3)
    outside = jnp.where(lane >= HALF, NEG, 0.0)
    lev_term = jnp.where(at_end[0], NEG, 0.0)
    lat_term = jnp.where(crossing, jnp.where(at_end[1], NEG, 0.0), 0.0)
    u_ref[...] = jnp.zeros(u_ref.shape, F32)
    base = 0
    for table, _, _ in kinds:
        heads = table.shape[0]
        for g, row in table_groups():
            for half in range(2):
                u_ref[half, pl.ds(base + row, heads, stride=32)] = table_slice(table, g * RUN + half * HALF_RUN)
        base += heads * 32
    u = jnp.concatenate([u_ref[0, :base], u_ref[1, :base]], axis=1)
    hi = low(u)
    mid = low(u - hi.astype(F32))
    for first in range(0, 12, 2):
        sel = diagonal_select(first)
        x = mm(hi, sel) + mm(mid, sel)
        base = 0
        for table, may_end, out_ref in kinds:
            same = outside + lat_term if may_end else outside
            terms = same, same + lev_term
            for n in range(table.shape[0]):
                for zq in range(2):
                    for zk in range(2):
                        at = base + zq * 16 + zk * 8
                        for k in range(2):
                            to = n * TOK + zq * HALF + (first + k) * 6
                            part = x[at : at + 8, 128 * k : 128 * k + 128]
                            out_ref[zk, to : to + 6] = (part + terms[zq != zk])[:6]
                base += 32


def fold_tables(types, heads, grad_ref, y_ref, acc_ref, out_to):
    y_ref[...] = jnp.zeros(y_ref.shape, F32)
    for t in range(types):
        acc = None
        for first in range(0, 12, 2):
            sel = diagonal_select(first)
            for n in range(heads):
                for zq in range(2):
                    for zk in range(2):
                        at = n * 32 + zq * 16 + zk * 8
                        for k in range(2):
                            to = n * TOK + zq * HALF + (first + k) * 6
                            y_ref[at : at + 6, 128 * k : 128 * k + 128] = grad_ref[t, zk, to : to + 6]
            y = y_ref[...]
            hi = low(y)
            part = mm_t(hi, sel) + mm_t(low(y - hi.astype(F32)), sel)
            acc = part if acc is None else acc + part
        for half in range(2):
            acc_ref[half, : heads * 32] = acc[:, 128 * half : 128 * half + 128]
        for g, row in table_groups():
            for half in range(2):
                out_to(t, g * RUN + half * HALF_RUN, acc_ref[half, pl.ds(row, heads, stride=32)][:, :HALF_RUN])


def bias_kernel(fine_ref, next_ref, coarse_ref, fine_out, coarse_out, u_ref):
    at_end = [lax.axis_index(name) == lax.axis_size(name) - 1 for name in ("rep", "lat")]
    own, later, coarse = fine_ref[...], next_ref[...], coarse_ref[...]
    kinds = [
        (own[:, 0, :], False, fine_out.at[0]),
        (own[:, 1, :], True, fine_out.at[1]),
        (later[:, 0, :], False, fine_out.at[2]),
        (coarse[:, 0, :], True, coarse_out.at[0]),
    ]
    expand_tables(at_end, kinds, u_ref)


FIELD_PAD, COT_PAD = 176, 24
MESSAGE = FIELD_PAD + FIELD_PAD // 2 + 3 * COT_PAD


def pack_kernel(field_ref, cot_ref, *outs):
    r = iota((FIELD_PAD, 1), 0)
    row = div_const(r, 18)
    rc = iota((COT_PAD, 1), 0)
    crow = div_const(rc, 6)
    hots, cot_hots = [], []
    for t in range(2):
        for u in range(2):
            target = (row + (0 if t else 3)) * 24 + r - row * 18 + (0 if u else 6)
            hots.append(one_hot(jnp.where(r < 162, target, -1), 288))
    hot = jnp.concatenate(hots, axis=0)
    for s in range(2):
        for t in range(2):
            for u in range(2):
                target = (crow + (0 if t else 3)) * 12 + rc - crow * 6 + (0 if u else 6)
                cot_hots.append(one_hot(jnp.where(rc < 18, target * 2 + 1 - s, -1), TOK))
    cot = mm(jnp.concatenate(cot_hots, axis=0), low(cot_ref[...].astype(F32).reshape(TOK, 384)))
    half = FIELD_PAD // 2
    for s in range(2):
        rows = mm(hot, low(field_ref[1 - s].astype(F32).reshape(288, 192)))
        for n in range(4):
            out = outs[4 * s + n]
            part = rows[n * FIELD_PAD : (n + 1) * FIELD_PAD]
            out[:FIELD_PAD] = low(part[:, :128])
            rest = [low(jnp.concatenate([part[:half, 128:], part[half:, 128:]], axis=1))]
            first = (4 * s + n) * COT_PAD
            rest += [low(cot[first : first + COT_PAD, 128 * c : 128 * c + 128]) for c in range(3)]
            out[FIELD_PAD:] = jnp.concatenate([x.astype(F32) for x in rest], axis=0).astype(BF)


def field_of(ref):
    half = FIELD_PAD // 2
    rest = ref[FIELD_PAD : FIELD_PAD + half].astype(F32)
    rest = jnp.concatenate([rest[:, :64], rest[:, 64:]], axis=0)
    return low(jnp.concatenate([ref[:FIELD_PAD].astype(F32), rest], axis=1))


def cot_of(ref):
    rows = ref[FIELD_PAD:].astype(F32)[FIELD_PAD // 2 :]
    return low(jnp.concatenate([rows[COT_PAD * c : COT_PAD * c + COT_PAD] for c in range(3)], axis=1))


def fine_weights(qkv_ref):
    w = qkv_ref[...]
    return w[:, :192], w[:, 192:384], w[:, 384:]


FINE_TILES = ((0, 128, 4), (128, 64, 2))


def tile_rows(start, slots):
    return slice(start // HEAD * TOK, (start // HEAD + slots) * TOK)


def store_keys(ref, x):
    gap = jnp.zeros((128 - HALF, x.shape[1]), F32)
    for n in range(ref.shape[0]):
        part = x[n * TOK : (n + 1) * TOK]
        for z in range(2):
            ref[n, 128 * z : 128 * z + 128] = low(jnp.concatenate([part[HALF * z : HALF * z + HALF], gap], axis=0))


def main_kernel(
    b000, b001, b010, b011, b100, b101, b110, b111,
    bias_ref, cbias_ref,
    fgain_ref, fqkv_ref, fproj_ref, mgain_ref, mw_ref, cgain_ref, cqkv_ref, cproj_ref,
    x_out, gfo_out, latp_out, lonp_out, cin_out, gy_out, xc_out, mnorm_out, gci_out, mix_ref, g_ref, gb_ref, gains_out,
    x_ref, fo_ref, fq_ref, fk_ref, fv_ref, fm_ref,
    q_ref, k_ref, v_ref, gm_ref,
):
    bufs = ((b000, b001), (b010, b011)), ((b100, b101), (b110, b111))
    _, hh, ww = window_index(HALF)
    seen = set()
    for t in range(2):
        for u in range(2):
            hots = []
            for wr in (t, t + 1):
                for wc in (u, u + 1):
                    lat = 6 * wr + hh - 9 * t
                    lon = 12 * wc + ww - 18 * u
                    good = (lat >= 0) & (lat < 9) & (lon >= 0) & (lon < 18)
                    hots.append(one_hot(jnp.where(good, lat * 18 + lon, -1), FIELD_PAD))
            hot = jnp.concatenate(hots, axis=0)
            for z in range(2):
                part = mm(hot, field_of(bufs[z][t][u]))
                for n in range(4):
                    place = 3 * (t + n // 2) + u + n % 2, slice(z * HALF, (z + 1) * HALF)
                    value = part[n * HALF : (n + 1) * HALF]
                    if (place[0], z) in seen:
                        value = value + x_ref[place]
                    seen.add((place[0], z))
                    x_ref[place] = value
    for wr in range(2):
        for wc in range(2):
            x_out[2 * wr + wc] = low(x_ref[3 * wr + wc])
    wq, wk, wv = fine_weights(fqkv_ref)
    x = x_ref[...].reshape(9 * TOK, 192)
    (hat,), _ = norm([x])
    xn = low(hat * fgain_ref[...].reshape(1, 192))
    fq_ref[...] = low(mm(xn, wq) * HEAD**-0.5).reshape(9, TOK, 192)
    store_keys(fk_ref, mm(xn, wk))
    store_keys(fv_ref, mm(xn, wv))

    def fine_window(w, table_ref, wr):
        for start, width, slots in FINE_TILES:
            lanes = slice(start, start + width)

            bias = load_bias(table_ref, wr, tile_rows(start, slots))
            fm_ref[w, :, lanes] = low(
                tile_forward(fq_ref[w, :, lanes], fk_ref[w, :, lanes], fv_ref[w, :, lanes], bias, slots)
            )

    @pl.loop(0, 9, unroll=3)
    def _(w):
        fine_window(w, bias_ref, div_const(w, 3))

    out = low(mm(fm_ref[...].reshape(9 * TOK, 192), fproj_ref[...])).astype(F32)
    fo_ref[...] = low(x_ref[...].reshape(9 * TOK, 192) + out)

    z, i, j = window_index(TOK)
    hots = []
    for p in range(4):
        lat = 3 + 2 * i + p // 2
        lon = 6 + 2 * j + p % 2
        wr, wc = div_const(lat, 6), div_const(lon, 12)
        target = (3 * wr + wc) * TOK + z * HALF + (lon - 12 * wc) * 6 + lat - 6 * wr
        hots.append(one_hot(target, 9 * TOK))
    merged = mm(jnp.concatenate(hots, axis=0), fo_ref[...])
    merged = [merged[p * TOK : (p + 1) * TOK] for p in range(4)]
    mhat, minv = norm(merged)
    mgain = mgain_ref[...].reshape(1, 768)
    mgain = [mgain[:, 192 * p : 192 * p + 192] for p in range(4)]
    mnorm = [low(h * g) for h, g in zip(mhat, mgain)]
    mweight = [mw_ref[192 * p : 192 * p + 192] for p in range(4)]
    cin = low(sum(mm(n, w) for n, w in zip(mnorm, mweight))).astype(F32)
    (chat,), cinv = norm([cin])
    cgain = cgain_ref[...].reshape(1, 384)
    xc = low(chat * cgain)
    _, ci, cj = window_index(HALF)
    cot_rows = [None, None]
    for t in range(2):
        for u in range(2):
            lat, lon = ci - 3 * t, cj - 6 * u
            good = (lat >= 0) & (lat < 3) & (lon >= 0) & (lon < 6)
            hot = one_hot(jnp.where(good, lat * 6 + lon, -1), COT_PAD)
            for s in range(2):
                part = mm(hot, cot_of(bufs[s][t][u]))
                cot_rows[s] = part if cot_rows[s] is None else cot_rows[s] + part
    cot = jnp.concatenate(cot_rows, axis=0)
    gy = low(cot)
    gmix = low(mm_t(gy, cproj_ref[...]))
    for tile in range(3):
        lanes = slice(128 * tile, 128 * tile + 128)
        q_ref[tile] = low(mm(xc, cqkv_ref[:, lanes]) * HEAD**-0.5)
        k_ref[tile] = pad_keys(mm(xc, cqkv_ref[:, 384 + 128 * tile : 512 + 128 * tile]))
        v_ref[tile] = pad_keys(mm(xc, cqkv_ref[:, 768 + 128 * tile : 896 + 128 * tile]))
        gm_ref[tile] = gmix[:, lanes]

    def coarse_tile(tile, carry):
        rows = pl.ds(pl.multiple_of(tile * 4 * TOK, 64), 4 * TOK)

        def bias_grad_to(gs):
            gb_ref[0, 0, rows] = gs[:, :128]
            gb_ref[0, 1, rows] = gs[:, 128:]

        mixed, gq, gk, gv = tile_both(
            q_ref[tile], k_ref[tile], v_ref[tile], gm_ref[tile], load_bias(cbias_ref, 0, rows), bias_grad_to, 4
        )
        mix_ref[tile] = low(mixed)
        g_ref[0, tile] = low(gq * HEAD**-0.5)
        g_ref[1, tile] = low(unpad_keys(gk))
        g_ref[2, tile] = low(unpad_keys(gv))
        return carry

    lax.fori_loop(0, 3, coarse_tile, 0, unroll=True)
    grolled = None
    for tile in range(3):
        for m in range(3):
            wcols = slice(384 * m + 128 * tile, 384 * m + 128 * tile + 128)
            part = mm_t(g_ref[m, tile], cqkv_ref[:, wcols])
            grolled = part if grolled is None else grolled + part
    cin_out[...] = low(cin)
    gy_out[...] = gy
    xc_out[...] = xc
    (gci,), (cgain_grad,) = norm_back([low(grolled).astype(F32)], [cgain], [chat], cinv)
    gci = low(cot + gci)
    gml = []
    gci_out[...] = gci
    for p in range(4):
        mnorm_out[p] = mnorm[p]
        gml.append(low(mm_t(gci, mweight[p])).astype(F32))
    gmerged, mgain_grad = norm_back(gml, mgain, mhat, minv)
    gains_out[...] = gain_rows(list(mgain_grad) + [cgain_grad])
    r48 = iota((48, 1), 0)
    zi = div_const(r48, 24)
    rest = r48 - 24 * zi
    lat_hot = one_hot(zi * HALF + lax.shift_right_logical(rest, 1) * 6 + 4 + (rest & 1), TOK)
    r40 = iota((40, 1), 0)
    zi = jnp.where(r40 >= 18, 1, 0)
    lon_hot = one_hot(jnp.where(r40 < 36, zi * HALF + 54 + r40 - 18 * zi, -1), TOK)
    hot = jnp.concatenate([lat_hot, lon_hot], axis=0)
    for p in range(4):
        g = low(gmerged[p])
        gfo_out[p] = g
        part = low(mm(hot, g))
        latp_out[48 * p : 48 * p + 48] = part[:48]
        lonp_out[40 * p : 40 * p + 40] = part[48:]


def side_kernel(
    cin_ref, gy_ref, xc_ref, mnorm_ref, gci_ref, mix_ref, g_ref, gb_ref, cproj_ref,
    cout_out, keep_out, send_out, ctab_out, y_ref, acc_ref, pack_out,
):
    gy, xc, gci = gy_ref[...], xc_ref[...], gci_ref[...]
    out = None
    for tile in range(3):
        lanes = slice(128 * tile, 128 * tile + 128)
        part = mm(mix_ref[tile], cproj_ref[lanes])
        out = part if out is None else out + part
        dproj = low(t_mm(mix_ref[tile], gy))
        for c in range(3):
            start = 5760 + 384 * c + 128 * tile
            put(pack_out, COARSE, start, dproj[:, 128 * c : 128 * c + 128])
    cout_out[...] = low(cin_ref[...].astype(F32) + low(out).astype(F32))
    for m in range(3):
        dqkv = low(t_mm(xc, jnp.concatenate([g_ref[m, tile] for tile in range(3)], axis=1)))
        for tile in range(3):
            start = 2304 + 384 * (3 * m + tile)
            put(pack_out, COARSE, start, dqkv[:, 128 * tile : 128 * tile + 128])
    for p in range(4):
        dmw = low(t_mm(mnorm_ref[p], gci))
        for c in range(3):
            start = 768 * c + 192 * p
            put(pack_out, COARSE, start, dmw[:, 128 * c : 128 * c + 128])
    split_halves(pack_out, keep_out, send_out)
    ctab_out[...] = jnp.zeros(ctab_out.shape, F32)

    def ctab(t, start, rows):
        ctab_out[:12, start : start + HALF_RUN] = rows

    fold_tables(1, 12, gb_ref, y_ref, acc_ref, ctab)


QUARTERS = ((0, 0), (0, 1), (1, 1), (1, 0))
FINE_PAD = (176, 64, 32, 64)
PIECE = tuple(n + 48 for n in FINE_PAD)
BASE = tuple(sum(PIECE[:n]) for n in range(5))


def fine_rows_of(s, t, u):
    r = iota((FINE_PAD[QUARTERS.index((t, u))], 1), 0)
    width, height = 6 if u else 18, 3 if t else 9
    row = div_const(r, width)
    lat, lon = row + 9 * t, r - row * width + 18 * u
    wr, wc = div_const(lat, 6), div_const(lon, 12)
    target = (2 * wr + wc) * TOK + s * HALF + (lon - 12 * wc) * 6 + lat - 6 * wr
    return jnp.where(row < height, target, -1)


def coarse_rows_of(s, t, u):
    r = iota((24, 1), 0)
    row = div_const(r, 6)
    return jnp.where(row < 3, s * HALF + (r - row * 6 + 6 * u) * 6 + row + 3 * t, -1)


def back_kernel(
    x_in, gfo_ref, latp_ref, lonp_ref, corner_ref, bias_ref, fgain_ref, fqkv_ref, fproj_ref, ctab_ref, gains_ref, cout_ref,
    near0_out, later0_out, near1_out, later1_out, keep_out, send_out,
    src_ref, fq_ref, fk_ref, fv_ref, fm_ref, gm_ref, g_ref, gb_ref, y_ref, acc_ref, tab_ref, pack_out,
):
    src_ref[:576] = gfo_ref[...]
    src_ref[576:768] = latp_ref[...]
    src_ref[768:928] = lonp_ref[...]
    src_ref[928:] = corner_ref[...]
    z, h, w = window_index(TOK)
    hots = []
    for wr in range(2):
        for wc in range(2):
            lat, lon = 6 * wr + h, 12 * wc + w
            behind, before = lat < 3, lon < 6
            lat = jnp.where(behind, lat + 9, lat - 3)
            lon = jnp.where(before, lon + 18, lon - 6)
            p = 2 * (lat & 1) + (lon & 1)
            i, j = lax.shift_right_logical(lat, 1), lax.shift_right_logical(lon, 1)
            own = p * TOK + z * HALF + j * 6 + i
            from_lat = 576 + p * 48 + z * 24 + j * 2 + i - 4
            from_lon = 768 + p * 40 + z * 18 + (j - 9) * 6 + i
            target = jnp.where(before, from_lon + jnp.where(behind, 160, 0), jnp.where(behind, from_lat, own))
            hots.append(one_hot(target, 1088))
    gy = low(mm(jnp.concatenate(hots, axis=0), src_ref[...]))
    gy32 = gy.astype(F32)
    gb_ref[...] = jnp.zeros(gb_ref.shape, F32)
    weights = fine_weights(fqkv_ref)
    gain = fgain_ref[...].reshape(1, 192)
    x = x_in[...].reshape(4 * TOK, 192).astype(F32)
    (hat,), inv = norm([x])
    xn = low(hat * gain)
    fq_ref[...] = low(mm(xn, weights[0]) * HEAD**-0.5).reshape(4, TOK, 192)
    store_keys(fk_ref, mm(xn, weights[1]))
    store_keys(fv_ref, mm(xn, weights[2]))
    gm_ref[...] = low(mm_t(gy, fproj_ref[...])).reshape(4, TOK, 192)

    @pl.loop(0, 4)
    def _(n):
        wr = lax.shift_right_logical(n, 1)
        for start, width, slots in FINE_TILES:
            lanes = slice(start, start + width)

            rows = tile_rows(start, slots)

            def bias_grad_to(gs):
                gb_ref[wr, 0, rows] += gs[:, :128]
                gb_ref[wr, 1, rows] += gs[:, 128:]

            mixed, gq, gk, gv = tile_both(
                fq_ref[n, :, lanes], fk_ref[n, :, lanes], fv_ref[n, :, lanes], gm_ref[n, :, lanes],
                load_bias(bias_ref, wr, rows), bias_grad_to, slots,
            )
            fm_ref[n, :, lanes] = low(mixed)
            g_ref[0, n, :, lanes] = low(gq * HEAD**-0.5)
            g_ref[1, n, :, lanes] = low(unpad_keys(gk))
            g_ref[2, n, :, lanes] = low(unpad_keys(gv))

    dproj = t_mm(fm_ref[...].reshape(4 * TOK, 192), gy)
    grads = [g_ref[m].reshape(4 * TOK, 192) for m in range(3)]
    dqkv = [t_mm(xn, g) for g in grads]
    grolled = sum(mm_t(g, w) for g, w in zip(grads, weights))
    (gx,), (ggain,) = norm_back([low(grolled).astype(F32)], [gain], [hat], inv)
    fg = low(gy32 + gx)
    cout = cout_ref[...]
    for s, outs in enumerate(((near0_out, later0_out), (near1_out, later1_out))):
        hots, coarse_hots = [], []
        for t, u in QUARTERS:
            hots.append(one_hot(fine_rows_of(s, t, u), 4 * TOK))
            coarse_hots.append(one_hot(coarse_rows_of(s, t, u), TOK))
        fine = low(mm(jnp.concatenate(hots, axis=0), fg))
        coarse = low(mm(jnp.concatenate(coarse_hots, axis=0), cout))
        at = 0
        for n, rows in enumerate(FINE_PAD):
            out, to = outs[n // 2], BASE[n] - BASE[n // 2 * 2]
            out[to : to + rows] = fine[at : at + rows]
            out[to + rows : to + rows + 24] = coarse[24 * n : 24 * n + 24, :192]
            out[to + rows + 24 : to + rows + 48] = coarse[24 * n : 24 * n + 24, 192:]
            at += rows
    first = low(jnp.concatenate([dqkv[0], dqkv[1]], axis=1))
    second = low(jnp.concatenate([dqkv[2], dproj], axis=1))
    for c in range(3):
        put(pack_out, FINE, 192 * c, first[:, 128 * c : 128 * c + 128])
        put(pack_out, FINE, 576 + 192 * c, second[:, 128 * c : 128 * c + 128])
    put(pack_out, FINE, 1152, gain_rows([ggain]))
    put(pack_out, FINE, 1168, gains_ref[...])
    put(pack_out, FINE, 1184, jnp.zeros((96, 128), BF))
    tab_ref[...] = jnp.zeros(tab_ref.shape, F32)
    tab_ref[16:32] = ctab_ref[...]

    def ftab(t, start, rows):
        tab_ref[8 * t : 8 * t + 6, start : start + HALF_RUN] = rows

    fold_tables(2, 6, gb_ref, y_ref, acc_ref, ftab)
    for c in range(13):
        for half in range(2):
            lanes = slice(256 * c + 128 * half, 256 * c + 128 * half + 128)
            pack_out[c, FINE + 32 * half : FINE + 32 * half + 32] = low(tab_ref[:, lanes])
    for c in range(13, 16):
        pack_out[c, FINE:] = jnp.zeros((TAB, 128), BF)
    split_halves(pack_out, keep_out, send_out)


def place_kernel(near0_ref, near1_ref, later0_ref, later1_ref, lon_ref, field_out, coarse_out, src_ref):
    def chosen(later_row, later_col, values):
        value = dict(zip(QUARTERS, values))
        near = jnp.where(later_row, value[1, 0], value[0, 0])
        return jnp.where(later_col, jnp.where(later_row, value[1, 1], value[0, 1]), near)

    base = BASE[:4]
    r = iota((288, 1), 0)
    lat = div_const(r, 24)
    col = r - lat * 24
    later_row, later_col = lat < 3, col < 6
    row = jnp.where(later_row, lat, lat - 3)
    inside = jnp.where(later_col, row * 6 + col, row * 18 + col - 6)
    hots = [one_hot(chosen(later_row, later_col, base) + inside, sum(PIECE))]
    r = iota((HALF, 1), 0)
    lat = div_const(r, 12)
    col = r - lat * 12
    later_row, later_col = lat < 3, col < 6
    inside = jnp.where(later_row, lat, lat - 3) * 6 + jnp.where(later_col, col, col - 6)
    inside = inside + chosen(later_row, later_col, [b + n for b, n in zip(base, FINE_PAD)])
    hots += [one_hot(inside, sum(PIECE)), one_hot(inside + 24, sum(PIECE))]
    hot = jnp.concatenate(hots, axis=0)
    placed = []
    for s in range(2):
        src_ref[: BASE[1]] = (near0_ref, near1_ref)[s][: BASE[1]]
        src_ref[BASE[1] : BASE[3]] = lon_ref[s]
        src_ref[BASE[3] :] = (later0_ref, later1_ref)[s][PIECE[2] :]
        out = low(mm(hot, src_ref[...]))
        for h in range(12):
            field_out[1 - s, h] = out[24 * h : 24 * h + 24]
        coarse = jnp.concatenate([out[288:360], out[360:]], axis=1).astype(F32)
        placed.append(coarse)
    for h in range(6):
        rows = slice(12 * h, 12 * h + 12)
        coarse_out[h] = low(jnp.stack([placed[1][rows], placed[0][rows]], axis=1))


def unpack_kernel(fine_scale, coarse_scale, fine_table_scale, coarse_table_scale, mine_ref, other_ref, *outs):
    sums = mine_ref, other_ref, lax.axis_index("lon") % 2
    fgain_out, qkv_out, proj_out, ftab_out, mgain_out, mw_out, cgain_out, cqkv_out, cproj_out, ctab_out = outs
    def coarse_get(start, count):
        return get(sums, COARSE, 0, start, count) * coarse_scale

    def fine_get(start, count, scale):
        return get(sums, FINE, COARSE, start, count) * scale

    for c in range(3):
        lanes = slice(128 * c, 128 * c + 128)
        mw_out[:, lanes] = coarse_get(768 * c, 768)
        cproj_out[:, lanes] = coarse_get(5760 + 384 * c, 384)
        qkv_out[:, lanes] = fine_get(192 * c, 192, fine_scale)
    for c in range(9):
        cqkv_out[:, 128 * c : 128 * c + 128] = coarse_get(2304 + 384 * c, 384)
    second = [fine_get(576 + 192 * c, 192, fine_scale) for c in range(3)]
    qkv_out[:, 384:512] = second[0]
    qkv_out[:, 512:] = second[1][:, :64]
    proj_out[...] = jnp.concatenate([second[1][:, 64:], second[2]], axis=1)
    gains = fine_get(1168, 16, coarse_scale)
    for c in range(6):
        mgain_out[pl.ds(128 * c, 128)] = gains[c]
    for c in range(3):
        cgain_out[pl.ds(128 * c, 128)] = gains[6 + c]
    gains = fine_get(1152, 16, fine_scale)
    fgain_out[...] = jnp.concatenate([gains[:1], gains[1:2, :64]], axis=1).reshape(192)
    for c in range(13):
        for half in range(2):
            start = 256 * c + 128 * half
            n = min(128, POS - start)
            block = get_chunk(sums, c, slice(GRAIN + 32 * half, GRAIN + 32 * half + 32))[:, :n]
            both = jnp.stack([block[:6], block[8:14]], axis=1)
            ftab_out[:, :, start : start + n] = both * fine_table_scale
            ctab_out[:, 0, start : start + n] = block[16:28] * coarse_table_scale


def call(kernel, out_shapes, scratch=(), smem=0, flops=0, moved=0, vmem=VMEM_LIMIT):
    def run(*args):
        specs = [pl.BlockSpec(memory_space=pltpu.SMEM)] * smem
        specs += [pl.BlockSpec(memory_space=pltpu.VMEM)] * (len(args) - smem)
        return pl.pallas_call(
            kernel,
            out_shape=[jax.ShapeDtypeStruct(s, d) for s, d in out_shapes],
            in_specs=specs,
            out_specs=[pl.BlockSpec(memory_space=pltpu.VMEM)] * len(out_shapes),
            scratch_shapes=[pltpu.VMEM(s, d) for s, d in scratch],
            compiler_params=pltpu.CompilerParams(vmem_limit_bytes=vmem),
            cost_estimate=pl.CostEstimate(flops=flops, bytes_accessed=moved, transcendentals=0),
        )(*args)

    return run


def shifted(x, offset, sign):
    names = [n for n, o in zip(("lon", "lat", "rep"), offset[::-1]) if o]
    sizes = [lax.axis_size(n) for n in names]
    pairs = []
    for place in np.ndindex(*sizes):
        target = [(p - sign) % s for p, s in zip(place, sizes)]
        pairs.append((int(np.ravel_multi_index(place, sizes)), int(np.ravel_multi_index(target, sizes))))
    return lax.ppermute(x, tuple(names), pairs)


CORNERS = [(s, t, u) for s in range(2) for t in range(2) for u in range(2)]


def exchange(x, axes):
    return lax.all_to_all(lax.optimization_barrier(x), axes, 0, 0, tiled=True)


def summed(x):
    return jnp.sum(x.astype(F32), axis=0, keepdims=True).astype(BF)


def spread(x, count):
    return jnp.broadcast_to(x, (count,) + x.shape[1:])


def sibling(x):
    return lax.ppermute(x, "lon", [(i, i ^ 1) for i in range(lax.axis_size("lon"))])


def exchange_columns(x):
    size = lax.axis_size("lon")
    groups = [list(range(core, size, 2)) for core in range(2)]
    return lax.all_to_all(lax.optimization_barrier(x), "lon", 0, 0, axis_index_groups=groups, tiled=True)


def reduce_everywhere(keep, other, near0, later0, near1, later1):
    rest = lax.axis_size("lat") * lax.axis_size("rep")
    keep, other = lax.optimization_barrier((keep, other))
    pair = [(a.astype(F32) + b.astype(F32)).astype(BF) for a, b in zip(keep, other)]
    pack = exchange_columns(jnp.concatenate(pair, axis=1))
    part = summed(pack[:, :GRAIN]).reshape(rest, -1, 128)
    tables = summed(pack[:, GRAIN:])
    near1, later0, later1 = (
        shifted(x, place, -1) for x, place in ((near1, (1, 0, 0)), (later0, (0, 1, 0)), (later1, (1, 1, 0)))
    )
    part = exchange(part, ("lat", "rep"))
    part, near1, later0, later1 = lax.optimization_barrier((part, near1, later0, later1))
    part = spread(summed(part), rest)
    column = [jnp.concatenate([x[BASE[1] :], y[: PIECE[2]]]) for x, y in ((near0, later0), (near1, later1))]
    column = shifted(jnp.stack(column), (0, 0, 1), -1)
    part, column = lax.optimization_barrier((exchange(part, ("lat", "rep")), column))
    mine = jnp.concatenate([part.reshape(1, GRAIN, 128), tables], axis=1)
    mine = exchange_columns(spread(mine, lax.axis_size("lon") // 2))
    return (mine, sibling(mine)), (near0, near1, later0, later1, column)


def body(
    fine_field, fine_gain, fine_qkv, fine_proj, fine_table, merge_gain, merge_weight,
    coarse_gain, coarse_qkv, coarse_proj, coarse_table, cotangent,
):
    rep, lat, lon = (lax.axis_size(n) for n in ("rep", "lat", "lon"))
    packs = call(pack_kernel, [((MESSAGE, 128), BF)] * 8)(fine_field, cotangent.transpose(1, 2, 0, 3))
    bufs = [shifted(b, place, 1) if any(place) else b for b, place in zip(packs, CORNERS)]
    table = fine_table[0].transpose(1, 0, 2)
    bias, cbias = call(
        bias_kernel,
        [((3, 2, FINE_ROWS, 128), F32), ((1, 2, COARSE_ROWS, 128), F32)],
        [((2, 34 * 32, 128), F32)],
        flops=1 << 32,
    )(table, shifted(fine_table, (0, 1, 0), 1)[0].transpose(1, 0, 2), coarse_table[0].transpose(1, 0, 2))
    x, gfo, latp, lonp, *coarse, cgains = call(
        main_kernel,
        [
            ((4, TOK, 192), BF), ((4, TOK, 192), BF), ((192, 192), BF), ((160, 192), BF),
            ((TOK, 384), BF), ((TOK, 384), BF), ((TOK, 384), BF), ((4, TOK, 192), BF), ((TOK, 384), BF),
            ((3, TOK, 128), BF), ((3, 3, TOK, 128), BF), ((1, 2, COARSE_ROWS, 128), F32), ((16, 128), BF),
        ],
        [
            ((9, TOK, 192), F32), ((9 * TOK, 192), BF),
            ((9, TOK, 192), BF), ((9, LANES, 192), BF), ((9, LANES, 192), BF), ((9, TOK, 192), BF),
            ((3, TOK, 128), BF), ((3, LANES, 128), BF), ((3, LANES, 128), BF), ((3, TOK, 128), BF),
        ],
        flops=1 << 34,
    )(
        *bufs, bias, cbias, fine_gain, fine_qkv, fine_proj, merge_gain,
        merge_weight, coarse_gain, coarse_qkv, coarse_proj,
    )
    lat_recv = shifted(latp, (0, 1, 0), -1)
    lon_recv = shifted(lonp, (0, 0, 1), -1)
    corner_recv = shifted(lonp, (0, 1, 1), -1)
    cout, ckeep, csend, ctab = call(
        side_kernel,
        [((TOK, 384), BF), ((8, COARSE, 128), BF), ((8, COARSE, 128), BF), ((16, WIDE), F32)],
        [((384, 256), F32), ((2, 512, 128), F32), ((16, COARSE, 128), BF)],
        flops=1 << 35,
    )(*coarse, coarse_proj)
    cother = sibling(csend)
    near0, later0, near1, later1, fkeep, fsend = call(
        back_kernel,
        [((BASE[2], 192), BF), ((BASE[4] - BASE[2], 192), BF),
         ((BASE[2], 192), BF), ((BASE[4] - BASE[2], 192), BF), ((8, FINE + TAB, 128), BF), ((8, FINE + TAB, 128), BF)],
        [
            ((1088, 192), BF), ((4, TOK, 192), BF), ((4, LANES, 192), BF), ((4, LANES, 192), BF),
            ((4, TOK, 192), BF), ((4, TOK, 192), BF), ((3, 4, TOK, 192), BF),
            ((2, 2, FINE_ROWS, 128), F32), ((192, 256), F32), ((2, 256, 128), F32), ((32, WIDE), F32), ((16, FINE + TAB, 128), BF),
        ],
        flops=1 << 33,
    )(x, gfo.reshape(4 * TOK, 192), lat_recv, lon_recv, corner_recv, bias, fine_gain, fine_qkv, fine_proj, ctab, cgains, cout)
    sums, back = reduce_everywhere((ckeep, fkeep), (cother, sibling(fsend)), near0, later0, near1, later1)
    field_grad, coarse_out = call(
        place_kernel, [((2, 12, 24, 192), BF), ((6, 12, 2, 384), BF)], [((sum(PIECE), 192), BF)]
    )(*back)
    levels, rows, cols = 2 * rep, 12 * lat, 24 * lon
    fine_scale = (levels * rows * cols) ** -0.5
    coarse_scale = (levels * rows * cols // 4) ** -0.5
    fine_table_scale = (cols // 12) ** -0.5
    coarse_table_scale = (cols // 24) ** -0.5
    fgain_g, fqkv_g, fproj_g, ftab_g, mgain_g, mw_g, cgain_g, cqkv_g, cproj_g, ctab_g = call(
        lambda *refs: unpack_kernel(fine_scale, coarse_scale, fine_table_scale, coarse_table_scale, *refs),
        [
            ((192,), F32), ((192, 576), F32), ((192, 192), F32), ((6, 2, POS), F32), ((768,), F32),
            ((768, 384), F32), ((384,), F32), ((384, 1152), F32), ((384, 384), F32), ((12, 1, POS), F32),
        ],
    )(*sums)
    return (
        coarse_out.transpose(2, 0, 1, 3), field_grad, fgain_g, fqkv_g, fproj_g, ftab_g.transpose(1, 0, 2)[None],
        mgain_g, mw_g, cgain_g, cqkv_g, cproj_g, ctab_g.transpose(1, 0, 2)[None],
    )


def solution(mesh):
    tokens, tables = P("rep", "lat", "lon", None), P("rep", "lat", None, None)
    return jax.shard_map(
        body,
        mesh=mesh,
        in_specs=(tokens, P(), P(), P(), tables, P(), P(), P(), P(), P(), tables, tokens),
        out_specs=(tokens, tokens, P(), P(), P(), tables, P(), P(), P(), P(), P(), tables),
        check_vma=False,
    )
```
